128 devices in a mesh: lvl: 4 (over y_hi, core), lat: 32 (over z, x, y_lo).
Axes of the slice: x: 4, y: 4 (y_hi: 2, y_lo: 2; y = y_hi * 2 + y_lo), z: 4, core: 2. Of those that a mesh axis runs over, the one named last changes fastest.
Arguments:
- tokens: bfloat16 [8, 192, 144, 384], P('lvl', 'lat'), may hold values from -60 to 60
- targets: bfloat16 [8, 192, 144, 160], P('lvl', 'lat'), may hold values from -6 to 6
- relief: int32 [192, 144], replicated, may hold values from 0 to 3
- earth_bias: float32 [4, 32, 12, 144, 144], P('lvl', 'lat'), may hold values from -4 to 300
- relief_table: bfloat16 [4, 384], replicated, may hold values from -3 to 3
- gain_attn: float32 [384], replicated, may hold values from 0.5 to 1.5
- gain_mlp: float32 [384], replicated, may hold values from 0.5 to 1.5
- w_qkv: bfloat16 [384, 1152], replicated, may hold values from -0.3125 to 0.3125
- w_proj: bfloat16 [384, 384], replicated, may hold values from -0.3125 to 0.3125
- w_up: bfloat16 [384, 1536], replicated, may hold values from -0.3125 to 0.3125
- w_down: bfloat16 [1536, 384], replicated, may hold values from -0.15625 to 0.15625
- w_out: bfloat16 [384, 160], replicated, may hold values from -0.3125 to 0.3125
- var_weight: float32 [5], replicated, may hold values from 0.5 to 4
Outputs:
- loss: float32 [], replicated
- grad_qkv: float32 [384, 1152], P(('lvl', 'lat'))
- grad_proj: float32 [384, 384], P(('lvl', 'lat'))
- grad_up: float32 [384, 1536], P(('lvl', 'lat'))
- grad_down: float32 [1536, 384], P(('lvl', 'lat'))
- grad_out: float32 [384, 160], P(('lvl', 'lat'))
- grad_gain_attn: float32 [384], P(('lvl', 'lat'))
- grad_gain_mlp: float32 [384], P(('lvl', 'lat'))
- grad_relief: float32 [384, 4], P(('lvl', 'lat'))
- grad_bias: float32 [4, 32, 12, 144, 144], P('lvl', 'lat')
The draws below stay inside these ranges and needn't reach their ends.
All inputs are finite; a program needn't handle non-finite values.
Results may differ from the reference program's by a relative error of at most 0.022.
Values may be sent and summed in bfloat16 or wider, within the bound.
No kernel may reach another device: no remote copies, remote signals or barrier semaphores. Data moves between devices by JAX's collectives and lax.ppermute only.
A program may use at most 256 MiB of HBM per device.

```python
import math
import jax
import jax.numpy as jnp
from jax import lax

D = 384
HEADS = 12
FF = 1536
VARS = 5
LVL_DEV = 2
ROWS_DEV = 6
WIN_LON = 12
CLASSES = 4
NLON = 144
OUT = 160
WIN = 144
NZ = 8
NLAT = 192
ZWIN = 4
LWIN = 32
N_LVL = 4
N_LAT = 32


def block_marks(key):
    key_p, key_s = jax.random.split(key, 2)
    feature_pick = jax.random.permutation(key_p, D)[:ZWIN * LWIN].astype(jnp.int32)
    sign_pick = (2 * jax.random.randint(key_s, (ZWIN * LWIN,), 0, 2) - 1).astype(jnp.float32)
    slot_block = jnp.arange(NZ, dtype=jnp.int32) // LVL_DEV
    row_block = jnp.arange(NLAT, dtype=jnp.int32) // ROWS_DEV
    block_ids = slot_block[:, None] * LWIN + row_block[None, :]
    chosen = feature_pick[block_ids]
    signs = sign_pick[block_ids]
    hit = (jnp.arange(D, dtype=jnp.int32)[None, None, :] == chosen[:, :, None]).astype(jnp.float32)
    return (15.0 * signs[:, :, None] * hit)[:, :, None, :]


def draw_tokens(key, part):
    key = jax.random.fold_in(key, 11)
    key_a = jax.random.fold_in(key, 0)
    key_b = jax.random.fold_in(key, 1)
    key_c = jax.random.fold_in(key, 2)
    key_e = jax.random.fold_in(key, 4)
    col_scale = jnp.exp(jax.random.uniform(key_b, (D,), jnp.float32, 0.0, math.log(10.0)))
    row_scale = jnp.exp(jax.random.uniform(key_c, (NZ, NLAT, NLON, 1), jnp.float32, -1.2, 1.2))
    marks = block_marks(key_e)
    base_draw = jax.random.truncated_normal(key_a, -4.0, 4.0, (NZ, NLAT, NLON, D), jnp.float32)
    values_out = base_draw * col_scale * row_scale * 0.4 + marks
    return jnp.clip(values_out, -60.0, 60.0).astype(jnp.bfloat16)


def draw_earth_bias(key, part):
    key = jax.random.fold_in(key, 23)
    key_a = jax.random.fold_in(key, 0)
    shape_all = (ZWIN, LWIN, HEADS, WIN, WIN)
    return jax.random.truncated_normal(key_a, -4.0, 4.0, shape_all, jnp.float32)


def touch_ends(entries, stream_key, low, top_value):
    longest = entries.shape.index(max(entries.shape))
    spots = []
    for shift in (0, 1):
        where = [jax.random.randint(jax.random.fold_in(stream_key, axis), (), 0, length) for axis, length in enumerate(entries.shape)]
        where[longest] = (where[longest] + shift) % entries.shape[longest]
        spots.append(tuple(where))
    return entries.at[spots[0]].set(low).at[spots[1]].set(top_value)


def block_levels(key, extent, cuts, low, largest):
    gain, own = 1.0, jax.random.fold_in(key, 6)
    for dim, shards_of in cuts:
        heights = jnp.exp(jax.random.uniform(jax.random.fold_in(own, dim), (shards_of,), jnp.float32, low / len(cuts), largest / len(cuts)))
        gain = gain * jnp.repeat(heights, extent[dim] // shards_of).reshape([-1 if axis == dim else 1 for axis in range(len(extent))])
    return gain


def bell_draw(rng, shape, scale, reach, shards=(), kind=jnp.bfloat16):
    entries = scale * jax.random.normal(rng, shape, jnp.float32)
    if shards:
        entries = entries * block_levels(rng, shape, shards, -0.22, 0.18)
    return jnp.clip(entries, -reach, reach).astype(kind)


def setup_inputs(seed: int = 0) -> dict:
    seeds = jax.random.split(jax.random.key(seed), 14)
    tokens = draw_tokens(jax.random.fold_in(seeds[13], 71), 0)
    targets = bell_draw(seeds[1], (NZ, NLAT, NLON, OUT), 1.0, 6.0, ((0, 4), (1, 32)))
    relief = touch_ends(jax.random.randint(seeds[2], (NLAT, NLON), 0, CLASSES), jax.random.fold_in(seeds[2], 1), 0, CLASSES - 1).astype(jnp.int32)
    earth_bias = draw_earth_bias(jax.random.fold_in(seeds[13], 71), 0)
    relief_table = bell_draw(seeds[4], (CLASSES, D), 0.5, 3.0)
    gain_attn = jnp.clip(1.0 + 0.1 * jax.random.normal(seeds[5], (D,), jnp.float32), 0.5, 1.5)
    gain_mlp = jnp.clip(1.0 + 0.1 * jax.random.normal(seeds[6], (D,), jnp.float32), 0.5, 1.5)
    w_qkv = bell_draw(seeds[7], (D, 3 * D), D ** -0.5, 0.3125)
    w_proj = bell_draw(seeds[8], (D, D), D ** -0.5, 0.3125)
    w_up = bell_draw(seeds[9], (D, FF), D ** -0.5, 0.3125)
    w_down = bell_draw(seeds[10], (FF, D), FF ** -0.5, 0.15625)
    w_out = bell_draw(seeds[11], (D, OUT), D ** -0.5, 0.3125)
    var_weight = jnp.clip(jnp.exp(jax.random.uniform(seeds[12], (VARS,), jnp.float32, math.log(0.5), math.log(4.0))), 0.5, 4.0)
    return dict(tokens=tokens, targets=targets, relief=relief, earth_bias=earth_bias, relief_table=relief_table, gain_attn=gain_attn, gain_mlp=gain_mlp, w_qkv=w_qkv, w_proj=w_proj, w_up=w_up, w_down=w_down, w_out=w_out, var_weight=var_weight)


norm_eps = 1e-05
loss_scale = 32768.0
smooth_sq = 0.01
masked_score = -1e+30

def mult(formula, left_op, right_op):
    return jnp.einsum(formula, left_op.astype(jnp.float32), right_op.astype(jnp.float32))

def exact_mult(formula, left_op, right_op):
    return jnp.einsum(formula, left_op, right_op, precision=lax.Precision.HIGHEST)

def ln_gain(values, gain_vec):
    centre = lax.optimization_barrier(jnp.mean(values, -1, keepdims=True))
    spread = lax.optimization_barrier(jnp.mean((values - centre) ** 2, -1, keepdims=True))
    return (values - centre) * lax.rsqrt(spread + norm_eps) * gain_vec

def gelu_exact(values):
    return jax.nn.gelu(values, approximate=False)

def lat_weights(row_ids, lat_rows):
    fine_rows = 4 * row_ids[:, None] + jnp.arange(4, dtype=jnp.int32)[None, :]
    angle_rad = (90.0 - 180.0 * (fine_rows.astype(jnp.float32) + 0.5) / (4.0 * lat_rows)) * (math.pi / 180.0)
    return jnp.cos(angle_rad)

def cell_weights(level_ids, row_ids, relief_rows, var_weight, lat_rows):
    lat_weight = lat_weights(row_ids, lat_rows)
    levels = 2 * level_ids[:, None] + jnp.arange(2, dtype=jnp.int32)[None, :]
    valid_cells = (levels[:, None, None, :] >= relief_rows[None, :, :, None]).astype(jnp.float32)
    var_count = var_weight.shape[0]
    slots_n, rows_n, lon_n = (valid_cells.shape[0], valid_cells.shape[1], valid_cells.shape[2])
    weight_grid = var_weight[None, None, None, :, None, None, None] * valid_cells[:, :, :, None, :, None, None] * lat_weight[None, :, None, None, None, :, None]
    weight_grid = jnp.broadcast_to(weight_grid, (slots_n, rows_n, lon_n, var_count, 2, 4, 4))
    return weight_grid.reshape(slots_n, rows_n, lon_n, var_count * 32)

def weight_total(relief, var_weight, level_count):
    lat_rows = relief.shape[0]
    lat_weight = lax.optimization_barrier(jnp.sum(lat_weights(jnp.arange(lat_rows, dtype=jnp.int32), lat_rows), 1))
    live_levels = (2 * level_count - relief).astype(jnp.float32)
    return jnp.sum(var_weight) * 4.0 * jnp.sum(lat_weight[:, None] * live_levels)

def window_mask(last_level, last_band, slots_n, rows_n, win_lon):
    slot_label = jnp.where(last_level & (jnp.arange(slots_n) >= slots_n // 2), 2, 0)
    row_label = jnp.where(last_band & (jnp.arange(rows_n) >= rows_n // 2), 1, 0)
    labels = slot_label[:, None, None] + row_label[None, :, None] + jnp.zeros((1, 1, win_lon), jnp.int32)
    labels = labels.reshape(-1)
    return labels[:, None] == labels[None, :]

def windows(field_in, win_lon):
    slots_n, rows_n, lon_n, chans = field_in.shape
    count_w = lon_n // win_lon
    parted = field_in.reshape(slots_n, rows_n, count_w, win_lon, chans).transpose(2, 0, 1, 3, 4)
    return parted.reshape(count_w, slots_n * rows_n * win_lon, chans)

def unwindows(win_in, slots_n, rows_n, win_lon):
    count_w, tokens_n, chans = win_in.shape
    parted = win_in.reshape(count_w, slots_n, rows_n, win_lon, chans).transpose(1, 2, 0, 3, 4)
    return parted.reshape(slots_n, rows_n, count_w * win_lon, chans)

def split_heads(qkv_all, heads_n):
    groups_n, tokens_n, three_d = qkv_all.shape
    model_d = three_d // 3
    head_d = model_d // heads_n
    query_h = qkv_all[..., :model_d].reshape(groups_n, tokens_n, heads_n, head_d)
    key_h = qkv_all[..., model_d:2 * model_d].reshape(groups_n, tokens_n, heads_n, head_d)
    value_h = qkv_all[..., 2 * model_d:].reshape(groups_n, tokens_n, heads_n, head_d)
    return (query_h, key_h, value_h, head_d ** (-0.5))

def attend(qkv_all, bias_blk, allowed):
    query_h, key_h, value_h, factor = split_heads(qkv_all, bias_blk.shape[0])
    groups_n, tokens_n = (qkv_all.shape[0], qkv_all.shape[1])
    scores = mult('gqhe,gkhe->ghqk', query_h, key_h) * factor + bias_blk[None]
    scores = jnp.where(allowed[None, None], scores, masked_score)
    top_row = lax.optimization_barrier(jnp.max(scores, -1, keepdims=True))
    exp_scores = jnp.exp(scores - top_row)
    attn_prob = exp_scores / lax.optimization_barrier(jnp.sum(exp_scores, -1, keepdims=True))
    attended = mult('ghqk,gkhe->gqhe', attn_prob.astype(jnp.bfloat16), value_h).astype(jnp.bfloat16)
    return (attended.reshape(groups_n, tokens_n, -1), attn_prob)

def attend_back(qkv_all, attn_prob, grad_att):
    heads_n = attn_prob.shape[1]
    query_h, key_h, value_h, factor = split_heads(qkv_all, heads_n)
    groups_n, tokens_n = (qkv_all.shape[0], qkv_all.shape[1])
    grad_h = grad_att.reshape(query_h.shape)
    prob_b = attn_prob.astype(jnp.bfloat16)
    grad_prob = mult('gqhe,gkhe->ghqk', grad_h, value_h)
    grad_value = mult('ghqk,gqhe->gkhe', prob_b, grad_h).astype(jnp.bfloat16)
    grad_score = attn_prob * (grad_prob - lax.optimization_barrier(jnp.sum(grad_prob * attn_prob, -1, keepdims=True)))
    score_b = grad_score.astype(jnp.bfloat16)
    grad_query = (mult('ghqk,gkhe->gqhe', score_b, key_h) * factor).astype(jnp.bfloat16)
    grad_key = (mult('ghqk,gqhe->gkhe', score_b, query_h) * factor).astype(jnp.bfloat16)
    grad_heads = jnp.concatenate([grad_query.reshape(groups_n, tokens_n, -1), grad_key.reshape(groups_n, tokens_n, -1), grad_value.reshape(groups_n, tokens_n, -1)], -1)
    return (grad_heads, lax.optimization_barrier(jnp.sum(grad_score, 0)))

def tail(stream, branch, targ_blk, cell_w, gain_mlp, w_up, w_down, w_out, inv_total):
    stream2 = stream + branch.astype(jnp.float32)
    normed2 = ln_gain(stream2, gain_mlp).astype(jnp.bfloat16)
    pre_act = mult('zrwd,df->zrwf', normed2, w_up)
    hidden = gelu_exact(pre_act).astype(jnp.bfloat16)
    output_field = (stream2 + mult('zrwf,fd->zrwd', hidden, w_down)).astype(jnp.bfloat16)
    prediction = mult('zrwd,do->zrwo', output_field, w_out)
    differ = prediction - targ_blk.astype(jnp.float32)
    smooth_err = jnp.sqrt(differ * differ + smooth_sq)
    numerator = jnp.sum(cell_w * smooth_err)
    grad_pred = (inv_total * cell_w * differ / smooth_err).astype(jnp.bfloat16)
    grad_out = mult('zrwd,zrwo->do', output_field, grad_pred)
    grad_field = mult('zrwo,do->zrwd', grad_pred, w_out)
    grad_field_b = grad_field.astype(jnp.bfloat16)
    grad_down = mult('zrwf,zrwd->fd', hidden, grad_field_b)
    grad_hidden = mult('zrwd,fd->zrwf', grad_field_b, w_down)
    gelu_val, gelu_back = jax.vjp(gelu_exact, pre_act)
    grad_pre = gelu_back(grad_hidden)[0].astype(jnp.bfloat16)
    grad_up = mult('zrwd,zrwf->df', normed2, grad_pre)
    grad_normed2 = mult('zrwf,df->zrwd', grad_pre, w_up)
    ln_val, ln_back = jax.vjp(ln_gain, stream2, gain_mlp)
    grad_ln, grad_gain_mlp = ln_back(grad_normed2)
    grad_stream2 = grad_field + grad_ln
    return (numerator, grad_stream2, grad_stream2.astype(jnp.bfloat16), (grad_up, grad_down, grad_out, grad_gain_mlp))

def block_grads(tok_blk, targ_blk, relief_blk, cell_w, bias_blk, allowed, params, inv_total, win_lon):
    relief_table, gain_attn, gain_mlp, w_qkv, w_proj, w_up, w_down, w_out = params
    slots_n, rows_n = (tok_blk.shape[0], tok_blk.shape[1])
    one_hot = (relief_blk[:, :, None] == jnp.arange(relief_table.shape[0], dtype=jnp.int32)).astype(jnp.float32)
    stream = tok_blk.astype(jnp.float32) + exact_mult('rwc,cd->rwd', one_hot, relief_table.astype(jnp.float32))[None]
    normed = ln_gain(stream, gain_attn).astype(jnp.bfloat16)
    win_in = windows(normed, win_lon)
    qkv_all = mult('nqd,de->nqe', win_in, w_qkv).astype(jnp.bfloat16)
    attended, attn_prob = attend(qkv_all, bias_blk, allowed)
    mixed = mult('nqd,de->nqe', attended, w_proj).astype(jnp.bfloat16)
    branch = unwindows(mixed, slots_n, rows_n, win_lon)
    numerator, grad_stream2, grad_branch, tail_grads = tail(stream, branch, targ_blk, cell_w, gain_mlp, w_up, w_down, w_out, inv_total)
    grad_mixed = windows(grad_branch, win_lon)
    grad_proj = mult('nqd,nqe->de', attended, grad_mixed)
    grad_att = mult('nqe,de->nqd', grad_mixed, w_proj).astype(jnp.bfloat16)
    grad_heads, grad_bias = attend_back(qkv_all, attn_prob, grad_att)
    grad_qkv = mult('nqd,nqe->de', win_in, grad_heads)
    grad_shifted = mult('nqe,de->nqd', grad_heads, w_qkv).astype(jnp.bfloat16)
    grad_normed = unwindows(grad_shifted, slots_n, rows_n, win_lon)
    ln_val, ln_back = jax.vjp(ln_gain, stream, gain_attn)
    grad_front, grad_gain_attn = ln_back(grad_normed.astype(jnp.float32))
    grad_stream = grad_stream2 + grad_front
    grad_relief = exact_mult('rwc,zrwd->dc', one_hot, grad_stream)
    grad_up, grad_down, grad_out, grad_gain_mlp = tail_grads
    return (numerator, (grad_qkv, grad_proj, grad_up, grad_down, grad_out, grad_gain_attn, grad_gain_mlp, grad_relief), grad_bias)

def reference(tokens, targets, relief, earth_bias, relief_table, gain_attn, gain_mlp, w_qkv, w_proj, w_up, w_down, w_out, var_weight):
    block_count = N_LVL * N_LAT
    half_rows = ROWS_DEV // 2
    half_lon = WIN_LON // 2
    weight_sum = weight_total(relief, var_weight, NZ)
    inv_total = loss_scale / weight_sum
    rolled_tok = jnp.roll(tokens, (-(LVL_DEV // 2), -half_rows, -half_lon), (0, 1, 2))
    rolled_targ = jnp.roll(targets, (-(LVL_DEV // 2), -half_rows, -half_lon), (0, 1, 2))
    rolled_relief = jnp.roll(relief, (-half_rows, -half_lon), (0, 1))

    def to_blocks(grid_in):
        chans = grid_in.shape[-1]
        parted = grid_in.reshape(N_LVL, LVL_DEV, N_LAT, ROWS_DEV, NLON, chans).transpose(0, 2, 1, 3, 4, 5)
        return parted.reshape(block_count, LVL_DEV, ROWS_DEV, NLON, chans)
    level_grid = jnp.repeat(jnp.arange(N_LVL, dtype=jnp.int32), N_LAT)
    band_grid = jnp.tile(jnp.arange(N_LAT, dtype=jnp.int32), N_LVL)
    bias_blocks = earth_bias.reshape(block_count, HEADS, WIN, WIN)
    params = (relief_table, gain_attn, gain_mlp, w_qkv, w_proj, w_up, w_down, w_out)

    def step_fn(carry, inputs):
        tok_blk, targ_blk, level_id, band_id, bias_blk = inputs
        relief_blk = lax.dynamic_slice_in_dim(rolled_relief, (band_id * ROWS_DEV).astype(jnp.int32), ROWS_DEV, 0)
        level_ids = (level_id * LVL_DEV + jnp.arange(LVL_DEV, dtype=jnp.int32) + LVL_DEV // 2) % NZ
        row_ids = (band_id * ROWS_DEV + jnp.arange(ROWS_DEV, dtype=jnp.int32) + half_rows) % NLAT
        allowed = window_mask(level_id == N_LVL - 1, band_id == N_LAT - 1, LVL_DEV, ROWS_DEV, WIN_LON)
        cell_w = cell_weights(level_ids, row_ids, relief_blk, var_weight, NLAT)
        numerator, grad_set, grad_bias = block_grads(tok_blk, targ_blk, relief_blk, cell_w, bias_blk, allowed, params, inv_total, WIN_LON)
        return ((carry[0] + numerator, jax.tree.map(jnp.add, carry[1], grad_set)), grad_bias)
    zero_set = (jnp.zeros((D, 3 * D), jnp.float32), jnp.zeros((D, D), jnp.float32), jnp.zeros((D, FF), jnp.float32), jnp.zeros((FF, D), jnp.float32), jnp.zeros((D, OUT), jnp.float32), jnp.zeros((D,), jnp.float32), jnp.zeros((D,), jnp.float32), jnp.zeros((D, CLASSES), jnp.float32))
    carry_out, bias_grads = lax.scan(step_fn, (jnp.zeros((), jnp.float32), zero_set), (to_blocks(rolled_tok), to_blocks(rolled_targ), level_grid, band_grid, bias_blocks))
    numerator, grad_set = carry_out
    loss = numerator / weight_sum
    grad_bias = bias_grads.reshape(N_LVL, N_LAT, HEADS, WIN, WIN)
    return (loss, grad_set[0], grad_set[1], grad_set[2], grad_set[3], grad_set[4], grad_set[5], grad_set[6], grad_set[7], grad_bias)
```

```python
import functools
import math

import jax
import jax.numpy as jnp
from jax import lax
from jax.experimental import pallas as pl
from jax.experimental.pallas import tpu as pltpu
from jax.sharding import PartitionSpec as P

WIN_LON = 12
HEADS = 12
norm_eps = 1e-05
loss_scale = 32768.0
smooth_sq = 0.01
masked_score = -1e30
log2_e = math.log2(math.e)
f32 = jnp.float32
bf16 = jnp.bfloat16


def nn(left, right):
    return lax.dot_general(left, right, (((1,), (0,)), ((), ())), preferred_element_type=f32)


def nt(left, right):
    return lax.dot_general(left, right, (((1,), (1,)), ((), ())), preferred_element_type=f32)


def tn(left, right):
    return lax.dot_general(left, right, (((0,), (0,)), ((), ())), preferred_element_type=f32)


def normalize(values):
    width = values.shape[-1]
    centre = jnp.sum(values, -1, keepdims=True) * (1.0 / width)
    moved = values - centre
    spread = jnp.sum(moved * moved, -1, keepdims=True) * (1.0 / width)
    rstd = lax.rsqrt(spread + norm_eps)
    return moved * rstd, rstd


def norm_back(grad_hat, hat, rstd):
    width = hat.shape[-1]
    mean_g = jnp.sum(grad_hat, -1, keepdims=True) * (1.0 / width)
    mean_gh = jnp.sum(grad_hat * hat, -1, keepdims=True) * (1.0 / width)
    return rstd * (grad_hat - mean_g - hat * mean_gh)


def gelu_both(x):
    dens = jnp.exp2(x * x * (-0.5 * log2_e))
    den = 1.0 + jnp.abs(x) * (0.3275911 / math.sqrt(2.0))
    t = pl.reciprocal(den, approx=True)
    t = t * (2.0 - den * t)
    poly = 0.5 * 1.061405429
    for coef in (-1.453152027, 1.421413741, -0.284496736, 0.254829592):
        poly = poly * t + 0.5 * coef
    side = poly * t * dens
    cdf = jnp.where(x >= 0.0, 1.0 - side, side)
    return x * cdf, cdf + x * dens * (1.0 / math.sqrt(2.0 * math.pi))


def one_hot_of(relief_col, classes):
    ids = lax.broadcasted_iota(jnp.int32, (relief_col.shape[0], classes), 1)
    return (relief_col == ids).astype(f32).astype(bf16)


def stream_of(x_ref, relief_ref, table_ref):
    one_hot = one_hot_of(relief_ref[...], table_ref.shape[0])
    return x_ref[...].astype(f32) + nn(one_hot, table_ref[...]), one_hot


def att_kernel(
    x_ref,
    relief_ref,
    table_ref,
    gain_ref,
    wt_ref,
    wv_ref,
    wk_ref,
    wproj_ref,
    bias_ref,
    stream2_ref,
    qkt_ref,
    v_ref,
    prob_ref,
    att_ref,
):
    stream, _ = stream_of(x_ref, relief_ref, table_ref)
    hat, _ = normalize(stream)
    normed = (hat * gain_ref[...]).astype(bf16)
    d = normed.shape[1]
    e = d // HEADS
    qkvt = nt(wt_ref[...], normed)
    qt = (qkvt[:d] * (log2_e * e**-0.5)).astype(bf16)
    kt = qkvt[d : 2 * d].astype(bf16)
    vt = qkvt[2 * d :].astype(bf16)
    qkt_ref[0, :d] = qt
    qkt_ref[0, d:] = kt
    k_tok = nn(normed, wk_ref[...]).astype(bf16)
    v_ref[...] = nn(normed, wv_ref[...]).astype(bf16)
    per = 128 // e
    for h in range(HEADS):
        g, j = h // per, h % per
        parts = [jnp.zeros((e, qt.shape[1]), bf16)] * per
        parts[j] = qt[h * e : (h + 1) * e]
        q_one = jnp.concatenate(parts, 0)
        scores = nn(k_tok[:, g * 128 : (g + 1) * 128], q_one) + bias_ref[h]
        top = jnp.max(scores, 0, keepdims=True)
        probs = jnp.exp2(scores - top)
        probs = (probs * (1.0 / jnp.sum(probs, 0, keepdims=True))).astype(bf16)
        prob_ref[0, h] = probs
        att_ref[0, h * e : (h + 1) * e] = nn(vt[h * e : (h + 1) * e], probs).astype(bf16)
    mixed = tn(att_ref[0], wproj_ref[...]).astype(bf16)
    stream2_ref[...] = stream + mixed.astype(f32)


def tail_kernel(
    scale_ref,
    stream2_ref,
    targ_ref,
    relief_ref,
    lev_ref,
    base_ref,
    att_ref,
    gain_ref,
    wup_ref,
    wdown_ref,
    wout_ref,
    num_ref,
    gs2_ref,
    gproj_ref,
    gup_ref,
    gdown_ref,
    gout_ref,
    hid_ref,
    slope_ref,
    *,
    block_f,
):
    step = pl.program_id(0)

    @pl.when(step == 0)
    def _():
        num_ref[...] = jnp.zeros_like(num_ref)
        gproj_ref[...] = jnp.zeros_like(gproj_ref)
        gup_ref[...] = jnp.zeros_like(gup_ref)
        gdown_ref[...] = jnp.zeros_like(gdown_ref)
        gout_ref[...] = jnp.zeros_like(gout_ref)

    stream2 = stream2_ref[...]
    wins, win = att_ref.shape[0], att_ref.shape[2]
    ff = wup_ref.shape[1]
    hat, rstd = normalize(stream2)
    gain = gain_ref[...]
    normed2 = (hat * gain).astype(bf16)
    for n in range(0, ff, block_f):
        cols = slice(n, n + block_f)
        hidden, slope = gelu_both(nn(normed2, wup_ref[:, cols]))
        hid_ref[:, cols] = hidden.astype(bf16)
        slope_ref[:, cols] = slope.astype(bf16)
    field = (stream2 + nn(hid_ref[...], wdown_ref[...])).astype(bf16)
    pred = nn(field, wout_ref[...])
    relief = relief_ref[...]
    lev = jnp.concatenate([lev_ref[...]] * wins, 0)
    base = jnp.concatenate([base_ref[...]] * wins, 0)
    cell_w = jnp.where(lev >= relief, base, 0.0)
    differ = pred - targ_ref[...].astype(f32)
    square = differ * differ + smooth_sq
    inv_err = lax.rsqrt(square)
    num_ref[...] += jnp.sum(cell_w * (square * inv_err), 0, keepdims=True)
    gpred = (scale_ref[0] * cell_w * differ * inv_err).astype(bf16)
    gout_ref[...] += nn(field.T, gpred)
    gfield = nt(gpred, wout_ref[...])
    gfb = gfield.astype(bf16)
    gfbt = gfb.T
    normed2t = normed2.T
    for n in range(0, ff, block_f):
        cols = slice(n, n + block_f)
        gdown_ref[:, cols] += nn(gfbt, hid_ref[:, cols])
        ghid = nt(gfb, wdown_ref[cols, :])
        gpre = (slope_ref[:, cols].astype(f32) * ghid).astype(bf16)
        slope_ref[:, cols] = gpre
        gup_ref[:, cols] += nn(normed2t, gpre)
    gnorm2 = nt(slope_ref[...], wup_ref[...])
    gs2 = gfield + norm_back(gnorm2 * gain, hat, rstd)
    gs2_ref[...] = gs2
    gmix = gs2.astype(bf16)
    for w in range(wins):
        gproj_ref[...] += nn(att_ref[w], gmix[w * win : (w + 1) * win])


def back_kernel(
    x_ref,
    relief_ref,
    table_ref,
    gain_ref,
    wqkv_ref,
    wproj_ref,
    qkt_ref,
    v_ref,
    prob_ref,
    att_ref,
    gs2_ref,
    gbias_ref,
    gqkv_ref,
    grel_ref,
    gh_ref,
):
    step = pl.program_id(0)

    @pl.when(step == 0)
    def _():
        gbias_ref[...] = jnp.zeros_like(gbias_ref)
        gqkv_ref[...] = jnp.zeros_like(gqkv_ref)
        grel_ref[...] = jnp.zeros_like(grel_ref)

    stream, one_hot = stream_of(x_ref, relief_ref, table_ref)
    hat, rstd = normalize(stream)
    gain = gain_ref[...]
    normed = (hat * gain).astype(bf16)
    d = normed.shape[1]
    e = d // HEADS
    per = 128 // e
    gs2 = gs2_ref[...]
    gatt = nt(wproj_ref[...], gs2.astype(bf16))
    gatt_b = gatt.astype(bf16)
    prod = gatt_b.astype(f32) * att_ref[0].astype(f32)
    for h in range(HEADS):
        g, j = h // per, h % per
        rows = slice(h * e, (h + 1) * e)
        go = gatt_b[rows]
        parts = [jnp.zeros_like(go)] * per
        parts[j] = go
        delta = jnp.sum(prod[rows], 0, keepdims=True)
        gprob = nn(v_ref[:, g * 128 : (g + 1) * 128], jnp.concatenate(parts, 0))
        probs = prob_ref[0, h]
        gscore = probs.astype(f32) * (gprob - delta)
        gbias_ref[h] += gscore
        gsb = gscore.astype(bf16)
        gh_ref[rows] = (nn(qkt_ref[0, d + h * e : d + (h + 1) * e], gsb) * e**-0.5).astype(bf16)
        gh_ref[d + h * e : d + (h + 1) * e] = (nt(qkt_ref[0, rows], gsb) * (1.0 / log2_e)).astype(
            bf16
        )
        gh_ref[2 * d + h * e : 2 * d + (h + 1) * e] = nt(go, probs).astype(bf16)
    gheads = gh_ref[...]
    gqkv_ref[...] += nn(gheads, normed)
    gshift = nn(wqkv_ref[...], gheads).astype(bf16).T.astype(f32)
    gstream = gs2 + norm_back(gshift * gain, hat, rstd)
    grel_ref[...] += tn(one_hot, gstream.astype(bf16))


def whole(shape):
    return pl.BlockSpec(shape, lambda i: (0,) * len(shape))


def lead(shape):
    return pl.BlockSpec(shape, lambda i: (i,) + (0,) * (len(shape) - 1))


def params_of():
    return pltpu.CompilerParams(
        vmem_limit_bytes=56 * 2**20, dimension_semantics=("arbitrary",)
    )


def attention_forward(x, relief_col, table, gain, w_qkv, w_proj, bias_t):
    t, d = x.shape
    win = bias_t.shape[-1]
    count = t // win
    sds = jax.ShapeDtypeStruct
    return pl.pallas_call(
        att_kernel,
        grid=(count,),
        in_specs=[
            lead((win, d)),
            lead((win, 1)),
            whole(table.shape),
            whole((1, d)),
            whole((3 * d, d)),
            whole((d, d)),
            whole((d, d)),
            whole((d, d)),
            whole(bias_t.shape),
        ],
        out_specs=[
            lead((win, d)),
            lead((1, 2 * d, win)),
            lead((win, d)),
            lead((1, HEADS, win, win)),
            lead((1, d, win)),
        ],
        out_shape=[
            sds((t, d), f32),
            sds((count, 2 * d, win), bf16),
            sds((t, d), bf16),
            sds((count, HEADS, win, win), bf16),
            sds((count, d, win), bf16),
        ],
        compiler_params=params_of(),
        name="attention_forward",
    )(
        x,
        relief_col,
        table,
        gain[None],
        w_qkv.T,
        w_qkv[:, 2 * d :],
        w_qkv[:, d : 2 * d],
        w_proj,
        bias_t,
    )


def tail_both(scale, stream2, targ, relief_col, lev, base, att, gain, w_up, w_down, w_out, group):
    t, d = stream2.shape
    win = att.shape[-1]
    m = group * win
    ff, out = w_up.shape[1], w_out.shape[1]
    sds = jax.ShapeDtypeStruct
    return pl.pallas_call(
        functools.partial(tail_kernel, block_f=256),
        grid=(t // m,),
        in_specs=[
            pl.BlockSpec(memory_space=pltpu.SMEM),
            lead((m, d)),
            lead((m, out)),
            lead((m, 1)),
            whole((win, out)),
            whole((win, out)),
            lead((group, d, win)),
            whole((1, d)),
            whole((d, ff)),
            whole((ff, d)),
            whole((d, out)),
        ],
        out_specs=[
            whole((1, out)),
            lead((m, d)),
            whole((d, d)),
            whole((d, ff)),
            whole((d, ff)),
            whole((d, out)),
        ],
        out_shape=[
            sds((1, out), f32),
            sds((t, d), f32),
            sds((d, d), f32),
            sds((d, ff), f32),
            sds((d, ff), f32),
            sds((d, out), f32),
        ],
        scratch_shapes=[pltpu.VMEM((m, ff), bf16), pltpu.VMEM((m, ff), bf16)],
        compiler_params=params_of(),
        name="tail_both",
    )(scale, stream2, targ, relief_col, lev, base, att, gain[None], w_up, w_down, w_out)


def attention_back(x, relief_col, table, gain, w_qkv, w_proj, qkt, v_tok, probs, att, gs2):
    t, d = x.shape
    count, win = att.shape[0], att.shape[2]
    sds = jax.ShapeDtypeStruct
    return pl.pallas_call(
        back_kernel,
        grid=(count,),
        in_specs=[
            lead((win, d)),
            lead((win, 1)),
            whole(table.shape),
            whole((1, d)),
            whole((d, 3 * d)),
            whole((d, d)),
            lead((1, 2 * d, win)),
            lead((win, d)),
            lead((1, HEADS, win, win)),
            lead((1, d, win)),
            lead((win, d)),
        ],
        out_specs=[
            whole((HEADS, win, win)),
            whole((3 * d, d)),
            whole((table.shape[0], d)),
        ],
        out_shape=[
            sds((HEADS, win, win), f32),
            sds((3 * d, d), f32),
            sds((table.shape[0], d), f32),
        ],
        scratch_shapes=[pltpu.VMEM((3 * d, win), bf16)],
        compiler_params=params_of(),
        name="attention_back",
    )(x, relief_col, table, gain[None], w_qkv, w_proj, qkt, v_tok, probs, att, gs2)


def lat_weights(row_ids, lat_rows):
    fine_rows = 4 * row_ids[:, None] + jnp.arange(4, dtype=jnp.int32)[None, :]
    angle_rad = (90.0 - 180.0 * (fine_rows.astype(f32) + 0.5) / (4.0 * lat_rows)) * (
        math.pi / 180.0
    )
    return jnp.cos(angle_rad)


def weight_total(relief, var_weight, level_count):
    lat_rows = relief.shape[0]
    lat_weight = jnp.sum(lat_weights(jnp.arange(lat_rows, dtype=jnp.int32), lat_rows), 1)
    live_levels = (2 * level_count - relief).astype(f32)
    return jnp.sum(var_weight) * 4.0 * jnp.sum(lat_weight[:, None] * live_levels)


def window_mask(last_level, last_band, slots_n, rows_n, win_lon):
    slot_label = jnp.where(last_level & (jnp.arange(slots_n) >= slots_n // 2), 2, 0)
    row_label = jnp.where(last_band & (jnp.arange(rows_n) >= rows_n // 2), 1, 0)
    labels = (
        slot_label[:, None, None] + row_label[None, :, None] + jnp.zeros((1, 1, win_lon), jnp.int32)
    )
    labels = labels.reshape(-1)
    return labels[:, None] == labels[None, :]


def windows(field_in):
    slots_n, rows_n, lon_n, chans = field_in.shape
    count_w = lon_n // WIN_LON
    parted = field_in.reshape(slots_n, rows_n, count_w, WIN_LON, chans).transpose(2, 0, 1, 3, 4)
    return parted.reshape(count_w * slots_n * rows_n * WIN_LON, chans)


def from_next(value, axes):
    sizes = [lax.axis_size(a) for a in ("lvl", "lat")]
    move = [1 if a in axes else 0 for a in ("lvl", "lat")]
    pairs = []
    for i in range(sizes[0]):
        for j in range(sizes[1]):
            src = (i + move[0]) % sizes[0] * sizes[1] + (j + move[1]) % sizes[1]
            pairs.append((src, i * sizes[1] + j))
    return lax.ppermute(value, ("lvl", "lat"), pairs)


def shifted_windows(field_in):
    slots_n, rows_n = field_in.shape[:2]
    hs, hr = slots_n // 2, rows_n // 2
    up = from_next(field_in[:hs, hr:], ("lvl",))
    side = from_next(field_in[hs:, :hr], ("lat",))
    both = from_next(field_in[:hs, :hr], ("lvl", "lat"))
    rolled = jnp.concatenate(
        [
            jnp.concatenate([field_in[hs:, hr:], side], 1),
            jnp.concatenate([up, both], 1),
        ],
        0,
    )
    return windows(jnp.roll(rolled, -(WIN_LON // 2), 2))


def local_inputs(tokens_shape, relief, earth_bias, var_weight):
    slots_dev, rows_dev, lon_cells, _ = tokens_shape
    lvl_count, lat_count = lax.axis_size("lvl"), lax.axis_size("lat")
    lvl_id, lat_id = lax.axis_index("lvl"), lax.axis_index("lat")
    level_total, lat_rows = slots_dev * lvl_count, rows_dev * lat_count
    allowed = window_mask(
        lvl_id == lvl_count - 1, lat_id == lat_count - 1, slots_dev, rows_dev, WIN_LON
    )
    level_ids = (
        lvl_id * slots_dev + jnp.arange(slots_dev, dtype=jnp.int32) + slots_dev // 2
    ) % level_total
    row_ids = (
        lat_id * rows_dev + jnp.arange(rows_dev, dtype=jnp.int32) + rows_dev // 2
    ) % lat_rows
    relief_blk = jnp.roll(jnp.take(relief, row_ids, axis=0), -(WIN_LON // 2), 1)
    relief_col = windows(
        jnp.broadcast_to(relief_blk[None, :, :, None], (slots_dev, rows_dev, lon_cells, 1))
    )
    shape = (slots_dev, rows_dev, WIN_LON, var_weight.shape[0], 2, 4, 4)
    levels = 2 * level_ids[:, None] + jnp.arange(2, dtype=jnp.int32)[None, :]
    lev = jnp.broadcast_to(levels[:, None, None, None, :, None, None], shape)
    base = jnp.broadcast_to(
        var_weight[None, None, None, :, None, None, None]
        * lat_weights(row_ids, lat_rows)[None, :, None, None, None, :, None],
        shape,
    )
    win = slots_dev * rows_dev * WIN_LON
    bias_t = jnp.where(allowed, earth_bias.transpose(0, 2, 1) * log2_e, masked_score)
    return relief_col, lev.reshape(win, -1), base.reshape(win, -1), bias_t


def body(
    tokens,
    targets,
    relief,
    earth_bias,
    relief_table,
    gain_attn,
    gain_mlp,
    w_qkv,
    w_proj,
    w_up,
    w_down,
    w_out,
    var_weight,
):
    axes = ("lvl", "lat")
    devs = lax.axis_size("lvl") * lax.axis_size("lat")
    level_total = tokens.shape[0] * lax.axis_size("lvl")
    weight_sum = weight_total(relief, var_weight, level_total)
    x = shifted_windows(tokens)
    targ = shifted_windows(targets)
    relief_col, lev, base, bias_t = local_inputs(tokens.shape, relief, earth_bias[0, 0], var_weight)
    stream2, qkt, v_tok, probs, att = attention_forward(
        x, relief_col, relief_table, gain_attn, w_qkv, w_proj, bias_t
    )
    scale = (loss_scale / weight_sum).reshape(1)
    num, gs2, gproj, gup, gdown_t, gout = tail_both(
        scale, stream2, targ, relief_col, lev, base, att, gain_mlp, w_up, w_down, w_out, 3
    )
    gbias_t, gqkv_t, grel = attention_back(
        x, relief_col, relief_table, gain_attn, w_qkv, w_proj, qkt, v_tok, probs, att, gs2
    )
    gbias = gbias_t.transpose(0, 2, 1)
    pieces = [
        gqkv_t.T.reshape(devs, -1),
        gproj.reshape(devs, -1),
        gup.reshape(devs, -1),
        gdown_t.T.reshape(devs, -1),
        gout.reshape(devs, -1),
        grel.T.reshape(devs, -1),
        jnp.broadcast_to(jnp.sum(num), (devs, 1)),
    ]
    flat = jnp.concatenate(pieces, 1)
    high = flat.astype(bf16)
    low_num = (flat[:, -1:] - high[:, -1:].astype(f32)).astype(bf16)
    send = jnp.concatenate([high, low_num], 1)
    pad = -send.shape[1] % 2048
    send = jnp.pad(send, ((0, 0), (0, pad))).reshape(devs, -1, 128)
    got = lax.all_to_all(send, axes, 0, 0, tiled=True)
    total = jnp.sum(got.astype(f32), 0).reshape(-1)
    outs, at = [], 0
    d = tokens.shape[-1]
    for cols in (
        (d // devs, w_qkv.shape[1]),
        (d // devs, d),
        (d // devs, w_up.shape[1]),
        (w_down.shape[0] // devs, d),
        (d // devs, w_out.shape[1]),
        (d // devs, relief_table.shape[0]),
    ):
        size = cols[0] * cols[1]
        outs.append(total[at : at + size].reshape(cols))
        at += size
    grad_qkv, grad_proj, grad_up, grad_down, grad_out, grad_relief = outs
    numerator = total[at] + total[at + 1]
    me = lax.axis_index(axes)

    def mine(array):
        return lax.dynamic_slice_in_dim(array, me * (d // devs), d // devs, 0)

    grad_gain_attn = jnp.sum(mine(w_qkv).astype(f32) * grad_qkv, 1) / mine(gain_attn)
    grad_gain_mlp = jnp.sum(mine(w_up).astype(f32) * grad_up, 1) / mine(gain_mlp)
    return (
        numerator / weight_sum,
        grad_qkv,
        grad_proj,
        grad_up,
        grad_down,
        grad_out,
        grad_gain_attn,
        grad_gain_mlp,
        grad_relief,
        gbias[None, None],
    )


def solution(mesh):
    field = P("lvl", "lat", None, None)
    bias = P("lvl", "lat", None, None, None)
    rows = P(("lvl", "lat"), None)
    vec = P(("lvl", "lat"))
    return jax.shard_map(
        body,
        mesh=mesh,
        in_specs=(field, field, P(), bias) + (P(),) * 9,
        out_specs=(P(), rows, rows, rows, rows, rows, vec, vec, rows, bias),
        check_vma=False,
    )
```

```python
import functools
import math

import jax
import jax.numpy as jnp
from jax import lax
from jax.experimental import pallas as pl
from jax.experimental.pallas import tpu as pltpu
from jax.sharding import PartitionSpec as P

WIN_LON = 12
HEADS = 12
GROUP = 6
DEVS = 128
WIDE = 256
TOGETHER = 3
norm_eps = 1e-05
loss_scale = 32768.0
smooth_sq = 0.01
masked_score = -1e30
log2_e = math.log2(math.e)
f32 = jnp.float32
bf16 = jnp.bfloat16


def nn(left, right):
    return lax.dot_general(left, right, (((1,), (0,)), ((), ())), preferred_element_type=f32)


def nt(left, right):
    return lax.dot_general(left, right, (((1,), (1,)), ((), ())), preferred_element_type=f32)


def tn(left, right):
    return lax.dot_general(left, right, (((0,), (0,)), ((), ())), preferred_element_type=f32)


def normalize(values):
    width = values.shape[-1]
    centre = jnp.sum(values, -1, keepdims=True) * (1.0 / width)
    moved = values - centre
    spread = jnp.sum(moved * moved, -1, keepdims=True) * (1.0 / width)
    rstd = lax.rsqrt(spread + norm_eps)
    return moved * rstd, rstd


def norm_back(grad_hat, hat, rstd):
    width = hat.shape[-1]
    mean_g = jnp.sum(grad_hat, -1, keepdims=True) * (1.0 / width)
    mean_gh = jnp.sum(grad_hat * hat, -1, keepdims=True) * (1.0 / width)
    return rstd * (grad_hat - mean_g - hat * mean_gh)


def gelu_both(x):
    dens = jnp.exp2(x * x * (-0.5 * log2_e))
    den = 1.0 + jnp.abs(x) * (0.3275911 / math.sqrt(2.0))
    t = pl.reciprocal(den, approx=True)
    t = t * (2.0 - den * t)
    poly = 0.5 * 1.061405429
    for coef in (-1.453152027, 1.421413741, -0.284496736, 0.254829592):
        poly = poly * t + 0.5 * coef
    side = poly * t * dens
    cdf = jnp.where(x >= 0.0, 1.0 - side, side)
    return x * cdf, cdf + x * dens * (1.0 / math.sqrt(2.0 * math.pi))


def own_rows(me, weight_ref):
    rows = weight_ref.shape[0]
    share = rows // DEVS
    ids = lax.broadcasted_iota(jnp.int32, (8, rows), 0) + me * share
    picks = (lax.broadcasted_iota(jnp.int32, (8, rows), 1) == ids).astype(f32).astype(bf16)
    return nn(picks, weight_ref[...])


def pack_rows(send_ref, at, piece_ref):
    pieces, rows, _ = piece_ref.shape
    share = rows // DEVS
    every = send_ref.shape[0] // DEVS
    for i in range(share):
        for c in range(pieces):
            block = piece_ref[c, pl.ds(i, DEVS, stride=share), :]
            send_ref[pl.ds(at, DEVS, stride=every), :] = block
            at += 1
    return at


def fill_rows(send_ref, at):
    every = send_ref.shape[0] // DEVS
    for j in range(at, every):
        send_ref[pl.ds(j, DEVS, stride=every), :] = jnp.zeros((DEVS, 128), f32)


def cut_pieces(piece_ref, grad_ref):
    for c in range(piece_ref.shape[0]):
        piece_ref[c] = grad_ref[:, c * 128 : (c + 1) * 128]


def turn_pieces(piece_ref, grad_t_ref):
    for c in range(piece_ref.shape[0]):
        piece_ref[c] = grad_t_ref[c * 128 : (c + 1) * 128].T


def one_hot_of(relief_col, classes):
    ids = lax.broadcasted_iota(jnp.int32, (relief_col.shape[0], classes), 1)
    return (relief_col == ids).astype(f32).astype(bf16)


def alone(part, place, count):
    parts = [jnp.zeros_like(part)] * count
    parts[place] = part
    return jnp.concatenate(parts, 0)


def stream_of(x_ref, relief_ref, table_ref):
    one_hot = one_hot_of(relief_ref[...], table_ref.shape[0])
    return x_ref[...].astype(f32) + nn(one_hot, table_ref[...]), one_hot


def att_kernel(
    x_ref,
    relief_ref,
    table_ref,
    gain_ref,
    wt_ref,
    wv_ref,
    wk_ref,
    wproj_ref,
    bias_ref,
    stream2_ref,
    qkt_ref,
    v_ref,
    prob_ref,
    att_ref,
):
    stream, _ = stream_of(x_ref, relief_ref, table_ref)
    hat, _ = normalize(stream)
    normed = (hat * gain_ref[...]).astype(bf16)
    d = normed.shape[1]
    count, win = att_ref.shape[0], att_ref.shape[2]
    k_tok = nn(normed, wk_ref[...]).astype(bf16)
    v_tok = nn(normed, wv_ref[...]).astype(bf16)
    e = d // HEADS
    per = 128 // e
    qkvts = []
    for u in range(count):
        rows = slice(u * win, (u + 1) * win)
        filled = jnp.concatenate([normed[rows], jnp.zeros((WIDE - win, d), bf16)], 0)
        qkvts.append(nt(wt_ref[...], filled))
    mixed = []
    for u in range(count):
        rows = slice(u * win, (u + 1) * win)
        qt = (qkvts[u][:d] * (log2_e * e**-0.5)).astype(bf16)
        kt = qkvts[u][d : 2 * d].astype(bf16)
        vt = qkvts[u][2 * d :].astype(bf16)
        att = []
        for g in range(d // 128):
            k_four = k_tok[rows, g * 128 : (g + 1) * 128]
            heads = range(g * per, (g + 1) * per)
            scores = [nn(k_four, alone(qt[h * e : (h + 1) * e], h % per, per)) for h in heads]
            probs = []
            for h, score in zip(heads, scores):
                score = score + bias_ref[h]
                top = jnp.max(score, 0, keepdims=True)
                prob = jnp.exp2(score - top)
                prob = (prob * (1.0 / jnp.sum(prob, 0, keepdims=True))).astype(bf16)
                probs.append(prob)
                prob_ref[u, h] = prob
            att += [nn(vt[h * e : (h + 1) * e, :win], prob) for h, prob in zip(heads, probs)]
        att = jnp.concatenate(att, 0).astype(bf16)[:, :win]
        att_ref[u] = att
        qkt_ref[u, :d] = qt
        qkt_ref[u, d:] = kt
        mixed.append(tn(att, wproj_ref[...]).astype(bf16))
    v_ref[...] = v_tok
    stream2_ref[...] = stream + jnp.concatenate(mixed, 0).astype(f32)


def tail_kernel(
    me_ref,
    scale_ref,
    stream2_ref,
    targ_ref,
    relief_ref,
    levels_ref,
    base_ref,
    att_ref,
    gain_ref,
    wup_ref,
    wdown_ref,
    wout_ref,
    num_ref,
    gs2_ref,
    send_ref,
    wsel_ref,
    lev_ref,
    wide_ref,
    gproj_ref,
    gup_ref,
    gdown_ref,
    gout_ref,
    piece_ref,
    gdown_t_ref,
    pack_ref,
    *,
    block_f,
):
    step = pl.program_id(0)
    me = me_ref[0]

    @pl.when(step == 0)
    def _():
        slots, rows = levels_ref.shape[0], base_ref.shape[0]
        shape = lev_ref.shape
        token = lax.broadcasted_iota(jnp.int32, shape, 0)
        upper = (lax.broadcasted_iota(jnp.int32, shape, 1) // 16) % 2
        line = token // WIN_LON
        lev = jnp.full(shape, 2 * levels_ref[0], jnp.int32)
        for s in range(1, slots):
            lev = jnp.where(line >= s * rows, 2 * levels_ref[s], lev)
        lev_ref[...] = lev + upper
        wide = jnp.zeros(shape, f32)
        for r in range(rows):
            wide = jnp.where(line % rows == r, base_ref[r : r + 1], wide)
        wide_ref[...] = wide
        num_ref[...] = jnp.zeros_like(num_ref)
        gproj_ref[...] = jnp.zeros_like(gproj_ref)
        gup_ref[...] = jnp.zeros_like(gup_ref)
        gdown_ref[...] = jnp.zeros_like(gdown_ref)
        gout_ref[...] = jnp.zeros_like(gout_ref)

    stream2 = stream2_ref[...]
    wins, win = att_ref.shape[0], att_ref.shape[2]
    ff = wup_ref.shape[1]
    hat, rstd = normalize(stream2)
    gain = gain_ref[...]
    normed2 = (hat * gain).astype(bf16)
    hids, slopes, gpres = [], [], []
    for n in range(0, ff, block_f):
        cols = slice(n, n + block_f)
        hidden, slope = gelu_both(nn(normed2, wup_ref[:, cols]))
        hids.append(hidden.astype(bf16))
        slopes.append(slope.astype(bf16))
    field = (stream2 + nn(jnp.concatenate(hids, 1), wdown_ref[...])).astype(bf16)
    pred = nn(field, wout_ref[...])
    relief = relief_ref[...]
    lev = jnp.concatenate([lev_ref[...]] * wins, 0)
    base = jnp.concatenate([wide_ref[...]] * wins, 0)
    cell_w = jnp.where(lev >= relief, base, 0.0)
    differ = pred - targ_ref[...].astype(f32)
    square = differ * differ + smooth_sq
    inv_err = lax.rsqrt(square)
    num_ref[...] += jnp.sum(cell_w * (square * inv_err), 0, keepdims=True)
    gpred = (scale_ref[0] * cell_w * differ * inv_err).astype(bf16)
    out = gpred.shape[1]
    gout_ref[:, :out] += nn(field.T, gpred)
    gfield = nt(gpred, wout_ref[...])
    gfb = gfield.astype(bf16)
    gfbt = gfb.T
    normed2t = normed2.T
    for n in range(0, ff, block_f):
        cols = slice(n, n + block_f)
        ghid = nt(gfb, wdown_ref[cols, :])
        gpres.append((slopes[n // block_f].astype(f32) * ghid).astype(bf16))
    for n in range(0, ff, block_f):
        cols = slice(n, n + block_f)
        gdown_ref[:, cols] += nn(gfbt, hids[n // block_f])
        gup_ref[:, cols] += nn(normed2t, gpres[n // block_f])
    gnorm2 = nt(jnp.concatenate(gpres, 1), wup_ref[...])
    gs2 = gfield + norm_back(gnorm2 * gain, hat, rstd)
    gs2_ref[...] = gs2
    gmix = gs2.astype(bf16)
    for w in range(wins):
        gproj_ref[...] += nn(att_ref[w], gmix[w * win : (w + 1) * win])

    @pl.when(step == pl.num_programs(0) - 1)
    def _():
        wsel_ref[...] = own_rows(me, wup_ref)
        at = 0
        for ref in (gup_ref, gproj_ref, gout_ref):
            pieces = piece_ref.at[: ref.shape[1] // 128]
            cut_pieces(pieces, ref)
            at = pack_rows(pack_ref, at, pieces)
        turn_pieces(gdown_t_ref, gdown_ref)
        at = pack_rows(pack_ref, at, gdown_t_ref)
        fill_rows(pack_ref, at)
        send_ref[...] = pack_ref[...].astype(bf16)


def back_kernel(
    me_ref,
    x_ref,
    relief_ref,
    table_ref,
    gain_ref,
    wqkv_ref,
    wproj_ref,
    qkt_ref,
    v_ref,
    prob_ref,
    att_ref,
    gs2_ref,
    num_ref,
    gbias_ref,
    send_ref,
    wsel_ref,
    gqkv_ref,
    gqkv_t_ref,
    grel_ref,
    grel_t_ref,
    pack_ref,
):
    step = pl.program_id(0)

    @pl.when(step == 0)
    def _():
        gbias_ref[...] = jnp.zeros_like(gbias_ref)
        gqkv_ref[...] = jnp.zeros_like(gqkv_ref)
        grel_ref[...] = jnp.zeros_like(grel_ref)

    stream, one_hot = stream_of(x_ref, relief_ref, table_ref)
    hat, rstd = normalize(stream)
    gain = gain_ref[...]
    normed = (hat * gain).astype(bf16)
    d = normed.shape[1]
    count, win = att_ref.shape[0], att_ref.shape[2]
    e = d // HEADS
    per = 128 // e
    gs2 = gs2_ref[...]
    gmix = gs2.astype(bf16)
    pad = jnp.zeros((WIDE - win, d), bf16)
    gatts = []
    for u in range(count):
        filled = jnp.concatenate([gmix[u * win : (u + 1) * win], pad], 0)
        gatts.append(nt(wproj_ref[...], filled).astype(bf16))
    v_tok = v_ref[...]
    gshift = []
    for u in range(count):
        wrows = slice(u * win, (u + 1) * win)
        gatt_b = gatts[u]
        prod = gatt_b[:, :win].astype(f32) * att_ref[u].astype(f32)
        prod = jnp.concatenate([prod, jnp.zeros((d, WIDE - win), f32)], 1)
        qt, kt = qkt_ref[u, :d], qkt_ref[u, d:, :win]
        gqs, gks, gvs = [], [], []
        for g in range(d // 128):
            v_four = v_tok[wrows, g * 128 : (g + 1) * 128]
            heads = range(g * per, (g + 1) * per)
            gprobs = [nn(v_four, alone(gatt_b[h * e : (h + 1) * e], h % per, per)) for h in heads]
            gscores = []
            probs = [prob_ref[u, h] for h in heads]
            for h, gprob, prob in zip(heads, gprobs, probs):
                delta = jnp.sum(prod[h * e : (h + 1) * e], 0, keepdims=True)
                gscore = prob.astype(f32) * (gprob - delta)
                gbias_ref[h] += gscore
                gscores.append(gscore.astype(bf16))
            for h, gsb, prob in zip(heads, gscores, probs):
                rows = slice(h * e, (h + 1) * e)
                gqs.append((nn(kt[rows], gsb) * e**-0.5).astype(bf16)[:, :win])
                gks.append((nt(qt[rows], gsb) * (1.0 / log2_e)).astype(bf16))
                gvs.append(nt(gatt_b[rows], prob).astype(bf16))
        gheads = jnp.concatenate(gqs + gks + gvs, 0)
        gqkv_ref[...] += nn(gheads, normed[wrows])
        gshift.append(nn(wqkv_ref[...], gheads).astype(bf16).T.astype(f32))
    gshift = jnp.concatenate(gshift, 0)
    gstream = gs2 + norm_back(gshift * gain, hat, rstd)
    grel_ref[...] += tn(one_hot, gstream.astype(bf16))

    @pl.when(step == pl.num_programs(0) - 1)
    def _():
        wsel_ref[...] = own_rows(me_ref[0], wqkv_ref)
        turn_pieces(gqkv_t_ref, gqkv_ref)
        at = pack_rows(pack_ref, 0, gqkv_t_ref)
        classes = grel_ref.shape[0]
        wide = jnp.concatenate([grel_ref[...], jnp.zeros((128 - classes, d), f32)], 0)
        grel_t_ref[...] = wide.T
        share = d // DEVS
        num = jnp.sum(num_ref[...], 1, keepdims=True)
        high = num.astype(bf16).astype(f32)
        lane = lax.broadcasted_iota(jnp.int32, (DEVS, 128), 1)
        last = jnp.where(lane == 126, high, jnp.where(lane == 127, num - high, 0.0))
        for i in range(share):
            part = grel_t_ref[pl.ds(i, DEVS, stride=share), :]
            last += pltpu.roll(part, i * classes, 1) if i else part
        every = pack_ref.shape[0] // DEVS
        pack_ref[pl.ds(at, DEVS, stride=every), :] = last
        fill_rows(pack_ref, at + 1)
        send_ref[...] = pack_ref[...].astype(bf16)


def assemble_kernel(own_ref, up_ref, side_ref, both_ref, out_ref, scr_ref):
    slots, rows, lon, _ = own_ref.shape
    hs, hr = slots // 2, rows // 2
    half = WIN_LON // 2
    win = slots * rows * WIN_LON
    for s in range(slots):
        for r in range(rows):
            if s < hs:
                plane = own_ref[hs + s, hr + r] if r < hr else side_ref[s, r - hr]
            else:
                plane = up_ref[s - hs, r] if r < hr else both_ref[s - hs, r - hr]
            plane = plane.astype(f32)
            plane = jnp.concatenate([plane[half:], plane[:half]], 0)
            for w in range(lon // WIN_LON):
                at = w * win + (s * rows + r) * WIN_LON
                scr_ref[at : at + WIN_LON] = plane[w * WIN_LON : (w + 1) * WIN_LON]
    out_ref[...] = scr_ref[...].astype(bf16)


def assemble(own, up, side, both):
    count = own.shape[0] * own.shape[1] * own.shape[2]
    return pl.pallas_call(
        assemble_kernel,
        out_shape=jax.ShapeDtypeStruct((count, own.shape[3]), bf16),
        scratch_shapes=[pltpu.VMEM((count, own.shape[3]), f32)],
        compiler_params=pltpu.CompilerParams(vmem_limit_bytes=40 * 2**20),
        name="assemble_windows",
    )(own, up, side, both)


def finish_kernel(
    weight_sum_ref, gott_ref, gotq_ref, wup_ref, wqkv_ref, gmlp_ref, gatt_ref, *outs
):
    loss_ref, gqkv_ref, gproj_ref, gup_ref, gdown_ref, gout_ref, ga_ref, gm_ref, grel_ref = outs
    got = jnp.sum(gott_ref[...].astype(f32), 0)
    at = 0
    for ref in (gup_ref, gproj_ref, gout_ref, gdown_ref):
        rows, cols = ref.shape
        for i in range(rows):
            for c in range(0, cols, 128):
                size = min(128, cols - c)
                ref[i : i + 1, c : c + size] = got[at : at + 1, :size]
                at += 1
    got = jnp.sum(gotq_ref[...].astype(f32), 0)
    at = 0
    rows, cols = gqkv_ref.shape
    for i in range(rows):
        for c in range(0, cols, 128):
            gqkv_ref[i : i + 1, c : c + 128] = got[at : at + 1]
            at += 1
    last = got[at : at + 1]
    classes = grel_ref.shape[1]
    for i in range(rows):
        grel_ref[i : i + 1, :] = last[:, i * classes : (i + 1) * classes]
    loss_ref[...] = (last[:, 126:127] + last[:, 127:128]) / weight_sum_ref[0]
    ga_ref[...] = jnp.sum(wqkv_ref[:rows] * gqkv_ref[...], 1, keepdims=True) / gatt_ref[...]
    gm_ref[...] = jnp.sum(wup_ref[:rows] * gup_ref[...], 1, keepdims=True) / gmlp_ref[...]


def finish(weight_sum, got_t, got_q, w_up, w_qkv, gain_mlp, gain_attn, shapes):
    smem = pl.BlockSpec(memory_space=pltpu.SMEM)
    vmem = pl.BlockSpec(memory_space=pltpu.VMEM)
    return pl.pallas_call(
        finish_kernel,
        in_specs=[smem] + [vmem] * 6,
        out_specs=[vmem] * len(shapes),
        out_shape=[jax.ShapeDtypeStruct(shape, f32) for shape in shapes],
        compiler_params=pltpu.CompilerParams(vmem_limit_bytes=40 * 2**20),
        name="finish_sums",
    )(weight_sum, got_t, got_q, w_up, w_qkv, gain_mlp, gain_attn)


def whole(shape):
    return pl.BlockSpec(shape, lambda i: (0,) * len(shape))


def lead(shape):
    return pl.BlockSpec(shape, lambda i: (i,) + (0,) * (len(shape) - 1))


def params_of():
    return pltpu.CompilerParams(
        vmem_limit_bytes=56 * 2**20, dimension_semantics=("arbitrary",)
    )


def attention_forward(x, relief_col, table, gain, w_qkv, wt, w_proj, bias_t):
    t, d = x.shape
    win = bias_t.shape[1]
    count = t // win
    sds = jax.ShapeDtypeStruct
    return pl.pallas_call(
        att_kernel,
        grid=(count // TOGETHER,),
        in_specs=[
            lead((TOGETHER * win, d)),
            lead((TOGETHER * win, 1)),
            whole(table.shape),
            whole((1, d)),
            whole((3 * d, d)),
            whole((d, d)),
            whole((d, d)),
            whole((d, d)),
            whole(bias_t.shape),
        ],
        out_specs=[
            lead((TOGETHER * win, d)),
            lead((TOGETHER, 2 * d, WIDE)),
            lead((TOGETHER * win, d)),
            lead((TOGETHER, HEADS, win, WIDE)),
            lead((TOGETHER, d, win)),
        ],
        out_shape=[
            sds((t, d), f32),
            sds((count, 2 * d, WIDE), bf16),
            sds((t, d), bf16),
            sds((count, HEADS, win, WIDE), bf16),
            sds((count, d, win), bf16),
        ],
        compiler_params=params_of(),
        name="attention_forward",
    )(
        x,
        relief_col,
        table,
        gain[None],
        wt,
        w_qkv[:, 2 * d :],
        w_qkv[:, d : 2 * d],
        w_proj,
        bias_t,
    )


def cost(flops, moved, trans):
    return pl.CostEstimate(flops=flops, bytes_accessed=moved, transcendentals=trans)


def tail_both(me, scale, stream2, targ, relief_col, lev, base, att, gain, w_up, w_down, w_out, group):
    t, d = stream2.shape
    win = att.shape[-1]
    m = group * win
    ff, out = w_up.shape[1], w_out.shape[1]
    pieces = (d * ff + d * d + d * 256 + d * ff) // (DEVS * 128)
    pieces += -pieces % 8
    sds = jax.ShapeDtypeStruct
    return pl.pallas_call(
        functools.partial(tail_kernel, block_f=256),
        grid=(t // m,),
        in_specs=[
            pl.BlockSpec(memory_space=pltpu.SMEM),
            pl.BlockSpec(memory_space=pltpu.SMEM),
            lead((m, d)),
            lead((m, out)),
            lead((m, 1)),
            pl.BlockSpec(memory_space=pltpu.SMEM),
            whole(base.shape),
            lead((group, d, win)),
            whole((1, d)),
            whole((d, ff)),
            whole((ff, d)),
            whole((d, out)),
        ],
        out_specs=[
            whole((1, out)),
            lead((m, d)),
            whole((DEVS * pieces, 128)),
            whole((8, ff)),
        ],
        out_shape=[
            sds((1, out), f32),
            sds((t, d), f32),
            sds((DEVS * pieces, 128), bf16),
            sds((8, ff), f32),
        ],
        scratch_shapes=[
            pltpu.VMEM((win, out), jnp.int32),
            pltpu.VMEM((win, out), f32),
            pltpu.VMEM((d, d), f32),
            pltpu.VMEM((d, ff), f32),
            pltpu.VMEM((d, ff), f32),
            pltpu.VMEM((d, 256), f32),
            pltpu.VMEM((ff // 128, d, 128), f32),
            pltpu.VMEM((d // 128, ff, 128), f32),
            pltpu.VMEM((DEVS * pieces, 128), f32),
        ],
        compiler_params=params_of(),
        name="tail_both",
    )(me, scale, stream2, targ, relief_col, lev, base, att, gain[None], w_up, w_down, w_out)


def attention_back(me, num, x, relief_col, table, gain, w_qkv, w_proj, qkt, v_tok, probs, att, gs2):
    t, d = x.shape
    count, win = att.shape[0], att.shape[2]
    sds = jax.ShapeDtypeStruct
    return pl.pallas_call(
        back_kernel,
        grid=(count // TOGETHER,),
        in_specs=[
            pl.BlockSpec(memory_space=pltpu.SMEM),
            lead((TOGETHER * win, d)),
            lead((TOGETHER * win, 1)),
            whole(table.shape),
            whole((1, d)),
            whole((d, 3 * d)),
            whole((d, d)),
            lead((TOGETHER, 2 * d, WIDE)),
            lead((TOGETHER * win, d)),
            lead((TOGETHER, HEADS, win, WIDE)),
            lead((TOGETHER, d, win)),
            lead((TOGETHER * win, d)),
            whole(num.shape),
        ],
        out_specs=[
            whole((HEADS, win, WIDE)),
            whole((DEVS * 32, 128)),
            whole((8, 3 * d)),
        ],
        out_shape=[
            sds((HEADS, win, WIDE), f32),
            sds((DEVS * 32, 128), bf16),
            sds((8, 3 * d), f32),
        ],
        scratch_shapes=[
            pltpu.VMEM((3 * d, d), f32),
            pltpu.VMEM((3 * d // 128, d, 128), f32),
            pltpu.VMEM((table.shape[0], d), f32),
            pltpu.VMEM((d, 128), f32),
            pltpu.VMEM((DEVS * 32, 128), f32),
        ],
        compiler_params=params_of(),
        cost_estimate=cost(10 * 2**30, 20 * 2**20, 0),
        name="attention_back",
    )(me, x, relief_col, table, gain[None], w_qkv, w_proj, qkt, v_tok, probs, att, gs2, num)


def lat_weights(row_ids, lat_rows):
    fine_rows = 4 * row_ids[:, None] + jnp.arange(4, dtype=jnp.int32)[None, :]
    angle_rad = (90.0 - 180.0 * (fine_rows.astype(f32) + 0.5) / (4.0 * lat_rows)) * (
        math.pi / 180.0
    )
    return jnp.cos(angle_rad)


def weight_total(relief, var_weight, level_count):
    lat_rows = relief.shape[0]
    lat_weight = jnp.sum(lat_weights(jnp.arange(lat_rows, dtype=jnp.int32), lat_rows), 1)
    live_levels = (2 * level_count - relief).astype(f32)
    return jnp.sum(var_weight) * 4.0 * jnp.sum(lat_weight[:, None] * live_levels)


def window_mask(last_level, last_band, slots_n, rows_n, win_lon):
    slot_label = jnp.where(last_level & (jnp.arange(slots_n) >= slots_n // 2), 2, 0)
    row_label = jnp.where(last_band & (jnp.arange(rows_n) >= rows_n // 2), 1, 0)
    labels = (
        slot_label[:, None, None] + row_label[None, :, None] + jnp.zeros((1, 1, win_lon), jnp.int32)
    )
    labels = labels.reshape(-1)
    return labels[:, None] == labels[None, :]


def windows(field_in):
    slots_n, rows_n, lon_n, chans = field_in.shape
    count_w = lon_n // WIN_LON
    parted = field_in.reshape(slots_n, rows_n, count_w, WIN_LON, chans).transpose(2, 0, 1, 3, 4)
    return parted.reshape(count_w * slots_n * rows_n * WIN_LON, chans)


def from_next(value, axes):
    sizes = [lax.axis_size(a) for a in ("lvl", "lat")]
    move = [1 if a in axes else 0 for a in ("lvl", "lat")]
    pairs = []
    for i in range(sizes[0]):
        for j in range(sizes[1]):
            src = (i + move[0]) % sizes[0] * sizes[1] + (j + move[1]) % sizes[1]
            pairs.append((src, i * sizes[1] + j))
    return lax.ppermute(value, ("lvl", "lat"), pairs)


def halo_of(field_in):
    slots_n, rows_n = field_in.shape[:2]
    hs, hr = slots_n // 2, rows_n // 2
    up = from_next(field_in[:hs, hr:], ("lvl",))
    side = from_next(field_in[hs:, :hr], ("lat",))
    both = from_next(field_in[:hs, :hr], ("lvl", "lat"))
    return up, side, both


def local_inputs(tokens_shape, relief, earth_bias, var_weight):
    slots_dev, rows_dev, lon_cells, _ = tokens_shape
    lvl_count, lat_count = lax.axis_size("lvl"), lax.axis_size("lat")
    lvl_id, lat_id = lax.axis_index("lvl"), lax.axis_index("lat")
    level_total, lat_rows = slots_dev * lvl_count, rows_dev * lat_count
    allowed = window_mask(
        lvl_id == lvl_count - 1, lat_id == lat_count - 1, slots_dev, rows_dev, WIN_LON
    )
    level_ids = (
        lvl_id * slots_dev + jnp.arange(slots_dev, dtype=jnp.int32) + slots_dev // 2
    ) % level_total
    row_ids = (
        lat_id * rows_dev + jnp.arange(rows_dev, dtype=jnp.int32) + rows_dev // 2
    ) % lat_rows
    relief_blk = jnp.roll(jnp.take(relief, row_ids, axis=0), -(WIN_LON // 2), 1)
    relief_col = windows(
        jnp.broadcast_to(relief_blk[None, :, :, None], (slots_dev, rows_dev, lon_cells, 1))
    )
    vars_n = var_weight.shape[0]
    base = jnp.broadcast_to(
        var_weight[None, :, None, None, None]
        * lat_weights(row_ids, lat_rows)[:, None, None, :, None],
        (rows_dev, vars_n, 2, 4, 4),
    ).reshape(rows_dev, vars_n * 32)
    bias_t = jnp.where(allowed, earth_bias.transpose(0, 2, 1) * log2_e, masked_score)
    bias_t = jnp.pad(bias_t, ((0, 0), (0, 0), (0, WIDE - bias_t.shape[2])))
    return relief_col, level_ids, base, bias_t


def body(
    tokens,
    targets,
    relief,
    earth_bias,
    relief_table,
    gain_attn,
    gain_mlp,
    w_qkv,
    w_proj,
    w_up,
    w_down,
    w_out,
    var_weight,
):
    axes = ("lvl", "lat")
    devs = lax.axis_size("lvl") * lax.axis_size("lat")
    level_total = tokens.shape[0] * lax.axis_size("lvl")
    weight_sum = weight_total(relief, var_weight, level_total)
    token_halo = halo_of(tokens)
    targ_halo = halo_of(targets)
    relief_col, lev, base, bias_t = local_inputs(tokens.shape, relief, earth_bias[0, 0], var_weight)
    scale = (loss_scale / weight_sum).reshape(1)
    wt = w_qkv.T
    tokens, relief_col, bias_t, base, scale, wt = lax.optimization_barrier(
        (tokens, relief_col, bias_t, base, scale, wt)
    )
    x = assemble(tokens, *token_halo)
    stream2, qkt, v_tok, probs, att = attention_forward(
        x, relief_col, relief_table, gain_attn, w_qkv, wt, w_proj, bias_t
    )
    stream2, targets = lax.optimization_barrier((stream2, targets))
    targ = assemble(targets, *targ_halo)
    me = lax.axis_index(axes)
    num, gs2, send_t, up_rows = tail_both(
        me.reshape(1), scale, stream2, targ, relief_col, lev, base, att, gain_mlp, w_up, w_down, w_out, GROUP
    )
    got_t = lax.all_to_all(send_t.reshape(devs, -1, 128), axes, 0, 0, tiled=True)
    gbias_t, send_q, qkv_rows = attention_back(
        me.reshape(1), num, x, relief_col, relief_table, gain_attn, w_qkv, w_proj, qkt, v_tok, probs, att, gs2
    )
    send_q, got_t = lax.optimization_barrier((send_q.reshape(devs, -1, 128), got_t))
    got_q = lax.all_to_all(send_q, axes, 0, 0, tiled=True)
    d = tokens.shape[-1]
    share = d // devs

    def mine(array):
        return lax.dynamic_slice_in_dim(array, me * share, share, 0)[:, None]

    shapes = (
        (1, 1),
        (share, w_qkv.shape[1]),
        (share, d),
        (share, w_up.shape[1]),
        (w_down.shape[0] // devs, d),
        (share, w_out.shape[1]),
        (share, 1),
        (share, 1),
        (share, relief_table.shape[0]),
    )
    sums = finish(
        weight_sum.reshape(1), got_t, got_q, up_rows, qkv_rows, mine(gain_mlp), mine(gain_attn), shapes
    )
    return (
        sums[0][0, 0],
        *sums[1:6],
        sums[6][:, 0],
        sums[7][:, 0],
        sums[8],
        gbias_t[..., : gbias_t.shape[1]].transpose(0, 2, 1)[None, None],
    )


def solution(mesh):
    field = P("lvl", "lat", None, None)
    bias = P("lvl", "lat", None, None, None)
    rows = P(("lvl", "lat"), None)
    vec = P(("lvl", "lat"))
    return jax.shard_map(
        body,
        mesh=mesh,
        in_specs=(field, field, P(), bias) + (P(),) * 9,
        out_specs=(P(), rows, rows, rows, rows, rows, vec, vec, rows, bias),
        check_vma=False,
    )
```

```python
import functools
import math

import jax
import jax.numpy as jnp
from jax import lax
from jax.experimental import pallas as pl
from jax.experimental.pallas import tpu as pltpu
from jax.sharding import PartitionSpec as P

WIN_LON = 12
HEADS = 12
GROUP = 6
DEVS = 128
WIDE = 256
SLOTS = 2
TOGETHER = 3
norm_eps = 1e-05
loss_scale = 32768.0
smooth_sq = 0.01
masked_score = -1e30
log2_e = math.log2(math.e)
f32 = jnp.float32
bf16 = jnp.bfloat16


def nn(left, right):
    return lax.dot_general(left, right, (((1,), (0,)), ((), ())), preferred_element_type=f32)


def nt(left, right):
    return lax.dot_general(left, right, (((1,), (1,)), ((), ())), preferred_element_type=f32)


def tn(left, right):
    return lax.dot_general(left, right, (((0,), (0,)), ((), ())), preferred_element_type=f32)


def normalize(values):
    width = values.shape[-1]
    centre = jnp.sum(values, -1, keepdims=True) * (1.0 / width)
    moved = values - centre
    spread = jnp.sum(moved * moved, -1, keepdims=True) * (1.0 / width)
    rstd = lax.rsqrt(spread + norm_eps)
    return moved * rstd, rstd


def norm_back(grad_hat, hat, rstd):
    width = hat.shape[-1]
    mean_g = jnp.sum(grad_hat, -1, keepdims=True) * (1.0 / width)
    mean_gh = jnp.sum(grad_hat * hat, -1, keepdims=True) * (1.0 / width)
    return rstd * (grad_hat - mean_g - hat * mean_gh)


def gelu_both(x):
    dens = jnp.exp2(x * x * (-0.5 * log2_e))
    den = 1.0 + jnp.abs(x) * (0.3275911 / math.sqrt(2.0))
    t = pl.reciprocal(den, approx=True)
    t = t * (2.0 - den * t)
    poly = 0.5 * 1.061405429
    for coef in (-1.453152027, 1.421413741, -0.284496736, 0.254829592):
        poly = poly * t + 0.5 * coef
    side = poly * t * dens
    cdf = jnp.where(x >= 0.0, 1.0 - side, side)
    return x * cdf, cdf + x * dens * (1.0 / math.sqrt(2.0 * math.pi))


def own_rows(me, weight_ref):
    rows = weight_ref.shape[0]
    share = rows // DEVS
    ids = lax.broadcasted_iota(jnp.int32, (8, rows), 0) + me * share
    picks = (lax.broadcasted_iota(jnp.int32, (8, rows), 1) == ids).astype(f32).astype(bf16)
    return nn(picks, weight_ref[...])


def pack_rows(send_ref, at, piece_ref):
    pieces, rows, _ = piece_ref.shape
    share = rows // DEVS
    every = send_ref.shape[0] // DEVS
    for i in range(share):
        for c in range(pieces):
            block = piece_ref[c, pl.ds(i, DEVS, stride=share), :]
            send_ref[pl.ds(at, DEVS, stride=every), :] = block
            at += 1
    return at


def fill_rows(send_ref, at):
    every = send_ref.shape[0] // DEVS
    for j in range(at, every):
        send_ref[pl.ds(j, DEVS, stride=every), :] = jnp.zeros((DEVS, 128), f32)


def cut_pieces(piece_ref, grad_ref):
    for c in range(piece_ref.shape[0]):
        piece_ref[c] = grad_ref[:, c * 128 : (c + 1) * 128]


def turn_pieces(piece_ref, grad_t_ref):
    for c in range(piece_ref.shape[0]):
        piece_ref[c] = grad_t_ref[c * 128 : (c + 1) * 128].T


def one_hot_of(relief_col, classes):
    ids = lax.broadcasted_iota(jnp.int32, (relief_col.shape[0], classes), 1)
    return (relief_col == ids).astype(f32).astype(bf16)


def alone(part, place, count):
    parts = [jnp.zeros_like(part)] * count
    parts[place] = part
    return jnp.concatenate(parts, 0)


def stream_of(x_ref, relief_ref, table_ref):
    one_hot = one_hot_of(relief_ref[...], table_ref.shape[0])
    return x_ref[...].astype(f32) + nn(one_hot, table_ref[...]), one_hot


def att_kernel(
    x_ref,
    relief_ref,
    table_ref,
    gain_ref,
    wt_ref,
    wqkv_ref,
    wproj_ref,
    bias_ref,
    stream2_ref,
    qt_ref,
    prob_ref,
    att_ref,
):
    stream, _ = stream_of(x_ref, relief_ref, table_ref)
    hat, _ = normalize(stream)
    normed = (hat * gain_ref[...]).astype(bf16)
    d = normed.shape[1]
    count, win = att_ref.shape[0], att_ref.shape[2]
    k_tok = nn(normed, wqkv_ref[:, d : 2 * d]).astype(bf16)
    e = d // HEADS
    per = 128 // e
    qvts = []
    for u in range(count):
        rows = slice(u * win, (u + 1) * win)
        filled = jnp.concatenate([normed[rows], jnp.zeros((WIDE - win, d), bf16)], 0)
        qvts.append((nt(wt_ref[:d], filled), nt(wt_ref[2 * d :], filled)))
    mixed = []
    for u in range(count):
        rows = slice(u * win, (u + 1) * win)
        qt = (qvts[u][0] * (log2_e * e**-0.5)).astype(bf16)
        vt = qvts[u][1].astype(bf16)
        att = []
        for g in range(d // 128):
            k_four = k_tok[rows, g * 128 : (g + 1) * 128]
            heads = range(g * per, (g + 1) * per)
            scores = [nn(k_four, alone(qt[h * e : (h + 1) * e], h % per, per)) for h in heads]
            probs = []
            for h, score in zip(heads, scores):
                score = score + bias_ref[h]
                top = jnp.max(score, 0, keepdims=True)
                prob = jnp.exp2(score - top)
                prob = (prob * (1.0 / jnp.sum(prob, 0, keepdims=True))).astype(bf16)
                probs.append(prob)
                prob_ref[u, h] = prob
            att += [nn(vt[h * e : (h + 1) * e, :win], prob) for h, prob in zip(heads, probs)]
        att = jnp.concatenate(att, 0).astype(bf16)[:, :win]
        att_ref[u] = att
        qt_ref[u] = qt
        mixed.append(tn(att, wproj_ref[...]).astype(bf16))
    stream2_ref[...] = stream + jnp.concatenate(mixed, 0).astype(f32)


def tail_kernel(
    me_ref,
    scale_ref,
    stream2_ref,
    targ_ref,
    relief_ref,
    levels_ref,
    base_ref,
    att_ref,
    gain_ref,
    wup_ref,
    wdown_ref,
    wout_ref,
    num_ref,
    gs2_ref,
    send_ref,
    wsel_ref,
    lev_ref,
    wide_ref,
    gproj_ref,
    gup_ref,
    gdown_ref,
    gout_ref,
    piece_ref,
    gdown_t_ref,
    pack_ref,
    *,
    block_f,
):
    step = pl.program_id(0)
    me = me_ref[0]

    @pl.when(step == 0)
    def _():
        slots, rows = levels_ref.shape[0], base_ref.shape[0]
        shape = lev_ref.shape
        token = lax.broadcasted_iota(jnp.int32, shape, 0)
        upper = (lax.broadcasted_iota(jnp.int32, shape, 1) // 16) % 2
        line = token // WIN_LON
        lev = jnp.full(shape, 2 * levels_ref[0], jnp.int32)
        for s in range(1, slots):
            lev = jnp.where(line >= s * rows, 2 * levels_ref[s], lev)
        lev_ref[...] = lev + upper
        wide = jnp.zeros(shape, f32)
        for r in range(rows):
            wide = jnp.where(line % rows == r, base_ref[r : r + 1], wide)
        wide_ref[...] = wide
        num_ref[...] = jnp.zeros_like(num_ref)
        gproj_ref[...] = jnp.zeros_like(gproj_ref)
        gup_ref[...] = jnp.zeros_like(gup_ref)
        gdown_ref[...] = jnp.zeros_like(gdown_ref)
        gout_ref[...] = jnp.zeros_like(gout_ref)

    stream2 = stream2_ref[...]
    wins, win = att_ref.shape[0], att_ref.shape[2]
    ff = wup_ref.shape[1]
    hat, rstd = normalize(stream2)
    gain = gain_ref[...]
    normed2 = (hat * gain).astype(bf16)
    hids, slopes, gpres = [], [], []
    for n in range(0, ff, block_f):
        cols = slice(n, n + block_f)
        hidden, slope = gelu_both(nn(normed2, wup_ref[:, cols]))
        hids.append(hidden.astype(bf16))
        slopes.append(slope.astype(bf16))
    field = (stream2 + nn(jnp.concatenate(hids, 1), wdown_ref[...])).astype(bf16)
    pred = nt(field, wout_ref[...])
    relief = relief_ref[...]
    lev = jnp.concatenate([lev_ref[...]] * wins, 0)
    base = jnp.concatenate([wide_ref[...]] * wins, 0)
    cell_w = jnp.where(lev >= relief, base, 0.0)
    differ = pred - targ_ref[...].astype(f32)
    square = differ * differ + smooth_sq
    inv_err = lax.rsqrt(square)
    num_ref[...] += jnp.sum(cell_w * (square * inv_err), 0, keepdims=True)
    gpred = (scale_ref[0] * cell_w * differ * inv_err).astype(bf16)
    out = gpred.shape[1]
    gout_ref[:, :out] += nn(field.T, gpred)
    gfield = nn(gpred, wout_ref[...])
    gfb = gfield.astype(bf16)
    gfbt = gfb.T
    normed2t = normed2.T
    for n in range(0, ff, block_f):
        cols = slice(n, n + block_f)
        ghid = nt(gfb, wdown_ref[cols, :])
        gpres.append((slopes[n // block_f].astype(f32) * ghid).astype(bf16))
    for n in range(0, ff, block_f):
        cols = slice(n, n + block_f)
        gdown_ref[:, cols] += nn(gfbt, hids[n // block_f])
        gup_ref[:, cols] += nn(normed2t, gpres[n // block_f])
    gnorm2 = nt(jnp.concatenate(gpres, 1), wup_ref[...])
    gs2 = gfield + norm_back(gnorm2 * gain, hat, rstd)
    gs2_ref[...] = gs2
    gmix = gs2.astype(bf16)
    for w in range(wins):
        gproj_ref[...] += nn(att_ref[w], gmix[w * win : (w + 1) * win])

    @pl.when(step == pl.num_programs(0) - 1)
    def _():
        wsel_ref[...] = own_rows(me, wup_ref)
        at = 0
        for ref in (gup_ref, gproj_ref, gout_ref):
            pieces = piece_ref.at[: ref.shape[1] // 128]
            cut_pieces(pieces, ref)
            at = pack_rows(pack_ref, at, pieces)
        turn_pieces(gdown_t_ref, gdown_ref)
        at = pack_rows(pack_ref, at, gdown_t_ref)
        fill_rows(pack_ref, at)
        send_ref[...] = pack_ref[...].astype(bf16)


def back_kernel(
    me_ref,
    x_ref,
    relief_ref,
    table_ref,
    gain_ref,
    wqkv_ref,
    wt_ref,
    wproj_ref,
    qt_ref,
    prob_ref,
    att_ref,
    gs2_ref,
    num_ref,
    gbias_ref,
    send_ref,
    wsel_ref,
    gqkv_ref,
    gqkv_t_ref,
    grel_ref,
    grel_t_ref,
    pack_ref,
):
    step = pl.program_id(0)

    @pl.when(step == 0)
    def _():
        gbias_ref[...] = jnp.zeros_like(gbias_ref)
        gqkv_ref[...] = jnp.zeros_like(gqkv_ref)
        grel_ref[...] = jnp.zeros_like(grel_ref)

    stream, one_hot = stream_of(x_ref, relief_ref, table_ref)
    hat, rstd = normalize(stream)
    gain = gain_ref[...]
    normed = (hat * gain).astype(bf16)
    d = normed.shape[1]
    count, win = att_ref.shape[0], att_ref.shape[2]
    e = d // HEADS
    per = 128 // e
    gs2 = gs2_ref[...]
    gmix = gs2.astype(bf16)
    pad = jnp.zeros((WIDE - win, d), bf16)
    gatts = []
    for u in range(count):
        filled = jnp.concatenate([gmix[u * win : (u + 1) * win], pad], 0)
        gatts.append(nt(wproj_ref[...], filled).astype(bf16))
    v_tok = nn(normed, wqkv_ref[:, 2 * d :]).astype(bf16)
    kts = []
    for u in range(count):
        filled = jnp.concatenate([normed[u * win : (u + 1) * win], pad], 0)
        kts.append(nt(wt_ref[d : 2 * d], filled).astype(bf16)[:, :win])
    gshift = []
    for u in range(count):
        wrows = slice(u * win, (u + 1) * win)
        gatt_b = gatts[u]
        prod = gatt_b[:, :win].astype(f32) * att_ref[u].astype(f32)
        prod = jnp.concatenate([prod, jnp.zeros((d, WIDE - win), f32)], 1)
        qt, kt = qt_ref[u], kts[u]
        gqs, gks, gvs = [], [], []
        for g in range(d // 128):
            v_four = v_tok[wrows, g * 128 : (g + 1) * 128]
            heads = range(g * per, (g + 1) * per)
            gprobs = [nn(v_four, alone(gatt_b[h * e : (h + 1) * e], h % per, per)) for h in heads]
            gscores = []
            probs = [prob_ref[u, h] for h in heads]
            for h, gprob, prob in zip(heads, gprobs, probs):
                delta = jnp.sum(prod[h * e : (h + 1) * e], 0, keepdims=True)
                gscore = prob.astype(f32) * (gprob - delta)
                gbias_ref[h] += gscore
                gscores.append(gscore.astype(bf16))
            for h, gsb, prob in zip(heads, gscores, probs):
                rows = slice(h * e, (h + 1) * e)
                gqs.append((nn(kt[rows], gsb) * e**-0.5).astype(bf16)[:, :win])
                gks.append((nt(qt[rows], gsb) * (1.0 / log2_e)).astype(bf16))
                gvs.append(nt(gatt_b[rows], prob).astype(bf16))
        gheads = jnp.concatenate(gqs + gks + gvs, 0)
        gqkv_ref[...] += nn(gheads, normed[wrows])
        gshift.append(nn(wqkv_ref[...], gheads).astype(bf16).T.astype(f32))
    gshift = jnp.concatenate(gshift, 0)
    gstream = gs2 + norm_back(gshift * gain, hat, rstd)
    grel_ref[...] += tn(one_hot, gstream.astype(bf16))

    @pl.when(step == pl.num_programs(0) - 1)
    def _():
        wsel_ref[...] = own_rows(me_ref[0], wqkv_ref)
        turn_pieces(gqkv_t_ref, gqkv_ref)
        at = pack_rows(pack_ref, 0, gqkv_t_ref)
        classes = grel_ref.shape[0]
        wide = jnp.concatenate([grel_ref[...], jnp.zeros((128 - classes, d), f32)], 0)
        grel_t_ref[...] = wide.T
        share = d // DEVS
        num = jnp.sum(num_ref[...], 1, keepdims=True)
        high = num.astype(bf16).astype(f32)
        lane = lax.broadcasted_iota(jnp.int32, (DEVS, 128), 1)
        last = jnp.where(lane == 126, high, jnp.where(lane == 127, num - high, 0.0))
        for i in range(share):
            part = grel_t_ref[pl.ds(i, DEVS, stride=share), :]
            last += pltpu.roll(part, i * classes, 1) if i else part
        every = pack_ref.shape[0] // DEVS
        pack_ref[pl.ds(at, DEVS, stride=every), :] = last
        fill_rows(pack_ref, at + 1)
        send_ref[...] = pack_ref[...].astype(bf16)


def assemble_kernel(own_ref, up_ref, side_ref, both_ref, out_ref, scr_ref):
    slots, rows, lon, _ = own_ref.shape
    hs, hr = slots // 2, rows // 2
    half = WIN_LON // 2
    win = slots * rows * WIN_LON
    for s in range(slots):
        for r in range(rows):
            if s < hs:
                plane = own_ref[hs + s, hr + r] if r < hr else side_ref[s, r - hr]
            else:
                plane = up_ref[s - hs, r] if r < hr else both_ref[s - hs, r - hr]
            plane = plane.astype(f32)
            plane = jnp.concatenate([plane[half:], plane[:half]], 0)
            for w in range(lon // WIN_LON):
                at = w * win + (s * rows + r) * WIN_LON
                scr_ref[at : at + WIN_LON] = plane[w * WIN_LON : (w + 1) * WIN_LON]
    out_ref[...] = scr_ref[...].astype(bf16)


def assemble(own, up, side, both):
    count = own.shape[0] * own.shape[1] * own.shape[2]
    return pl.pallas_call(
        assemble_kernel,
        out_shape=jax.ShapeDtypeStruct((count, own.shape[3]), bf16),
        scratch_shapes=[pltpu.VMEM((count, own.shape[3]), f32)],
        compiler_params=pltpu.CompilerParams(vmem_limit_bytes=40 * 2**20),
        name="assemble_windows",
    )(own, up, side, both)


def finish_kernel(
    weight_sum_ref, gott_ref, gotq_ref, wup_ref, wqkv_ref, gmlp_ref, gatt_ref, *outs
):
    loss_ref, gqkv_ref, gproj_ref, gup_ref, gdown_ref, gout_ref, ga_ref, gm_ref, grel_ref = outs
    got = jnp.sum(gott_ref[...].astype(f32), 0)
    at = 0
    for ref in (gup_ref, gproj_ref, gout_ref, gdown_ref):
        rows, cols = ref.shape
        for i in range(rows):
            for c in range(0, cols, 128):
                size = min(128, cols - c)
                ref[i : i + 1, c : c + size] = got[at : at + 1, :size]
                at += 1
    got = jnp.sum(gotq_ref[...].astype(f32), 0)
    at = 0
    rows, cols = gqkv_ref.shape
    for i in range(rows):
        for c in range(0, cols, 128):
            gqkv_ref[i : i + 1, c : c + 128] = got[at : at + 1]
            at += 1
    last = got[at : at + 1]
    classes = grel_ref.shape[1]
    for i in range(rows):
        grel_ref[i : i + 1, :] = last[:, i * classes : (i + 1) * classes]
    loss_ref[...] = (last[:, 126:127] + last[:, 127:128]) / weight_sum_ref[0]
    diag = lax.broadcasted_iota(jnp.int32, (rows, rows), 0) == lax.broadcasted_iota(
        jnp.int32, (rows, rows), 1
    )
    ga = jnp.sum(wqkv_ref[:rows] * gqkv_ref[...], 1, keepdims=True)
    ga_ref[...] = jnp.sum(jnp.where(diag, ga, 0.0), 0, keepdims=True) / gatt_ref[...]
    gm = jnp.sum(wup_ref[:rows] * gup_ref[...], 1, keepdims=True)
    gm_ref[...] = jnp.sum(jnp.where(diag, gm, 0.0), 0, keepdims=True) / gmlp_ref[...]


def finish(weight_sum, got_t, got_q, w_up, w_qkv, gain_mlp, gain_attn, shapes):
    smem = pl.BlockSpec(memory_space=pltpu.SMEM)
    vmem = pl.BlockSpec(memory_space=pltpu.VMEM)
    return pl.pallas_call(
        finish_kernel,
        in_specs=[smem] + [vmem] * 6,
        out_specs=[vmem] * len(shapes),
        out_shape=[jax.ShapeDtypeStruct(shape, f32) for shape in shapes],
        compiler_params=pltpu.CompilerParams(vmem_limit_bytes=40 * 2**20),
        name="finish_sums",
    )(weight_sum, got_t, got_q, w_up, w_qkv, gain_mlp, gain_attn)


def whole(shape):
    return pl.BlockSpec(shape, lambda i: (0,) * len(shape))


def lead(shape):
    return pl.BlockSpec(shape, lambda i: (i,) + (0,) * (len(shape) - 1))


def params_of():
    return pltpu.CompilerParams(
        vmem_limit_bytes=56 * 2**20, dimension_semantics=("arbitrary",)
    )


def attention_forward(x, relief_col, table, gain, w_qkv, wt, w_proj, bias_t):
    t, d = x.shape
    win = bias_t.shape[1]
    count = t // win
    sds = jax.ShapeDtypeStruct
    return pl.pallas_call(
        att_kernel,
        grid=(count // TOGETHER,),
        in_specs=[
            lead((TOGETHER * win, d)),
            lead((TOGETHER * win, 1)),
            whole(table.shape),
            whole((1, d)),
            whole((3 * d, d)),
            whole((d, 3 * d)),
            whole((d, d)),
            whole(bias_t.shape),
        ],
        out_specs=[
            lead((TOGETHER * win, d)),
            lead((TOGETHER, d, WIDE)),
            lead((TOGETHER, HEADS, win, WIDE)),
            lead((TOGETHER, d, win)),
        ],
        out_shape=[
            sds((t, d), f32),
            sds((count, d, WIDE), bf16),
            sds((count, HEADS, win, WIDE), bf16),
            sds((count, d, win), bf16),
        ],
        compiler_params=params_of(),
        name="attention_forward",
    )(
        x,
        relief_col,
        table,
        gain[None],
        wt,
        w_qkv,
        w_proj,
        bias_t,
    )


def cost(flops, moved, trans):
    return pl.CostEstimate(flops=flops, bytes_accessed=moved, transcendentals=trans)


def tail_both(me, scale, stream2, targ, relief_col, lev, base, att, gain, w_up, w_down, w_out, group):
    t, d = stream2.shape
    win = att.shape[-1]
    m = group * win
    ff, out = w_up.shape[1], w_out.shape[1]
    pieces = (d * ff + d * d + d * 256 + d * ff) // (DEVS * 128)
    pieces += -pieces % 8
    sds = jax.ShapeDtypeStruct
    return pl.pallas_call(
        functools.partial(tail_kernel, block_f=256),
        grid=(t // m,),
        in_specs=[
            pl.BlockSpec(memory_space=pltpu.SMEM),
            pl.BlockSpec(memory_space=pltpu.SMEM),
            lead((m, d)),
            lead((m, out)),
            lead((m, 1)),
            pl.BlockSpec(memory_space=pltpu.SMEM),
            whole(base.shape),
            lead((group, d, win)),
            whole((1, d)),
            whole((d, ff)),
            whole((ff, d)),
            whole((out, d)),
        ],
        out_specs=[
            whole((1, out)),
            lead((m, d)),
            whole((DEVS * pieces, 128)),
            whole((8, ff)),
        ],
        out_shape=[
            sds((1, out), f32),
            sds((t, d), f32),
            sds((DEVS * pieces, 128), bf16),
            sds((8, ff), f32),
        ],
        scratch_shapes=[
            pltpu.VMEM((win, out), jnp.int32),
            pltpu.VMEM((win, out), f32),
            pltpu.VMEM((d, d), f32),
            pltpu.VMEM((d, ff), f32),
            pltpu.VMEM((d, ff), f32),
            pltpu.VMEM((d, 256), f32),
            pltpu.VMEM((ff // 128, d, 128), f32),
            pltpu.VMEM((d // 128, ff, 128), f32),
            pltpu.VMEM((DEVS * pieces, 128), f32),
        ],
        compiler_params=params_of(),
        name="tail_both",
    )(me, scale, stream2, targ, relief_col, lev, base, att, gain[None], w_up, w_down, w_out.T)


def attention_back(me, num, x, relief_col, table, gain, w_qkv, wt, w_proj, qt, probs, att, gs2):
    t, d = x.shape
    count, win = att.shape[0], att.shape[2]
    sds = jax.ShapeDtypeStruct
    return pl.pallas_call(
        back_kernel,
        grid=(count // TOGETHER,),
        in_specs=[
            pl.BlockSpec(memory_space=pltpu.SMEM),
            lead((TOGETHER * win, d)),
            lead((TOGETHER * win, 1)),
            whole(table.shape),
            whole((1, d)),
            whole((d, 3 * d)),
            whole((3 * d, d)),
            whole((d, d)),
            lead((TOGETHER, d, WIDE)),
            lead((TOGETHER, HEADS, win, WIDE)),
            lead((TOGETHER, d, win)),
            lead((TOGETHER * win, d)),
            whole(num.shape),
        ],
        out_specs=[
            whole((HEADS, win, WIDE)),
            whole((DEVS * 32, 128)),
            whole((8, 3 * d)),
        ],
        out_shape=[
            sds((HEADS, win, WIDE), f32),
            sds((DEVS * 32, 128), bf16),
            sds((8, 3 * d), f32),
        ],
        scratch_shapes=[
            pltpu.VMEM((3 * d, d), f32),
            pltpu.VMEM((3 * d // 128, d, 128), f32),
            pltpu.VMEM((table.shape[0], d), f32),
            pltpu.VMEM((d, 128), f32),
            pltpu.VMEM((DEVS * 32, 128), f32),
        ],
        compiler_params=params_of(),
        cost_estimate=cost(10 * 2**30, 20 * 2**20, 0),
        name="attention_back",
    )(me, x, relief_col, table, gain[None], w_qkv, wt, w_proj, qt, probs, att, gs2, num)


def lat_weights(row_ids, lat_rows):
    fine_rows = 4 * row_ids[:, None] + jnp.arange(4, dtype=jnp.int32)[None, :]
    angle_rad = (90.0 - 180.0 * (fine_rows.astype(f32) + 0.5) / (4.0 * lat_rows)) * (
        math.pi / 180.0
    )
    return jnp.cos(angle_rad)


def weight_total(relief, var_weight, level_count):
    lat_rows = relief.shape[0]
    lat_weight = jnp.sum(lat_weights(jnp.arange(lat_rows, dtype=jnp.int32), lat_rows), 1)
    live_levels = (2 * level_count - relief).astype(f32)
    return jnp.sum(var_weight) * 4.0 * jnp.sum(lat_weight[:, None] * live_levels)


def from_next(value, axes):
    sizes = [lax.axis_size(a) for a in ("lvl", "lat")]
    move = [1 if a in axes else 0 for a in ("lvl", "lat")]
    pairs = []
    for i in range(sizes[0]):
        for j in range(sizes[1]):
            src = (i + move[0]) % sizes[0] * sizes[1] + (j + move[1]) % sizes[1]
            pairs.append((src, i * sizes[1] + j))
    return lax.ppermute(value, ("lvl", "lat"), pairs)


def halo_of(field_in):
    slots_n, rows_n = field_in.shape[:2]
    hs, hr = slots_n // 2, rows_n // 2
    up = from_next(field_in[:hs, hr:], ("lvl",))
    side = from_next(field_in[hs:, :hr], ("lat",))
    both = from_next(field_in[:hs, :hr], ("lvl", "lat"))
    return up, side, both


def summed_by_chips(send):
    lvls, lats = lax.axis_size("lvl"), lax.axis_size("lat")
    odd = lax.axis_index("lvl") % 2
    halves = send.reshape(lvls // 2, 2, lats, *send.shape[1:])
    keep = lax.dynamic_index_in_dim(halves, odd, 1, False)
    give = lax.dynamic_index_in_dim(halves, 1 - odd, 1, False)
    got = lax.ppermute(give, "lvl", [(i, i ^ 1) for i in range(lvls)])
    pair = (keep.astype(f32) + got.astype(f32)).astype(bf16)
    groups = [
        [lvl * lats + lat for lvl in range(c, lvls, 2) for lat in range(lats)] for c in range(2)
    ]
    return lax.all_to_all(
        pair.reshape(-1, *send.shape[1:]), ("lvl", "lat"), 0, 0, axis_index_groups=groups, tiled=True
    )


def prepare_kernel(me_ref, bias_ref, relief_ref, wqkv_ref, bias_t_ref, col_ref, wt_ref, lane_ref, *, lvls, lats):
    me = me_ref[0]
    heads, win, _ = bias_ref.shape
    slots, rows, lon = SLOTS, win // (SLOTS * WIN_LON), relief_ref.shape[0]
    shape = (win, win)
    key, query = (lax.broadcasted_iota(jnp.int32, shape, dim) for dim in (0, 1))
    block = rows * WIN_LON
    split_slots = (key >= win // 2) != (query >= win // 2)
    half = rows // 2 * WIN_LON
    split_rows = (key % block >= half) != (query % block >= half)
    low = jnp.where(me // lats == lvls - 1, masked_score, 0.0)
    band = jnp.where(me % lats == lats - 1, masked_score, 0.0)
    hidden = jnp.where(split_slots, low, 0.0) + jnp.where(split_rows, band, 0.0)
    blank = jnp.zeros((win, WIDE - win), f32)
    for h in range(heads):
        bias_t_ref[h] = jnp.concatenate([bias_ref[h].T * log2_e + hidden, blank], 1)
    grid = relief_ref[...].astype(f32)
    lane = lax.broadcasted_iota(jnp.int32, grid.shape, 1)
    first = (me % lats) * rows + rows // 2
    for r in range(rows):
        row = (first + r) % (rows * lats)
        col = jnp.sum(jnp.where(lane == row, grid, 0.0), 1, keepdims=True)
        col = jnp.concatenate([col[WIN_LON // 2 :], col[: WIN_LON // 2]], 0)
        for w in range(lon // WIN_LON):
            for s in range(slots):
                at = w * win + (s * rows + r) * WIN_LON
                lane_ref[at : at + WIN_LON] = col[w * WIN_LON : (w + 1) * WIN_LON]
    col_ref[...] = lane_ref[...].astype(jnp.int32)
    wt_ref[...] = wqkv_ref[...].T


def prepare(me, earth_bias, relief, w_qkv, lvls, lats):
    heads, win, _ = earth_bias.shape
    rows = win // (SLOTS * WIN_LON)
    tokens = SLOTS * rows * relief.shape[1]
    sds = jax.ShapeDtypeStruct
    vmem = pl.BlockSpec(memory_space=pltpu.VMEM)
    return pl.pallas_call(
        functools.partial(prepare_kernel, lvls=lvls, lats=lats),
        in_specs=[pl.BlockSpec(memory_space=pltpu.SMEM)] + [vmem] * 3,
        out_specs=[vmem] * 3,
        out_shape=[
            sds((heads, win, WIDE), f32),
            sds((tokens, 1), jnp.int32),
            sds(w_qkv.shape[::-1], bf16),
        ],
        scratch_shapes=[pltpu.VMEM((tokens, 1), f32)],
        compiler_params=pltpu.CompilerParams(vmem_limit_bytes=40 * 2**20),
        name="prepare_inputs",
    )(me, earth_bias, relief.T, w_qkv)


def local_inputs(tokens_shape, var_weight):
    slots_dev, rows_dev, _, _ = tokens_shape
    lvl_count, lat_count = lax.axis_size("lvl"), lax.axis_size("lat")
    lvl_id, lat_id = lax.axis_index("lvl"), lax.axis_index("lat")
    level_total, lat_rows = slots_dev * lvl_count, rows_dev * lat_count
    level_ids = (
        lvl_id * slots_dev + jnp.arange(slots_dev, dtype=jnp.int32) + slots_dev // 2
    ) % level_total
    row_ids = (
        lat_id * rows_dev + jnp.arange(rows_dev, dtype=jnp.int32) + rows_dev // 2
    ) % lat_rows
    vars_n = var_weight.shape[0]
    base = jnp.broadcast_to(
        var_weight[None, :, None, None, None]
        * lat_weights(row_ids, lat_rows)[:, None, None, :, None],
        (rows_dev, vars_n, 2, 4, 4),
    ).reshape(rows_dev, vars_n * 32)
    return level_ids, base


def body(
    tokens,
    targets,
    relief,
    earth_bias,
    relief_table,
    gain_attn,
    gain_mlp,
    w_qkv,
    w_proj,
    w_up,
    w_down,
    w_out,
    var_weight,
):
    axes = ("lvl", "lat")
    devs = lax.axis_size("lvl") * lax.axis_size("lat")
    level_total = tokens.shape[0] * lax.axis_size("lvl")
    weight_sum = weight_total(relief, var_weight, level_total)
    token_halo = halo_of(tokens)
    me = lax.axis_index(axes)
    bias_t, relief_col, wt = prepare(
        me.reshape(1), earth_bias[0, 0], relief, w_qkv, lax.axis_size("lvl"), lax.axis_size("lat")
    )
    lev, base = local_inputs(tokens.shape, var_weight)
    scale = (loss_scale / weight_sum).reshape(1)
    tokens, targets, relief_col, bias_t, base, lev, scale, wt = lax.optimization_barrier(
        (tokens, targets, relief_col, bias_t, base, lev, scale, wt)
    )
    targ_halo = halo_of(targets)
    x = assemble(tokens, *token_halo)
    stream2, qt, probs, att = attention_forward(
        x, relief_col, relief_table, gain_attn, w_qkv, wt, w_proj, bias_t
    )
    stream2, targets = lax.optimization_barrier((stream2, targets))
    targ = assemble(targets, *targ_halo)
    num, gs2, send_t, up_rows = tail_both(
        me.reshape(1), scale, stream2, targ, relief_col, lev, base, att, gain_mlp, w_up, w_down, w_out, GROUP
    )
    got_t = lax.all_to_all(send_t.reshape(devs, -1, 128), axes, 0, 0, tiled=True)
    gbias_t, send_q, qkv_rows = attention_back(
        me.reshape(1), num, x, relief_col, relief_table, gain_attn, w_qkv, wt, w_proj, qt, probs, att, gs2
    )
    send_q, got_t = lax.optimization_barrier((send_q.reshape(devs, -1, 128), got_t))
    got_q = summed_by_chips(send_q)
    d = tokens.shape[-1]
    share = d // devs

    def mine(array):
        return lax.dynamic_slice_in_dim(array, me * share, share, 0)[None]

    shapes = (
        (1, 1),
        (share, w_qkv.shape[1]),
        (share, d),
        (share, w_up.shape[1]),
        (w_down.shape[0] // devs, d),
        (share, w_out.shape[1]),
        (1, share),
        (1, share),
        (share, relief_table.shape[0]),
    )
    sums = finish(
        weight_sum.reshape(1), got_t, got_q, up_rows, qkv_rows, mine(gain_mlp), mine(gain_attn), shapes
    )
    return (
        sums[0][0, 0],
        *sums[1:6],
        sums[6][0],
        sums[7][0],
        sums[8],
        gbias_t[..., : gbias_t.shape[1]].transpose(0, 2, 1)[None, None],
    )


def solution(mesh):
    field = P("lvl", "lat", None, None)
    bias = P("lvl", "lat", None, None, None)
    rows = P(("lvl", "lat"), None)
    vec = P(("lvl", "lat"))
    return jax.shard_map(
        body,
        mesh=mesh,
        in_specs=(field, field, P(), bias) + (P(),) * 9,
        out_specs=(P(), rows, rows, rows, rows, rows, vec, vec, rows, bias),
        check_vma=False,
    )
```

```python
import functools
import math

import jax
import jax.numpy as jnp
from jax import lax
from jax.experimental import pallas as pl
from jax.experimental.pallas import tpu as pltpu
from jax.sharding import PartitionSpec as P

WIN_LON = 12
HEADS = 12
GROUP = 6
DEVS = 128
WIDE = 256
SLOTS = 2
TOGETHER = 3
norm_eps = 1e-05
loss_scale = 32768.0
smooth_sq = 0.01
masked_score = -1e30
log2_e = math.log2(math.e)
f32 = jnp.float32
bf16 = jnp.bfloat16


def nn(left, right):
    return lax.dot_general(left, right, (((1,), (0,)), ((), ())), preferred_element_type=f32)


def nt(left, right):
    return lax.dot_general(left, right, (((1,), (1,)), ((), ())), preferred_element_type=f32)


def tn(left, right):
    return lax.dot_general(left, right, (((0,), (0,)), ((), ())), preferred_element_type=f32)


def normalize(values):
    width = values.shape[-1]
    centre = jnp.sum(values, -1, keepdims=True) * (1.0 / width)
    moved = values - centre
    spread = jnp.sum(moved * moved, -1, keepdims=True) * (1.0 / width)
    rstd = lax.rsqrt(spread + norm_eps)
    return moved * rstd, rstd


def norm_back(grad_hat, hat, rstd):
    width = hat.shape[-1]
    mean_g = jnp.sum(grad_hat, -1, keepdims=True) * (1.0 / width)
    mean_gh = jnp.sum(grad_hat * hat, -1, keepdims=True) * (1.0 / width)
    return rstd * (grad_hat - mean_g - hat * mean_gh)


def gelu_both(x):
    dens = jnp.exp2(x * x * (-0.5 * log2_e))
    den = 1.0 + jnp.abs(x) * (0.3275911 / math.sqrt(2.0))
    t = pl.reciprocal(den, approx=True)
    t = t * (2.0 - den * t)
    poly = 0.5 * 1.061405429
    for coef in (-1.453152027, 1.421413741, -0.284496736, 0.254829592):
        poly = poly * t + 0.5 * coef
    side = poly * t * dens
    cdf = jnp.where(x >= 0.0, 1.0 - side, side)
    return x * cdf, cdf + x * dens * (1.0 / math.sqrt(2.0 * math.pi))


def own_rows(me, weight_ref):
    rows = weight_ref.shape[0]
    share = rows // DEVS
    ids = lax.broadcasted_iota(jnp.int32, (8, rows), 0) + me * share
    picks = (lax.broadcasted_iota(jnp.int32, (8, rows), 1) == ids).astype(f32).astype(bf16)
    return nn(picks, weight_ref[...])


def pack_rows(send_ref, at, piece_ref):
    pieces, rows, _ = piece_ref.shape
    share = rows // DEVS
    every = send_ref.shape[0] // DEVS
    for i in range(share):
        for c in range(pieces):
            block = piece_ref[c, pl.ds(i, DEVS, stride=share), :]
            send_ref[pl.ds(at, DEVS, stride=every), :] = block
            at += 1
    return at


def fill_rows(send_ref, at):
    every = send_ref.shape[0] // DEVS
    for j in range(at, every):
        send_ref[pl.ds(j, DEVS, stride=every), :] = jnp.zeros((DEVS, 128), f32)


def add_pieces(piece_ref, at, grad):
    for c in range(grad.shape[1] // 128):
        piece_ref[at + c] += grad[:, c * 128 : (c + 1) * 128]


def turn_pieces(piece_ref, grad_t_ref):
    for c in range(piece_ref.shape[0]):
        piece_ref[c] = grad_t_ref[c * 128 : (c + 1) * 128].T


def one_hot_of(relief_col, classes):
    ids = lax.broadcasted_iota(jnp.int32, (relief_col.shape[0], classes), 1)
    return (relief_col == ids).astype(f32).astype(bf16)


def alone(part, place, count):
    parts = [jnp.zeros_like(part)] * count
    parts[place] = part
    return jnp.concatenate(parts, 0)


def stream_of(x_ref, relief_ref, table_ref):
    one_hot = one_hot_of(relief_ref[...], table_ref.shape[0])
    return x_ref[...].astype(f32) + nn(one_hot, table_ref[...]), one_hot


def att_kernel(
    x_ref,
    relief_ref,
    table_ref,
    gain_ref,
    wt_ref,
    wqkv_ref,
    wproj_ref,
    bias_ref,
    stream2_ref,
    qt_ref,
    prob_ref,
    att_ref,
):
    stream, _ = stream_of(x_ref, relief_ref, table_ref)
    hat, _ = normalize(stream)
    normed = (hat * gain_ref[:1]).astype(bf16)
    d = normed.shape[1]
    count, win = att_ref.shape[0], att_ref.shape[2]
    k_tok = nn(normed, wqkv_ref[:, d : 2 * d]).astype(bf16)
    e = d // HEADS
    per = 128 // e
    qvts = []
    for u in range(count):
        rows = slice(u * win, (u + 1) * win)
        filled = jnp.concatenate([normed[rows], jnp.zeros((WIDE - win, d), bf16)], 0)
        qvts.append((nt(wt_ref[:d], filled), nt(wt_ref[2 * d :], filled)))
    mixed, atts = [], []
    for u in range(count):
        rows = slice(u * win, (u + 1) * win)
        qt = (qvts[u][0] * (log2_e * e**-0.5)).astype(bf16)
        vt = qvts[u][1].astype(bf16)
        att = []
        for g in range(d // 128):
            k_four = k_tok[rows, g * 128 : (g + 1) * 128]
            heads = range(g * per, (g + 1) * per)
            scores = [nn(k_four, alone(qt[h * e : (h + 1) * e], h % per, per)) for h in heads]
            probs = []
            for h, score in zip(heads, scores):
                score = score + bias_ref[h]
                top = jnp.max(score, 0, keepdims=True)
                prob = jnp.exp2(score - top)
                prob = (prob * (1.0 / jnp.sum(prob, 0, keepdims=True))).astype(bf16)
                probs.append(prob)
                prob_ref[u, h] = prob
            att += [nn(vt[h * e : (h + 1) * e, :win], prob) for h, prob in zip(heads, probs)]
        att = jnp.concatenate(att, 0).astype(bf16)[:, :win]
        att_ref[u] = att
        qt_ref[u] = qt
        atts.append(att.T)
    stream2_ref[...] = stream + nn(jnp.concatenate(atts, 0), wproj_ref[...]).astype(bf16).astype(f32)


def tail_kernel(
    me_ref,
    wsum_ref,
    stream2_ref,
    targ_ref,
    relief_ref,
    base_ref,
    att_ref,
    gain_ref,
    wup_ref,
    wdown_ref,
    wout_ref,
    num_ref,
    gs2_ref,
    send_ref,
    wsel_ref,
    lev_ref,
    wide_ref,
    gproj_ref,
    gup_ref,
    gdown_ref,
    gout_ref,
    gdown_t_ref,
    pack_ref,
    *,
    block_f,
    lvls,
    lats,
):
    step = pl.program_id(0)
    me = me_ref[0]

    @pl.when(step == 0)
    def _():
        shape = lev_ref.shape
        slots, rows = SLOTS, shape[0] // (SLOTS * WIN_LON)
        own = (me // lats) * slots + slots // 2
        token = lax.broadcasted_iota(jnp.int32, shape, 0)
        upper = (lax.broadcasted_iota(jnp.int32, shape, 1) // 16) % 2
        line = token // WIN_LON
        lev_ref[...] = 2 * ((own + line // rows) % (slots * lvls)) + upper
        wide = jnp.zeros(shape, f32)
        for r in range(rows):
            wide = jnp.where(line % rows == r, base_ref[r : r + 1], wide)
        wide_ref[...] = wide
        num_ref[...] = jnp.zeros_like(num_ref)
        gproj_ref[...] = jnp.zeros_like(gproj_ref)
        gup_ref[...] = jnp.zeros_like(gup_ref)
        gdown_ref[...] = jnp.zeros_like(gdown_ref)
        gout_ref[...] = jnp.zeros_like(gout_ref)

    stream2 = stream2_ref[...]
    wins, win = att_ref.shape[0], att_ref.shape[2]
    ff = wup_ref.shape[1]
    hat, rstd = normalize(stream2)
    gain = gain_ref[1:2]
    normed2 = (hat * gain).astype(bf16)
    hids, slopes, gpres = [], [], []
    for n in range(0, ff, block_f):
        cols = slice(n, n + block_f)
        hidden, slope = gelu_both(nn(normed2, wup_ref[:, cols]))
        hids.append(hidden.astype(bf16))
        slopes.append(slope.astype(bf16))
    field = (stream2 + nn(jnp.concatenate(hids, 1), wdown_ref[...])).astype(bf16)
    pred = nt(field, wout_ref[...])
    relief = relief_ref[...]
    lev = jnp.concatenate([lev_ref[...]] * wins, 0)
    base = jnp.concatenate([wide_ref[...]] * wins, 0)
    cell_w = jnp.where(lev >= relief, base, 0.0)
    differ = pred - targ_ref[...].astype(f32)
    square = differ * differ + smooth_sq
    inv_err = lax.rsqrt(square)
    num_ref[...] += jnp.sum(cell_w * (square * inv_err), 0, keepdims=True)
    scale = loss_scale / wsum_ref[...]
    gpred = (scale * cell_w * differ * inv_err).astype(bf16)
    gout = nn(field.T, gpred)
    add_pieces(gout_ref, 0, gout[:, :128])
    gout_ref[1, :, : gout.shape[1] - 128] += gout[:, 128:]
    gfield = nn(gpred, wout_ref[...])
    gfb = gfield.astype(bf16)
    gfbt = gfb.T
    normed2t = normed2.T
    for n in range(0, ff, block_f):
        cols = slice(n, n + block_f)
        ghid = nt(gfb, wdown_ref[cols, :])
        gpres.append((slopes[n // block_f].astype(f32) * ghid).astype(bf16))
    for n in range(0, ff, block_f):
        cols = slice(n, n + block_f)
        gdown_ref[:, cols] += nn(gfbt, hids[n // block_f])
        add_pieces(gup_ref, n // 128, nn(normed2t, gpres[n // block_f]))
    gnorm2 = nt(jnp.concatenate(gpres, 1), wup_ref[...])
    gs2 = gfield + norm_back(gnorm2 * gain, hat, rstd)
    gs2_ref[...] = gs2
    gmix = gs2.astype(bf16)
    for w in range(wins):
        add_pieces(gproj_ref, 0, nn(att_ref[w], gmix[w * win : (w + 1) * win]))

    @pl.when(step == pl.num_programs(0) - 1)
    def _():
        wsel_ref[...] = own_rows(me, wup_ref)
        at = 0
        for ref in (gup_ref, gproj_ref, gout_ref):
            at = pack_rows(pack_ref, at, ref)
        turn_pieces(gdown_t_ref, gdown_ref)
        at = pack_rows(pack_ref, at, gdown_t_ref)
        fill_rows(pack_ref, at)
        send_ref[...] = pack_ref[...].astype(bf16)


def back_kernel(
    me_ref,
    x_ref,
    relief_ref,
    table_ref,
    gain_ref,
    wqkv_ref,
    wt_ref,
    wproj_ref,
    qt_ref,
    prob_ref,
    att_ref,
    gs2_ref,
    num_ref,
    gbias_ref,
    keep_ref,
    give_ref,
    wsel_ref,
    gqkv_ref,
    gqkv_t_ref,
    grel_ref,
    grel_t_ref,
    pack_ref,
):
    step = pl.program_id(0)

    @pl.when(step == 0)
    def _():
        gbias_ref[...] = jnp.zeros_like(gbias_ref)
        gqkv_ref[...] = jnp.zeros_like(gqkv_ref)
        grel_ref[...] = jnp.zeros_like(grel_ref)

    stream, one_hot = stream_of(x_ref, relief_ref, table_ref)
    hat, rstd = normalize(stream)
    gain = gain_ref[:1]
    normed = (hat * gain).astype(bf16)
    d = normed.shape[1]
    count, win = att_ref.shape[0], att_ref.shape[2]
    e = d // HEADS
    per = 128 // e
    gs2 = gs2_ref[...]
    gmix = gs2.astype(bf16)
    pad = jnp.zeros((WIDE - win, d), bf16)
    gatts = []
    for u in range(count):
        filled = jnp.concatenate([gmix[u * win : (u + 1) * win], pad], 0)
        gatts.append(nt(wproj_ref[...], filled).astype(bf16))
    v_tok = nn(normed, wqkv_ref[:, 2 * d :]).astype(bf16)
    kts = []
    for u in range(count):
        filled = jnp.concatenate([normed[u * win : (u + 1) * win], pad], 0)
        kts.append(nt(wt_ref[d : 2 * d], filled).astype(bf16)[:, :win])
    gshift = []
    for u in range(count):
        wrows = slice(u * win, (u + 1) * win)
        gatt_b = gatts[u]
        prod = gatt_b[:, :win].astype(f32) * att_ref[u].astype(f32)
        prod = jnp.concatenate([prod, jnp.zeros((d, WIDE - win), f32)], 1)
        qt, kt = qt_ref[u], kts[u]
        gqs, gks, gvs = [], [], []
        for g in range(d // 128):
            v_four = v_tok[wrows, g * 128 : (g + 1) * 128]
            heads = range(g * per, (g + 1) * per)
            gprobs = [nn(v_four, alone(gatt_b[h * e : (h + 1) * e], h % per, per)) for h in heads]
            gscores = []
            probs = [prob_ref[u, h] for h in heads]
            for h, gprob, prob in zip(heads, gprobs, probs):
                delta = jnp.sum(prod[h * e : (h + 1) * e], 0, keepdims=True)
                gscore = prob.astype(f32) * (gprob - delta)
                gbias_ref[h] += gscore
                gscores.append(gscore.astype(bf16))
            for h, gsb, prob in zip(heads, gscores, probs):
                rows = slice(h * e, (h + 1) * e)
                gqs.append((nn(kt[rows], gsb) * e**-0.5).astype(bf16)[:, :win])
                gks.append((nt(qt[rows], gsb) * (1.0 / log2_e)).astype(bf16))
                gvs.append(nt(gatt_b[rows], prob).astype(bf16))
        gheads = jnp.concatenate(gqs + gks + gvs, 0)
        gqkv_ref[...] += nn(gheads, normed[wrows])
        gshift.append(nn(wqkv_ref[...], gheads).astype(bf16).T.astype(f32))
    gshift = jnp.concatenate(gshift, 0)
    gstream = gs2 + norm_back(gshift * gain, hat, rstd)
    grel_ref[...] += tn(one_hot, gstream.astype(bf16))

    @pl.when(step == pl.num_programs(0) - 1)
    def _():
        wsel_ref[...] = own_rows(me_ref[0], wqkv_ref)
        turn_pieces(gqkv_t_ref, gqkv_ref)
        at = pack_rows(pack_ref, 0, gqkv_t_ref)
        classes = grel_ref.shape[0]
        wide = jnp.concatenate([grel_ref[...], jnp.zeros((128 - classes, d), f32)], 0)
        grel_t_ref[...] = wide.T
        share = d // DEVS
        num = jnp.sum(num_ref[...], 1, keepdims=True)
        high = num.astype(bf16).astype(f32)
        lane = lax.broadcasted_iota(jnp.int32, (DEVS, 128), 1)
        last = jnp.where(lane == 126, high, jnp.where(lane == 127, num - high, 0.0))
        for i in range(share):
            part = grel_t_ref[pl.ds(i, DEVS, stride=share), :]
            last += pltpu.roll(part, i * classes, 1) if i else part
        every = pack_ref.shape[0] // DEVS
        pack_ref[pl.ds(at, DEVS, stride=every), :] = last
        fill_rows(pack_ref, at + 1)
        lats = DEVS // 4
        odd = (me_ref[0] // lats) % 2
        size = lats * every
        for c in range(2):
            mine = pl.multiple_of((2 * c + odd) * size, size)
            other = pl.multiple_of((2 * c + 1 - odd) * size, size)
            keep_ref[c * size : (c + 1) * size] = pack_ref[pl.ds(mine, size), :].astype(bf16)
            give_ref[c * size : (c + 1) * size] = pack_ref[pl.ds(other, size), :].astype(bf16)


def assemble_kernel(own_ref, up_ref, side_ref, both_ref, out_ref, scr_ref):
    slots, rows, lon, _ = own_ref.shape
    hs, hr = slots // 2, rows // 2
    half = WIN_LON // 2
    win = slots * rows * WIN_LON
    for s in range(slots):
        for r in range(rows):
            if s < hs:
                plane = own_ref[hs + s, hr + r] if r < hr else side_ref[s, r - hr]
            else:
                plane = up_ref[s - hs, r] if r < hr else both_ref[s - hs, r - hr]
            plane = plane.astype(f32)
            plane = jnp.concatenate([plane[half:], plane[:half]], 0)
            for w in range(lon // WIN_LON):
                at = w * win + (s * rows + r) * WIN_LON
                scr_ref[at : at + WIN_LON] = plane[w * WIN_LON : (w + 1) * WIN_LON]
    out_ref[...] = scr_ref[...].astype(bf16)


def assemble(own, up, side, both):
    count = own.shape[0] * own.shape[1] * own.shape[2]
    return pl.pallas_call(
        assemble_kernel,
        out_shape=jax.ShapeDtypeStruct((count, own.shape[3]), bf16),
        scratch_shapes=[pltpu.VMEM((count, own.shape[3]), f32)],
        compiler_params=pltpu.CompilerParams(vmem_limit_bytes=40 * 2**20),
        name="assemble_windows",
    )(own, up, side, both)


def finish_kernel(
    weight_sum_ref, gott_ref, gotq_ref, wup_ref, wqkv_ref, gmlp_ref, gatt_ref, *outs
):
    loss_ref, gqkv_ref, gproj_ref, gup_ref, gdown_ref, gout_ref, ga_ref, gm_ref, grel_ref = outs
    got = jnp.sum(gott_ref[...].astype(f32), 0)
    at = 0
    for ref in (gup_ref, gproj_ref, gout_ref, gdown_ref):
        rows, cols = ref.shape
        for i in range(rows):
            for c in range(0, cols, 128):
                size = min(128, cols - c)
                ref[i : i + 1, c : c + size] = got[at : at + 1, :size]
                at += 1
    got = jnp.sum(gotq_ref[...].astype(f32), 0)
    at = 0
    rows, cols = gqkv_ref.shape
    for i in range(rows):
        for c in range(0, cols, 128):
            gqkv_ref[i : i + 1, c : c + 128] = got[at : at + 1]
            at += 1
    last = got[at : at + 1]
    classes = grel_ref.shape[1]
    for i in range(rows):
        grel_ref[i : i + 1, :] = last[:, i * classes : (i + 1) * classes]
    loss_ref[...] = (last[:, 126:127] + last[:, 127:128]) / weight_sum_ref[...]
    diag = lax.broadcasted_iota(jnp.int32, (rows, rows), 0) == lax.broadcasted_iota(
        jnp.int32, (rows, rows), 1
    )
    ga = jnp.sum(wqkv_ref[:rows] * gqkv_ref[...], 1, keepdims=True)
    ga_ref[...] = jnp.sum(jnp.where(diag, ga, 0.0), 0, keepdims=True) / gatt_ref[...]
    gm = jnp.sum(wup_ref[:rows] * gup_ref[...], 1, keepdims=True)
    gm_ref[...] = jnp.sum(jnp.where(diag, gm, 0.0), 0, keepdims=True) / gmlp_ref[...]


def finish(weight_sum, got_t, got_q, w_up, w_qkv, gain_mlp, gain_attn, shapes):
    vmem = pl.BlockSpec(memory_space=pltpu.VMEM)
    return pl.pallas_call(
        finish_kernel,
        in_specs=[vmem] * 7,
        out_specs=[vmem] * len(shapes),
        out_shape=[jax.ShapeDtypeStruct(shape, f32) for shape in shapes],
        compiler_params=pltpu.CompilerParams(vmem_limit_bytes=40 * 2**20),
        name="finish_sums",
    )(weight_sum, got_t, got_q, w_up, w_qkv, gain_mlp, gain_attn)


def whole(shape):
    return pl.BlockSpec(shape, lambda i: (0,) * len(shape))


def lead(shape):
    return pl.BlockSpec(shape, lambda i: (i,) + (0,) * (len(shape) - 1))


def params_of():
    return pltpu.CompilerParams(
        vmem_limit_bytes=56 * 2**20, dimension_semantics=("arbitrary",)
    )


def attention_forward(x, relief_col, table, gain, w_qkv, wt, w_proj, bias_t):
    t, d = x.shape
    win = bias_t.shape[1]
    count = t // win
    sds = jax.ShapeDtypeStruct
    return pl.pallas_call(
        att_kernel,
        grid=(count // TOGETHER,),
        in_specs=[
            lead((TOGETHER * win, d)),
            lead((TOGETHER * win, 1)),
            whole(table.shape),
            whole((2, d)),
            whole((3 * d, d)),
            whole((d, 3 * d)),
            whole((d, d)),
            whole(bias_t.shape),
        ],
        out_specs=[
            lead((TOGETHER * win, d)),
            lead((TOGETHER, d, WIDE)),
            lead((TOGETHER, HEADS, win, WIDE)),
            lead((TOGETHER, d, win)),
        ],
        out_shape=[
            sds((t, d), f32),
            sds((count, d, WIDE), bf16),
            sds((count, HEADS, win, WIDE), bf16),
            sds((count, d, win), bf16),
        ],
        compiler_params=params_of(),
        name="attention_forward",
    )(
        x,
        relief_col,
        table,
        gain,
        wt,
        w_qkv,
        w_proj,
        bias_t,
    )


def cost(flops, moved, trans):
    return pl.CostEstimate(flops=flops, bytes_accessed=moved, transcendentals=trans)


def tail_both(me, wsum, stream2, targ, relief_col, base, att, gains, w_up, w_down, w_out, group, lvls, lats):
    t, d = stream2.shape
    win = att.shape[-1]
    m = group * win
    ff, out = w_up.shape[1], w_out.shape[1]
    pieces = (d * ff + d * d + d * 256 + d * ff) // (DEVS * 128)
    pieces += -pieces % 8
    sds = jax.ShapeDtypeStruct
    return pl.pallas_call(
        functools.partial(tail_kernel, block_f=256, lvls=lvls, lats=lats),
        grid=(t // m,),
        in_specs=[
            pl.BlockSpec(memory_space=pltpu.SMEM),
            whole((1, 1)),
            lead((m, d)),
            lead((m, out)),
            lead((m, 1)),
            whole(base.shape),
            lead((group, d, win)),
            whole((2, d)),
            whole((d, ff)),
            whole((ff, d)),
            whole((out, d)),
        ],
        out_specs=[
            whole((1, out)),
            lead((m, d)),
            whole((DEVS * pieces, 128)),
            whole((8, ff)),
        ],
        out_shape=[
            sds((1, out), f32),
            sds((t, d), f32),
            sds((DEVS * pieces, 128), bf16),
            sds((8, ff), f32),
        ],
        scratch_shapes=[
            pltpu.VMEM((win, out), jnp.int32),
            pltpu.VMEM((win, out), f32),
            pltpu.VMEM((d // 128, d, 128), f32),
            pltpu.VMEM((ff // 128, d, 128), f32),
            pltpu.VMEM((d, ff), f32),
            pltpu.VMEM((2, d, 128), f32),
            pltpu.VMEM((d // 128, ff, 128), f32),
            pltpu.VMEM((DEVS * pieces, 128), f32),
        ],
        compiler_params=params_of(),
        name="tail_both",
    )(me, wsum, stream2, targ, relief_col, base, att, gains, w_up, w_down, w_out.T)


def attention_back(me, num, x, relief_col, table, gain, w_qkv, wt, w_proj, qt, probs, att, gs2):
    t, d = x.shape
    count, win = att.shape[0], att.shape[2]
    sds = jax.ShapeDtypeStruct
    return pl.pallas_call(
        back_kernel,
        grid=(count // TOGETHER,),
        in_specs=[
            pl.BlockSpec(memory_space=pltpu.SMEM),
            lead((TOGETHER * win, d)),
            lead((TOGETHER * win, 1)),
            whole(table.shape),
            whole((2, d)),
            whole((d, 3 * d)),
            whole((3 * d, d)),
            whole((d, d)),
            lead((TOGETHER, d, WIDE)),
            lead((TOGETHER, HEADS, win, WIDE)),
            lead((TOGETHER, d, win)),
            lead((TOGETHER * win, d)),
            whole(num.shape),
        ],
        out_specs=[
            whole((HEADS, win, WIDE)),
            whole((DEVS * 16, 128)),
            whole((DEVS * 16, 128)),
            whole((8, 3 * d)),
        ],
        out_shape=[
            sds((HEADS, win, WIDE), f32),
            sds((DEVS * 16, 128), bf16),
            sds((DEVS * 16, 128), bf16),
            sds((8, 3 * d), f32),
        ],
        scratch_shapes=[
            pltpu.VMEM((3 * d, d), f32),
            pltpu.VMEM((3 * d // 128, d, 128), f32),
            pltpu.VMEM((table.shape[0], d), f32),
            pltpu.VMEM((d, 128), f32),
            pltpu.VMEM((DEVS * 32, 128), f32),
        ],
        compiler_params=params_of(),
        cost_estimate=cost(10 * 2**30, 20 * 2**20, 0),
        name="attention_back",
    )(me, x, relief_col, table, gain, w_qkv, wt, w_proj, qt, probs, att, gs2, num)


def from_next(value, axes):
    sizes = [lax.axis_size(a) for a in ("lvl", "lat")]
    move = [1 if a in axes else 0 for a in ("lvl", "lat")]
    pairs = []
    for i in range(sizes[0]):
        for j in range(sizes[1]):
            src = (i + move[0]) % sizes[0] * sizes[1] + (j + move[1]) % sizes[1]
            pairs.append((src, i * sizes[1] + j))
    return lax.ppermute(value, ("lvl", "lat"), pairs)


def halo_of(field_in):
    slots_n, rows_n = field_in.shape[:2]
    hs, hr = slots_n // 2, rows_n // 2
    up = from_next(field_in[:hs, hr:], ("lvl",))
    side = from_next(field_in[hs:, :hr], ("lat",))
    both = from_next(field_in[:hs, :hr], ("lvl", "lat"))
    return up, side, both


def cos_latitude(fine_rows, lat_rows):
    angle = 90.0 - 180.0 * (fine_rows.astype(f32) + 0.5) / (4.0 * lat_rows)
    return jnp.cos(angle * (math.pi / 180.0))


def prepare_kernel(
    me_ref,
    var_ref,
    bias_ref,
    relief_ref,
    wqkv_ref,
    bias_t_ref,
    col_ref,
    wt_ref,
    base_ref,
    wsum_ref,
    lane_ref,
    *,
    lvls,
    lats,
):
    me = me_ref[0]
    heads, win, _ = bias_ref.shape
    slots, rows, lon = SLOTS, win // (SLOTS * WIN_LON), relief_ref.shape[0]
    shape = (win, win)
    key, query = (lax.broadcasted_iota(jnp.int32, shape, dim) for dim in (0, 1))
    block = rows * WIN_LON
    split_slots = (key >= win // 2) != (query >= win // 2)
    half = rows // 2 * WIN_LON
    split_rows = (key % block >= half) != (query % block >= half)
    low = jnp.where(me // lats == lvls - 1, masked_score, 0.0)
    band = jnp.where(me % lats == lats - 1, masked_score, 0.0)
    hidden = jnp.where(split_slots, low, 0.0) + jnp.where(split_rows, band, 0.0)
    blank = jnp.zeros((win, WIDE - win), f32)
    for h in range(heads):
        bias_t_ref[h] = jnp.concatenate([bias_ref[h].T * log2_e + hidden, blank], 1)
    grid = relief_ref[...].astype(f32)
    lane = lax.broadcasted_iota(jnp.int32, grid.shape, 1)
    first = (me % lats) * rows + rows // 2
    for r in range(rows):
        row = (first + r) % (rows * lats)
        col = jnp.sum(jnp.where(lane == row, grid, 0.0), 1, keepdims=True)
        col = jnp.concatenate([col[WIN_LON // 2 :], col[: WIN_LON // 2]], 0)
        for w in range(lon // WIN_LON):
            for s in range(slots):
                at = w * win + (s * rows + r) * WIN_LON
                lane_ref[at : at + WIN_LON] = col[w * WIN_LON : (w + 1) * WIN_LON]
    col_ref[...] = lane_ref[...].astype(jnp.int32)
    lat_rows = rows * lats
    vars_n = var_ref.shape[0]
    shape = base_ref.shape
    chan = lax.broadcasted_iota(jnp.int32, shape, 1)
    row = (first + lax.broadcasted_iota(jnp.int32, shape, 0)) % lat_rows
    var = jnp.zeros(shape, f32)
    var_sum = var_ref[0]
    for v in range(vars_n):
        var = jnp.where(chan // 32 == v, var_ref[v], var)
        var_sum = var_sum + var_ref[v] if v else var_sum
    base_ref[...] = var * cos_latitude(4 * row + (chan // 4) % 4, lat_rows)
    shape = (8, lat_rows)
    part = lax.broadcasted_iota(jnp.int32, shape, 0)
    fine = 4 * lax.broadcasted_iota(jnp.int32, shape, 1) + part
    lat_weight = jnp.sum(jnp.where(part < 4, cos_latitude(fine, lat_rows), 0.0), 0, keepdims=True)
    live = jnp.sum(2.0 * slots * lvls - grid, 0, keepdims=True)
    wsum_ref[...] = jnp.sum(lat_weight * live, 1, keepdims=True) * (4.0 * var_sum)
    wt_ref[...] = wqkv_ref[...].T


def prepare(me, var_weight, earth_bias, relief, w_qkv, lvls, lats):
    heads, win, _ = earth_bias.shape
    rows = win // (SLOTS * WIN_LON)
    tokens = SLOTS * rows * relief.shape[1]
    sds = jax.ShapeDtypeStruct
    vmem = pl.BlockSpec(memory_space=pltpu.VMEM)
    return pl.pallas_call(
        functools.partial(prepare_kernel, lvls=lvls, lats=lats),
        in_specs=[pl.BlockSpec(memory_space=pltpu.SMEM)] * 2 + [vmem] * 3,
        out_specs=[vmem] * 5,
        out_shape=[
            sds((heads, win, WIDE), f32),
            sds((tokens, 1), jnp.int32),
            sds(w_qkv.shape[::-1], bf16),
            sds((8, var_weight.shape[0] * 32), f32),
            sds((1, 1), f32),
        ],
        scratch_shapes=[pltpu.VMEM((tokens, 1), f32)],
        compiler_params=pltpu.CompilerParams(vmem_limit_bytes=40 * 2**20),
        name="prepare_inputs",
    )(me, var_weight, earth_bias, relief.T, w_qkv)


def body(
    tokens,
    targets,
    relief,
    earth_bias,
    relief_table,
    gain_attn,
    gain_mlp,
    w_qkv,
    w_proj,
    w_up,
    w_down,
    w_out,
    var_weight,
):
    axes = ("lvl", "lat")
    devs = lax.axis_size("lvl") * lax.axis_size("lat")
    token_halo = halo_of(tokens)
    me = lax.axis_index(axes)
    lvls, lats = lax.axis_size("lvl"), lax.axis_size("lat")
    bias_t, relief_col, wt, base, wsum = prepare(
        me.reshape(1), var_weight, earth_bias[0, 0], relief, w_qkv, lvls, lats
    )
    gains = jnp.stack([gain_attn, gain_mlp])
    tokens, targets, relief_col, bias_t, base, wsum, wt, gains = lax.optimization_barrier(
        (tokens, targets, relief_col, bias_t, base, wsum, wt, gains)
    )
    targ_halo = halo_of(targets)
    x = assemble(tokens, *token_halo)
    stream2, qt, probs, att = attention_forward(
        x, relief_col, relief_table, gains, w_qkv, wt, w_proj, bias_t
    )
    stream2, targets = lax.optimization_barrier((stream2, targets))
    targ = assemble(targets, *targ_halo)
    num, gs2, send_t, up_rows = tail_both(
        me.reshape(1), wsum, stream2, targ, relief_col, base, att, gains, w_up, w_down, w_out, GROUP, lvls, lats
    )
    got_t = lax.all_to_all(send_t.reshape(devs, -1, 128), axes, 0, 0, tiled=True)
    gbias_t, keep, give, qkv_rows = attention_back(
        me.reshape(1), num, x, relief_col, relief_table, gains, w_qkv, wt, w_proj, qt, probs, att, gs2
    )
    got = lax.ppermute(give, "lvl", [(i, i ^ 1) for i in range(lvls)])
    pair = (keep.astype(f32) + got.astype(f32)).astype(bf16)
    pair, got_t = lax.optimization_barrier((pair, got_t))
    groups = [
        [lvl * lats + lat for lvl in range(c, lvls, 2) for lat in range(lats)] for c in range(2)
    ]
    got_q = lax.all_to_all(
        pair.reshape(devs // 2, -1, 128), axes, 0, 0, axis_index_groups=groups, tiled=True
    )
    d = tokens.shape[-1]
    share = d // devs

    def mine(array):
        return lax.dynamic_slice_in_dim(array, me * share, share, 0)[None]

    shapes = (
        (1, 1),
        (share, w_qkv.shape[1]),
        (share, d),
        (share, w_up.shape[1]),
        (w_down.shape[0] // devs, d),
        (share, w_out.shape[1]),
        (1, share),
        (1, share),
        (share, relief_table.shape[0]),
    )
    sums = finish(
        wsum, got_t, got_q, up_rows, qkv_rows, mine(gain_mlp), mine(gain_attn), shapes
    )
    return (
        sums[0][0, 0],
        *sums[1:6],
        sums[6][0],
        sums[7][0],
        sums[8],
        gbias_t[..., : gbias_t.shape[1]].transpose(0, 2, 1)[None, None],
    )


def solution(mesh):
    field = P("lvl", "lat", None, None)
    bias = P("lvl", "lat", None, None, None)
    rows = P(("lvl", "lat"), None)
    vec = P(("lvl", "lat"))
    return jax.shard_map(
        body,
        mesh=mesh,
        in_specs=(field, field, P(), bias) + (P(),) * 9,
        out_specs=(P(), rows, rows, rows, rows, rows, vec, vec, rows, bias),
        check_vma=False,
    )
```

```python
import functools
import math

import jax
import jax.numpy as jnp
from jax import lax
from jax.experimental import pallas as pl
from jax.experimental.pallas import tpu as pltpu
from jax.sharding import PartitionSpec as P

WIN_LON = 12
HEADS = 12
GROUP = 6
DEVS = 128
WIDE = 256
SLOTS = 2
TOGETHER = 3
norm_eps = 1e-05
loss_scale = 32768.0
smooth_sq = 0.01
masked_score = -1e30
log2_e = math.log2(math.e)
f32 = jnp.float32
bf16 = jnp.bfloat16


def nn(left, right):
    return lax.dot_general(left, right, (((1,), (0,)), ((), ())), preferred_element_type=f32)


def nt(left, right):
    return lax.dot_general(left, right, (((1,), (1,)), ((), ())), preferred_element_type=f32)


def tn(left, right):
    return lax.dot_general(left, right, (((0,), (0,)), ((), ())), preferred_element_type=f32)


def normalize(values):
    width = values.shape[-1]
    centre = jnp.sum(values, -1, keepdims=True) * (1.0 / width)
    moved = values - centre
    spread = jnp.sum(moved * moved, -1, keepdims=True) * (1.0 / width)
    rstd = lax.rsqrt(spread + norm_eps)
    return moved * rstd, rstd


def norm_back(grad_hat, hat, rstd):
    width = hat.shape[-1]
    mean_g = jnp.sum(grad_hat, -1, keepdims=True) * (1.0 / width)
    mean_gh = jnp.sum(grad_hat * hat, -1, keepdims=True) * (1.0 / width)
    return rstd * (grad_hat - mean_g - hat * mean_gh)


def gelu_both(x):
    dens = jnp.exp2(x * x * (-0.5 * log2_e))
    den = 1.0 + jnp.abs(x) * (0.3275911 / math.sqrt(2.0))
    t = pl.reciprocal(den, approx=True)
    t = t * (2.0 - den * t)
    poly = 0.5 * 1.061405429
    for coef in (-1.453152027, 1.421413741, -0.284496736, 0.254829592):
        poly = poly * t + 0.5 * coef
    side = poly * t * dens
    cdf = jnp.where(x >= 0.0, 1.0 - side, side)
    return x * cdf, cdf + x * dens * (1.0 / math.sqrt(2.0 * math.pi))


def own_rows(me, weight_ref):
    rows = weight_ref.shape[0]
    share = rows // DEVS
    ids = lax.broadcasted_iota(jnp.int32, (8, rows), 0) + me * share
    picks = (lax.broadcasted_iota(jnp.int32, (8, rows), 1) == ids).astype(f32).astype(bf16)
    return nn(picks, weight_ref[...])


def pack_rows(send_ref, at, piece_ref):
    pieces, rows, _ = piece_ref.shape
    share = rows // DEVS
    every = send_ref.shape[0] // DEVS
    for i in range(share):
        for c in range(pieces):
            block = piece_ref[c, pl.ds(i, DEVS, stride=share), :]
            send_ref[pl.ds(at, DEVS, stride=every), :] = block
            at += 1
    return at


def fill_rows(send_ref, at):
    every = send_ref.shape[0] // DEVS
    for j in range(at, every):
        send_ref[pl.ds(j, DEVS, stride=every), :] = jnp.zeros((DEVS, 128), f32)


def add_pieces(piece_ref, at, grad):
    for c in range(grad.shape[1] // 128):
        piece_ref[at + c] += grad[:, c * 128 : (c + 1) * 128]


def turn_pieces(piece_ref, grad_t_ref):
    for c in range(piece_ref.shape[0]):
        piece_ref[c] = grad_t_ref[c * 128 : (c + 1) * 128].T


def one_hot_of(relief_col, classes):
    ids = lax.broadcasted_iota(jnp.int32, (relief_col.shape[0], classes), 1)
    return (relief_col == ids).astype(f32).astype(bf16)


def alone(part, place, count):
    parts = [jnp.zeros_like(part)] * count
    parts[place] = part
    return jnp.concatenate(parts, 0)


def stream_of(x_ref, relief_ref, table_ref):
    one_hot = one_hot_of(relief_ref[...], table_ref.shape[0])
    return x_ref[...].astype(f32) + nn(one_hot, table_ref[...]), one_hot


def att_kernel(
    x_ref,
    relief_ref,
    table_ref,
    gain_ref,
    wt_ref,
    wqkv_ref,
    wproj_ref,
    bias_ref,
    stream2_ref,
    qt_ref,
    prob_ref,
    att_ref,
):
    stream, _ = stream_of(x_ref, relief_ref, table_ref)
    hat, _ = normalize(stream)
    normed = (hat * gain_ref[:1]).astype(bf16)
    d = normed.shape[1]
    count, win = att_ref.shape[0], att_ref.shape[2]
    k_tok = nn(normed, wqkv_ref[:, d : 2 * d]).astype(bf16)
    e = d // HEADS
    per = 128 // e
    qvts = []
    for u in range(count):
        rows = slice(u * win, (u + 1) * win)
        filled = jnp.concatenate([normed[rows], jnp.zeros((WIDE - win, d), bf16)], 0)
        qvts.append((nt(wt_ref[:d], filled), nt(wt_ref[2 * d :], filled)))
    mixed, atts = [], []
    for u in range(count):
        rows = slice(u * win, (u + 1) * win)
        qt = (qvts[u][0] * (log2_e * e**-0.5)).astype(bf16)
        vt = qvts[u][1].astype(bf16)
        att = []
        for g in range(d // 128):
            k_four = k_tok[rows, g * 128 : (g + 1) * 128]
            heads = range(g * per, (g + 1) * per)
            scores = [nn(k_four, alone(qt[h * e : (h + 1) * e], h % per, per)) for h in heads]
            probs = []
            for h, score in zip(heads, scores):
                score = score + bias_ref[h]
                top = jnp.max(score, 0, keepdims=True)
                prob = jnp.exp2(score - top)
                prob = (prob * (1.0 / jnp.sum(prob, 0, keepdims=True))).astype(bf16)
                probs.append(prob)
                prob_ref[u, h] = prob
            att += [nn(vt[h * e : (h + 1) * e, :win], prob) for h, prob in zip(heads, probs)]
        att = jnp.concatenate(att, 0).astype(bf16)[:, :win]
        att_ref[u] = att
        qt_ref[u] = qt
        atts.append(att.T)
    stream2_ref[...] = stream + nn(jnp.concatenate(atts, 0), wproj_ref[...]).astype(bf16).astype(f32)


def tail_kernel(
    me_ref,
    wsum_ref,
    stream2_ref,
    targ_ref,
    relief_ref,
    base_ref,
    att_ref,
    gain_ref,
    wup_ref,
    wdown_ref,
    wout_ref,
    num_ref,
    gs2_ref,
    send_ref,
    wsel_ref,
    lev_ref,
    wide_ref,
    gproj_ref,
    gup_ref,
    gdown_ref,
    gout_ref,
    gdown_t_ref,
    pack_ref,
    *,
    block_f,
    lvls,
    lats,
):
    step = pl.program_id(0)
    me = me_ref[0]

    @pl.when(step == 0)
    def _():
        shape = lev_ref.shape
        slots, rows = SLOTS, shape[0] // (SLOTS * WIN_LON)
        own = (me // lats) * slots + slots // 2
        token = lax.broadcasted_iota(jnp.int32, shape, 0)
        upper = (lax.broadcasted_iota(jnp.int32, shape, 1) // 16) % 2
        line = token // WIN_LON
        lev_ref[...] = 2 * ((own + line // rows) % (slots * lvls)) + upper
        wide = jnp.zeros(shape, f32)
        for r in range(rows):
            wide = jnp.where(line % rows == r, base_ref[r : r + 1], wide)
        wide_ref[...] = wide
        num_ref[...] = jnp.zeros_like(num_ref)
        gproj_ref[...] = jnp.zeros_like(gproj_ref)
        gup_ref[...] = jnp.zeros_like(gup_ref)
        gdown_ref[...] = jnp.zeros_like(gdown_ref)
        gout_ref[...] = jnp.zeros_like(gout_ref)

    stream2 = stream2_ref[...]
    wins, win = att_ref.shape[0], att_ref.shape[2]
    ff = wup_ref.shape[1]
    hat, rstd = normalize(stream2)
    gain = gain_ref[1:2]
    normed2 = (hat * gain).astype(bf16)
    hids, slopes, gpres = [], [], []
    for n in range(0, ff, block_f):
        cols = slice(n, n + block_f)
        hidden, slope = gelu_both(nn(normed2, wup_ref[:, cols]))
        hids.append(hidden.astype(bf16))
        slopes.append(slope.astype(bf16))
    field = (stream2 + nn(jnp.concatenate(hids, 1), wdown_ref[...])).astype(bf16)
    pred = nt(field, wout_ref[...])
    relief = relief_ref[...]
    lev = jnp.concatenate([lev_ref[...]] * wins, 0)
    base = jnp.concatenate([wide_ref[...]] * wins, 0)
    cell_w = jnp.where(lev >= relief, base, 0.0)
    differ = pred - targ_ref[...].astype(f32)
    square = differ * differ + smooth_sq
    inv_err = lax.rsqrt(square)
    num_ref[...] += jnp.sum(cell_w * (square * inv_err), 0, keepdims=True)
    scale = loss_scale / wsum_ref[...]
    gpred = (scale * cell_w * differ * inv_err).astype(bf16)
    gout = nn(field.T, gpred)
    add_pieces(gout_ref, 0, gout[:, :128])
    gout_ref[1, :, : gout.shape[1] - 128] += gout[:, 128:]
    gfield = nn(gpred, wout_ref[...])
    gfb = gfield.astype(bf16)
    gfbt = gfb.T
    normed2t = normed2.T
    for n in range(0, ff, block_f):
        cols = slice(n, n + block_f)
        ghid = nt(gfb, wdown_ref[cols, :])
        gpres.append((slopes[n // block_f].astype(f32) * ghid).astype(bf16))
    for n in range(0, ff, block_f):
        cols = slice(n, n + block_f)
        gdown_ref[:, cols] += nn(gfbt, hids[n // block_f])
        add_pieces(gup_ref, n // 128, nn(normed2t, gpres[n // block_f]))
    gnorm2 = nt(jnp.concatenate(gpres, 1), wup_ref[...])
    gs2 = gfield + norm_back(gnorm2 * gain, hat, rstd)
    gs2_ref[...] = gs2
    gmix = gs2.astype(bf16)
    for w in range(wins):
        add_pieces(gproj_ref, 0, nn(att_ref[w], gmix[w * win : (w + 1) * win]))

    @pl.when(step == pl.num_programs(0) - 1)
    def _():
        wsel_ref[...] = own_rows(me, wup_ref)
        at = 0
        for ref in (gup_ref, gproj_ref, gout_ref):
            at = pack_rows(pack_ref, at, ref)
        turn_pieces(gdown_t_ref, gdown_ref)
        at = pack_rows(pack_ref, at, gdown_t_ref)
        fill_rows(pack_ref, at)
        send_ref[...] = pack_ref[...].astype(bf16)


def back_kernel(
    me_ref,
    x_ref,
    relief_ref,
    table_ref,
    gain_ref,
    wqkv_ref,
    wt_ref,
    wproj_ref,
    qt_ref,
    prob_ref,
    att_ref,
    gs2_ref,
    num_ref,
    gbias_ref,
    keep_ref,
    give_ref,
    wsel_ref,
    gqkv_ref,
    grel_ref,
    grel_t_ref,
    pack_ref,
):
    step = pl.program_id(0)

    @pl.when(step == 0)
    def _():
        gbias_ref[...] = jnp.zeros_like(gbias_ref)
        gqkv_ref[...] = jnp.zeros_like(gqkv_ref)
        grel_ref[...] = jnp.zeros_like(grel_ref)

    stream, one_hot = stream_of(x_ref, relief_ref, table_ref)
    hat, rstd = normalize(stream)
    gain = gain_ref[:1]
    normed = (hat * gain).astype(bf16)
    d = normed.shape[1]
    count, win = att_ref.shape[0], att_ref.shape[2]
    e = d // HEADS
    per = 128 // e
    gs2 = gs2_ref[...]
    gmix = gs2.astype(bf16)
    pad = jnp.zeros((WIDE - win, d), bf16)
    gatts = []
    for u in range(count):
        filled = jnp.concatenate([gmix[u * win : (u + 1) * win], pad], 0)
        gatts.append(nt(wproj_ref[...], filled).astype(bf16))
    v_tok = nn(normed, wqkv_ref[:, 2 * d :]).astype(bf16)
    kts = []
    for u in range(count):
        filled = jnp.concatenate([normed[u * win : (u + 1) * win], pad], 0)
        kts.append(nt(wt_ref[d : 2 * d], filled).astype(bf16)[:, :win])
    gturned = []
    for u in range(count):
        wrows = slice(u * win, (u + 1) * win)
        gatt_b = gatts[u]
        prod = gatt_b[:, :win].astype(f32) * att_ref[u].astype(f32)
        prod = jnp.concatenate([prod, jnp.zeros((d, WIDE - win), f32)], 1)
        qt, kt = qt_ref[u], kts[u]
        gqs, gks, gvs = [], [], []
        for g in range(d // 128):
            v_four = v_tok[wrows, g * 128 : (g + 1) * 128]
            heads = range(g * per, (g + 1) * per)
            gprobs = [nn(v_four, alone(gatt_b[h * e : (h + 1) * e], h % per, per)) for h in heads]
            gscores = []
            probs = [prob_ref[u, h] for h in heads]
            for h, gprob, prob in zip(heads, gprobs, probs):
                delta = jnp.sum(prod[h * e : (h + 1) * e], 0, keepdims=True)
                gscore = prob.astype(f32) * (gprob - delta)
                gbias_ref[h] += gscore
                gscores.append(gscore.astype(bf16))
            for h, gsb, prob in zip(heads, gscores, probs):
                rows = slice(h * e, (h + 1) * e)
                gqs.append((nn(kt[rows], gsb) * e**-0.5).astype(bf16)[:, :win])
                gks.append((nt(qt[rows], gsb) * (1.0 / log2_e)).astype(bf16))
                gvs.append(nt(gatt_b[rows], prob).astype(bf16))
        gheads = jnp.concatenate(gqs + gks + gvs, 0)
        gturned.append(gheads.T)
    gturned = jnp.concatenate(gturned, 0)
    gshift = nn(gturned, wt_ref[...]).astype(bf16).astype(f32)
    add_pieces(gqkv_ref, 0, nn(normed.T, gturned))
    gstream = gs2 + norm_back(gshift * gain, hat, rstd)
    grel_ref[...] += tn(one_hot, gstream.astype(bf16))

    @pl.when(step == pl.num_programs(0) - 1)
    def _():
        wsel_ref[...] = own_rows(me_ref[0], wqkv_ref)
        at = pack_rows(pack_ref, 0, gqkv_ref)
        classes = grel_ref.shape[0]
        wide = jnp.concatenate([grel_ref[...], jnp.zeros((128 - classes, d), f32)], 0)
        grel_t_ref[...] = wide.T
        share = d // DEVS
        num = jnp.sum(num_ref[...], 1, keepdims=True)
        high = num.astype(bf16).astype(f32)
        lane = lax.broadcasted_iota(jnp.int32, (DEVS, 128), 1)
        last = jnp.where(lane == 126, high, jnp.where(lane == 127, num - high, 0.0))
        for i in range(share):
            part = grel_t_ref[pl.ds(i, DEVS, stride=share), :]
            last += pltpu.roll(part, i * classes, 1) if i else part
        every = pack_ref.shape[0] // DEVS
        pack_ref[pl.ds(at, DEVS, stride=every), :] = last
        fill_rows(pack_ref, at + 1)
        lats = DEVS // 4
        odd = (me_ref[0] // lats) % 2
        size = lats * every
        for c in range(2):
            mine = pl.multiple_of((2 * c + odd) * size, size)
            other = pl.multiple_of((2 * c + 1 - odd) * size, size)
            keep_ref[c * size : (c + 1) * size] = pack_ref[pl.ds(mine, size), :].astype(bf16)
            give_ref[c * size : (c + 1) * size] = pack_ref[pl.ds(other, size), :].astype(bf16)


def assemble_kernel(own_ref, up_ref, side_ref, both_ref, out_ref, scr_ref):
    slots, rows, lon, _ = own_ref.shape
    hs, hr = slots // 2, rows // 2
    half = WIN_LON // 2
    win = slots * rows * WIN_LON
    for s in range(slots):
        for r in range(rows):
            if s < hs:
                plane = own_ref[hs + s, hr + r] if r < hr else side_ref[s, r - hr]
            else:
                plane = up_ref[s - hs, r] if r < hr else both_ref[s - hs, r - hr]
            plane = plane.astype(f32)
            plane = jnp.concatenate([plane[half:], plane[:half]], 0)
            for w in range(lon // WIN_LON):
                at = w * win + (s * rows + r) * WIN_LON
                scr_ref[at : at + WIN_LON] = plane[w * WIN_LON : (w + 1) * WIN_LON]
    out_ref[...] = scr_ref[...].astype(bf16)


def assemble(own, up, side, both):
    count = own.shape[0] * own.shape[1] * own.shape[2]
    return pl.pallas_call(
        assemble_kernel,
        out_shape=jax.ShapeDtypeStruct((count, own.shape[3]), bf16),
        scratch_shapes=[pltpu.VMEM((count, own.shape[3]), f32)],
        compiler_params=pltpu.CompilerParams(vmem_limit_bytes=40 * 2**20),
        name="assemble_windows",
    )(own, up, side, both)


def finish_kernel(
    weight_sum_ref, gott_ref, gotq_ref, wup_ref, wqkv_ref, gmlp_ref, gatt_ref, *outs
):
    loss_ref, gqkv_ref, gproj_ref, gup_ref, gdown_ref, gout_ref, ga_ref, gm_ref, grel_ref = outs
    got = jnp.sum(gott_ref[...].astype(f32), 0)
    at = 0
    for ref in (gup_ref, gproj_ref, gout_ref, gdown_ref):
        rows, cols = ref.shape
        for i in range(rows):
            for c in range(0, cols, 128):
                size = min(128, cols - c)
                ref[i : i + 1, c : c + size] = got[at : at + 1, :size]
                at += 1
    got = jnp.sum(gotq_ref[...].astype(f32), 0)
    at = 0
    rows, cols = gqkv_ref.shape
    for i in range(rows):
        for c in range(0, cols, 128):
            gqkv_ref[i : i + 1, c : c + 128] = got[at : at + 1]
            at += 1
    last = got[at : at + 1]
    classes = grel_ref.shape[1]
    for i in range(rows):
        grel_ref[i : i + 1, :] = last[:, i * classes : (i + 1) * classes]
    loss_ref[...] = (last[:, 126:127] + last[:, 127:128]) / weight_sum_ref[...]
    diag = lax.broadcasted_iota(jnp.int32, (rows, rows), 0) == lax.broadcasted_iota(
        jnp.int32, (rows, rows), 1
    )
    ga = jnp.sum(wqkv_ref[:rows] * gqkv_ref[...], 1, keepdims=True)
    ga_ref[...] = jnp.sum(jnp.where(diag, ga, 0.0), 0, keepdims=True) / gatt_ref[...]
    gm = jnp.sum(wup_ref[:rows] * gup_ref[...], 1, keepdims=True)
    gm_ref[...] = jnp.sum(jnp.where(diag, gm, 0.0), 0, keepdims=True) / gmlp_ref[...]


def finish(weight_sum, got_t, got_q, w_up, w_qkv, gain_mlp, gain_attn, shapes):
    vmem = pl.BlockSpec(memory_space=pltpu.VMEM)
    return pl.pallas_call(
        finish_kernel,
        in_specs=[vmem] * 7,
        out_specs=[vmem] * len(shapes),
        out_shape=[jax.ShapeDtypeStruct(shape, f32) for shape in shapes],
        compiler_params=pltpu.CompilerParams(vmem_limit_bytes=40 * 2**20),
        name="finish_sums",
    )(weight_sum, got_t, got_q, w_up, w_qkv, gain_mlp, gain_attn)


def whole(shape):
    return pl.BlockSpec(shape, lambda i: (0,) * len(shape))


def lead(shape):
    return pl.BlockSpec(shape, lambda i: (i,) + (0,) * (len(shape) - 1))


def params_of():
    return pltpu.CompilerParams(
        vmem_limit_bytes=56 * 2**20, dimension_semantics=("arbitrary",)
    )


def attention_forward(x, relief_col, table, gain, w_qkv, wt, w_proj, bias_t):
    t, d = x.shape
    win = bias_t.shape[1]
    count = t // win
    sds = jax.ShapeDtypeStruct
    return pl.pallas_call(
        att_kernel,
        grid=(count // TOGETHER,),
        in_specs=[
            lead((TOGETHER * win, d)),
            lead((TOGETHER * win, 1)),
            whole(table.shape),
            whole((2, d)),
            whole((3 * d, d)),
            whole((d, 3 * d)),
            whole((d, d)),
            whole(bias_t.shape),
        ],
        out_specs=[
            lead((TOGETHER * win, d)),
            lead((TOGETHER, d, WIDE)),
            lead((TOGETHER, HEADS, win, WIDE)),
            lead((TOGETHER, d, win)),
        ],
        out_shape=[
            sds((t, d), f32),
            sds((count, d, WIDE), bf16),
            sds((count, HEADS, win, WIDE), bf16),
            sds((count, d, win), bf16),
        ],
        compiler_params=params_of(),
        name="attention_forward",
    )(
        x,
        relief_col,
        table,
        gain,
        wt,
        w_qkv,
        w_proj,
        bias_t,
    )


def cost(flops, moved, trans):
    return pl.CostEstimate(flops=flops, bytes_accessed=moved, transcendentals=trans)


def tail_both(me, wsum, stream2, targ, relief_col, base, att, gains, w_up, w_down, w_out, group, lvls, lats):
    t, d = stream2.shape
    win = att.shape[-1]
    m = group * win
    ff, out = w_up.shape[1], w_out.shape[1]
    pieces = (d * ff + d * d + d * 256 + d * ff) // (DEVS * 128)
    pieces += -pieces % 8
    sds = jax.ShapeDtypeStruct
    return pl.pallas_call(
        functools.partial(tail_kernel, block_f=256, lvls=lvls, lats=lats),
        grid=(t // m,),
        in_specs=[
            pl.BlockSpec(memory_space=pltpu.SMEM),
            whole((1, 1)),
            lead((m, d)),
            lead((m, out)),
            lead((m, 1)),
            whole(base.shape),
            lead((group, d, win)),
            whole((2, d)),
            whole((d, ff)),
            whole((ff, d)),
            whole((out, d)),
        ],
        out_specs=[
            whole((1, out)),
            lead((m, d)),
            whole((DEVS * pieces, 128)),
            whole((8, ff)),
        ],
        out_shape=[
            sds((1, out), f32),
            sds((t, d), f32),
            sds((DEVS * pieces, 128), bf16),
            sds((8, ff), f32),
        ],
        scratch_shapes=[
            pltpu.VMEM((win, out), jnp.int32),
            pltpu.VMEM((win, out), f32),
            pltpu.VMEM((d // 128, d, 128), f32),
            pltpu.VMEM((ff // 128, d, 128), f32),
            pltpu.VMEM((d, ff), f32),
            pltpu.VMEM((2, d, 128), f32),
            pltpu.VMEM((d // 128, ff, 128), f32),
            pltpu.VMEM((DEVS * pieces, 128), f32),
        ],
        compiler_params=params_of(),
        name="tail_both",
    )(me, wsum, stream2, targ, relief_col, base, att, gains, w_up, w_down, w_out.T)


def attention_back(me, num, x, relief_col, table, gain, w_qkv, wt, w_proj, qt, probs, att, gs2):
    t, d = x.shape
    count, win = att.shape[0], att.shape[2]
    sds = jax.ShapeDtypeStruct
    return pl.pallas_call(
        back_kernel,
        grid=(count // TOGETHER,),
        in_specs=[
            pl.BlockSpec(memory_space=pltpu.SMEM),
            lead((TOGETHER * win, d)),
            lead((TOGETHER * win, 1)),
            whole(table.shape),
            whole((2, d)),
            whole((d, 3 * d)),
            whole((3 * d, d)),
            whole((d, d)),
            lead((TOGETHER, d, WIDE)),
            lead((TOGETHER, HEADS, win, WIDE)),
            lead((TOGETHER, d, win)),
            lead((TOGETHER * win, d)),
            whole(num.shape),
        ],
        out_specs=[
            whole((HEADS, win, WIDE)),
            whole((DEVS * 16, 128)),
            whole((DEVS * 16, 128)),
            whole((8, 3 * d)),
        ],
        out_shape=[
            sds((HEADS, win, WIDE), f32),
            sds((DEVS * 16, 128), bf16),
            sds((DEVS * 16, 128), bf16),
            sds((8, 3 * d), f32),
        ],
        scratch_shapes=[
            pltpu.VMEM((3 * d // 128, d, 128), f32),
            pltpu.VMEM((table.shape[0], d), f32),
            pltpu.VMEM((d, 128), f32),
            pltpu.VMEM((DEVS * 32, 128), f32),
        ],
        compiler_params=params_of(),
        cost_estimate=cost(10 * 2**30, 20 * 2**20, 0),
        name="attention_back",
    )(me, x, relief_col, table, gain, w_qkv, wt, w_proj, qt, probs, att, gs2, num)


def from_next(value, axes):
    sizes = [lax.axis_size(a) for a in ("lvl", "lat")]
    move = [1 if a in axes else 0 for a in ("lvl", "lat")]
    pairs = []
    for i in range(sizes[0]):
        for j in range(sizes[1]):
            src = (i + move[0]) % sizes[0] * sizes[1] + (j + move[1]) % sizes[1]
            pairs.append((src, i * sizes[1] + j))
    return lax.ppermute(value, ("lvl", "lat"), pairs)


def halo_of(field_in):
    slots_n, rows_n = field_in.shape[:2]
    hs, hr = slots_n // 2, rows_n // 2
    up = from_next(field_in[:hs, hr:], ("lvl",))
    side = from_next(field_in[hs:, :hr], ("lat",))
    both = from_next(field_in[:hs, :hr], ("lvl", "lat"))
    return up, side, both


def cos_latitude(fine_rows, lat_rows):
    angle = 90.0 - 180.0 * (fine_rows.astype(f32) + 0.5) / (4.0 * lat_rows)
    return jnp.cos(angle * (math.pi / 180.0))


def prepare_kernel(
    me_ref,
    var_ref,
    bias_ref,
    relief_ref,
    wqkv_ref,
    bias_t_ref,
    col_ref,
    wt_ref,
    base_ref,
    wsum_ref,
    lane_ref,
    *,
    lvls,
    lats,
):
    me = me_ref[0]
    heads, win, _ = bias_ref.shape
    slots, rows, lon = SLOTS, win // (SLOTS * WIN_LON), relief_ref.shape[0]
    shape = (win, win)
    key, query = (lax.broadcasted_iota(jnp.int32, shape, dim) for dim in (0, 1))
    block = rows * WIN_LON
    split_slots = (key >= win // 2) != (query >= win // 2)
    half = rows // 2 * WIN_LON
    split_rows = (key % block >= half) != (query % block >= half)
    low = jnp.where(me // lats == lvls - 1, masked_score, 0.0)
    band = jnp.where(me % lats == lats - 1, masked_score, 0.0)
    hidden = jnp.where(split_slots, low, 0.0) + jnp.where(split_rows, band, 0.0)
    blank = jnp.zeros((win, WIDE - win), f32)
    for h in range(heads):
        bias_t_ref[h] = jnp.concatenate([bias_ref[h].T * log2_e + hidden, blank], 1)
    grid = relief_ref[...].astype(f32)
    lane = lax.broadcasted_iota(jnp.int32, grid.shape, 1)
    first = (me % lats) * rows + rows // 2
    for r in range(rows):
        row = (first + r) % (rows * lats)
        col = jnp.sum(jnp.where(lane == row, grid, 0.0), 1, keepdims=True)
        col = jnp.concatenate([col[WIN_LON // 2 :], col[: WIN_LON // 2]], 0)
        for w in range(lon // WIN_LON):
            for s in range(slots):
                at = w * win + (s * rows + r) * WIN_LON
                lane_ref[at : at + WIN_LON] = col[w * WIN_LON : (w + 1) * WIN_LON]
    col_ref[...] = lane_ref[...].astype(jnp.int32)
    lat_rows = rows * lats
    vars_n = var_ref.shape[0]
    shape = base_ref.shape
    chan = lax.broadcasted_iota(jnp.int32, shape, 1)
    row = (first + lax.broadcasted_iota(jnp.int32, shape, 0)) % lat_rows
    var = jnp.zeros(shape, f32)
    var_sum = var_ref[0]
    for v in range(vars_n):
        var = jnp.where(chan // 32 == v, var_ref[v], var)
        var_sum = var_sum + var_ref[v] if v else var_sum
    base_ref[...] = var * cos_latitude(4 * row + (chan // 4) % 4, lat_rows)
    shape = (8, lat_rows)
    part = lax.broadcasted_iota(jnp.int32, shape, 0)
    fine = 4 * lax.broadcasted_iota(jnp.int32, shape, 1) + part
    lat_weight = jnp.sum(jnp.where(part < 4, cos_latitude(fine, lat_rows), 0.0), 0, keepdims=True)
    live = jnp.sum(2.0 * slots * lvls - grid, 0, keepdims=True)
    wsum_ref[...] = jnp.sum(lat_weight * live, 1, keepdims=True) * (4.0 * var_sum)
    wt_ref[...] = wqkv_ref[...].T


def prepare(me, var_weight, earth_bias, relief, w_qkv, lvls, lats):
    heads, win, _ = earth_bias.shape
    rows = win // (SLOTS * WIN_LON)
    tokens = SLOTS * rows * relief.shape[1]
    sds = jax.ShapeDtypeStruct
    vmem = pl.BlockSpec(memory_space=pltpu.VMEM)
    return pl.pallas_call(
        functools.partial(prepare_kernel, lvls=lvls, lats=lats),
        in_specs=[pl.BlockSpec(memory_space=pltpu.SMEM)] * 2 + [vmem] * 3,
        out_specs=[vmem] * 5,
        out_shape=[
            sds((heads, win, WIDE), f32),
            sds((tokens, 1), jnp.int32),
            sds(w_qkv.shape[::-1], bf16),
            sds((8, var_weight.shape[0] * 32), f32),
            sds((1, 1), f32),
        ],
        scratch_shapes=[pltpu.VMEM((tokens, 1), f32)],
        compiler_params=pltpu.CompilerParams(vmem_limit_bytes=40 * 2**20),
        name="prepare_inputs",
    )(me, var_weight, earth_bias, relief.T, w_qkv)


def body(
    tokens,
    targets,
    relief,
    earth_bias,
    relief_table,
    gain_attn,
    gain_mlp,
    w_qkv,
    w_proj,
    w_up,
    w_down,
    w_out,
    var_weight,
):
    axes = ("lvl", "lat")
    devs = lax.axis_size("lvl") * lax.axis_size("lat")
    token_halo = halo_of(tokens)
    me = lax.axis_index(axes)
    lvls, lats = lax.axis_size("lvl"), lax.axis_size("lat")
    bias_t, relief_col, wt, base, wsum = prepare(
        me.reshape(1), var_weight, earth_bias[0, 0], relief, w_qkv, lvls, lats
    )
    gains = jnp.stack([gain_attn, gain_mlp])
    tokens, targets, relief_col, bias_t, base, wsum, wt, gains = lax.optimization_barrier(
        (tokens, targets, relief_col, bias_t, base, wsum, wt, gains)
    )
    targ_halo = halo_of(targets)
    x = assemble(tokens, *token_halo)
    stream2, qt, probs, att = attention_forward(
        x, relief_col, relief_table, gains, w_qkv, wt, w_proj, bias_t
    )
    stream2, targets = lax.optimization_barrier((stream2, targets))
    targ = assemble(targets, *targ_halo)
    num, gs2, send_t, up_rows = tail_both(
        me.reshape(1), wsum, stream2, targ, relief_col, base, att, gains, w_up, w_down, w_out, GROUP, lvls, lats
    )
    got_t = lax.all_to_all(send_t.reshape(devs, -1, 128), axes, 0, 0, tiled=True)
    gbias_t, keep, give, qkv_rows = attention_back(
        me.reshape(1), num, x, relief_col, relief_table, gains, w_qkv, wt, w_proj, qt, probs, att, gs2
    )
    got = lax.ppermute(give, "lvl", [(i, i ^ 1) for i in range(lvls)])
    pair = (keep.astype(f32) + got.astype(f32)).astype(bf16)
    pair, got_t = lax.optimization_barrier((pair, got_t))
    groups = [
        [lvl * lats + lat for lvl in range(c, lvls, 2) for lat in range(lats)] for c in range(2)
    ]
    got_q = lax.all_to_all(
        pair.reshape(devs // 2, -1, 128), axes, 0, 0, axis_index_groups=groups, tiled=True
    )
    d = tokens.shape[-1]
    share = d // devs

    def mine(array):
        return lax.dynamic_slice_in_dim(array, me * share, share, 0)[None]

    shapes = (
        (1, 1),
        (share, w_qkv.shape[1]),
        (share, d),
        (share, w_up.shape[1]),
        (w_down.shape[0] // devs, d),
        (share, w_out.shape[1]),
        (1, share),
        (1, share),
        (share, relief_table.shape[0]),
    )
    sums = finish(
        wsum, got_t, got_q, up_rows, qkv_rows, mine(gain_mlp), mine(gain_attn), shapes
    )
    return (
        sums[0][0, 0],
        *sums[1:6],
        sums[6][0],
        sums[7][0],
        sums[8],
        gbias_t[..., : gbias_t.shape[1]].transpose(0, 2, 1)[None, None],
    )


def solution(mesh):
    field = P("lvl", "lat", None, None)
    bias = P("lvl", "lat", None, None, None)
    rows = P(("lvl", "lat"), None)
    vec = P(("lvl", "lat"))
    return jax.shard_map(
        body,
        mesh=mesh,
        in_specs=(field, field, P(), bias) + (P(),) * 9,
        out_specs=(P(), rows, rows, rows, rows, rows, vec, vec, rows, bias),
        check_vma=False,
    )
```

```python
import functools
import math

import jax
import jax.numpy as jnp
from jax import lax
from jax.experimental import pallas as pl
from jax.experimental.pallas import tpu as pltpu
from jax.sharding import PartitionSpec as P

WIN_LON = 12
HEADS = 12
GROUP = 6
DEVS = 128
WIDE = 256
SLOTS = 2
TOGETHER = 4
norm_eps = 1e-05
loss_scale = 32768.0
smooth_sq = 0.01
masked_score = -1e30
log2_e = math.log2(math.e)
f32 = jnp.float32
bf16 = jnp.bfloat16


def nn(left, right):
    return lax.dot_general(left, right, (((1,), (0,)), ((), ())), preferred_element_type=f32)


def nt(left, right):
    return lax.dot_general(left, right, (((1,), (1,)), ((), ())), preferred_element_type=f32)


def tn(left, right):
    return lax.dot_general(left, right, (((0,), (0,)), ((), ())), preferred_element_type=f32)


def normalize(values):
    width = values.shape[-1]
    centre = jnp.sum(values, -1, keepdims=True) * (1.0 / width)
    moved = values - centre
    spread = jnp.sum(moved * moved, -1, keepdims=True) * (1.0 / width)
    rstd = lax.rsqrt(spread + norm_eps)
    return moved * rstd, rstd


def norm_back(grad_hat, hat, rstd):
    width = hat.shape[-1]
    mean_g = jnp.sum(grad_hat, -1, keepdims=True) * (1.0 / width)
    mean_gh = jnp.sum(grad_hat * hat, -1, keepdims=True) * (1.0 / width)
    return rstd * (grad_hat - mean_g - hat * mean_gh)


def gelu_both(x):
    dens = jnp.exp2(x * x * (-0.5 * log2_e))
    den = 1.0 + jnp.abs(x) * (0.3275911 / math.sqrt(2.0))
    t = pl.reciprocal(den, approx=True)
    t = t * (2.0 - den * t)
    poly = 0.5 * 1.061405429
    for coef in (-1.453152027, 1.421413741, -0.284496736, 0.254829592):
        poly = poly * t + 0.5 * coef
    side = poly * t * dens
    cdf = jnp.where(x >= 0.0, 1.0 - side, side)
    return x * cdf, cdf + x * dens * (1.0 / math.sqrt(2.0 * math.pi))


def own_rows(me, weight_ref):
    rows = weight_ref.shape[0]
    share = rows // DEVS
    ids = lax.broadcasted_iota(jnp.int32, (8, rows), 0) + me * share
    picks = (lax.broadcasted_iota(jnp.int32, (8, rows), 1) == ids).astype(f32).astype(bf16)
    return nn(picks, weight_ref[...])


def pack_rows(send_ref, at, piece_ref):
    pieces, rows, _ = piece_ref.shape
    share = rows // DEVS
    every = send_ref.shape[0] // DEVS
    for i in range(share):
        for c in range(pieces):
            block = piece_ref[c, pl.ds(i, DEVS, stride=share), :]
            send_ref[pl.ds(at, DEVS, stride=every), :] = block
            at += 1
    return at


def fill_rows(send_ref, at):
    every = send_ref.shape[0] // DEVS
    for j in range(at, every):
        send_ref[pl.ds(j, DEVS, stride=every), :] = jnp.zeros((DEVS, 128), f32)


def add_pieces(piece_ref, at, grad):
    for c in range(grad.shape[1] // 128):
        piece_ref[at + c] += grad[:, c * 128 : (c + 1) * 128]


def turn_pieces(piece_ref, grad_t_ref):
    for c in range(piece_ref.shape[0]):
        piece_ref[c] = grad_t_ref[c * 128 : (c + 1) * 128].T


def one_hot_of(relief_col, classes):
    ids = lax.broadcasted_iota(jnp.int32, (relief_col.shape[0], classes), 1)
    return (relief_col == ids).astype(f32).astype(bf16)


def alone(part, place, count):
    parts = [jnp.zeros_like(part)] * count
    parts[place] = part
    return jnp.concatenate(parts, 0)


def stream_of(x_ref, relief_ref, table_ref):
    one_hot = one_hot_of(relief_ref[...], table_ref.shape[0])
    return x_ref[...].astype(f32) + nn(one_hot, table_ref[...]), one_hot


def att_kernel(
    x_ref,
    relief_ref,
    table_ref,
    gain_ref,
    wt_ref,
    wqkv_ref,
    wproj_ref,
    bias_ref,
    stream2_ref,
    qt_ref,
    prob_ref,
    att_ref,
):
    stream, _ = stream_of(x_ref, relief_ref, table_ref)
    hat, _ = normalize(stream)
    normed = (hat * gain_ref[:1]).astype(bf16)
    d = normed.shape[1]
    count, win = att_ref.shape[0], att_ref.shape[2]
    k_tok = nn(normed, wqkv_ref[:, d : 2 * d]).astype(bf16)
    e = d // HEADS
    per = 128 // e
    qvts = []
    for u in range(count):
        rows = slice(u * win, (u + 1) * win)
        filled = jnp.concatenate([normed[rows], jnp.zeros((WIDE - win, d), bf16)], 0)
        qvts.append((nt(wt_ref[:d], filled), nt(wt_ref[2 * d :], filled)))
    mixed, atts = [], []
    for u in range(count):
        rows = slice(u * win, (u + 1) * win)
        qt = (qvts[u][0] * (log2_e * e**-0.5)).astype(bf16)
        vt = qvts[u][1].astype(bf16)
        att = []
        for g in range(d // 128):
            k_four = k_tok[rows, g * 128 : (g + 1) * 128]
            heads = range(g * per, (g + 1) * per)
            scores = [nn(k_four, alone(qt[h * e : (h + 1) * e], h % per, per)) for h in heads]
            probs = []
            for h, score in zip(heads, scores):
                score = score + bias_ref[h]
                top = jnp.max(score, 0, keepdims=True)
                prob = jnp.exp2(score - top)
                prob = (prob * (1.0 / jnp.sum(prob, 0, keepdims=True))).astype(bf16)
                probs.append(prob)
                prob_ref[u, h] = prob
            att += [nn(vt[h * e : (h + 1) * e, :win], prob) for h, prob in zip(heads, probs)]
        att = jnp.concatenate(att, 0).astype(bf16)[:, :win]
        att_ref[u] = att
        qt_ref[u] = qt
        atts.append(att.T)
    stream2_ref[...] = stream + nn(jnp.concatenate(atts, 0), wproj_ref[...]).astype(bf16).astype(f32)


def tail_kernel(
    me_ref,
    wsum_ref,
    stream2_ref,
    targ_ref,
    relief_ref,
    base_ref,
    att_ref,
    gain_ref,
    wup_ref,
    wdown_ref,
    wout_ref,
    num_ref,
    gs2_ref,
    send_ref,
    wsel_ref,
    lev_ref,
    wide_ref,
    gproj_ref,
    gup_ref,
    gdown_ref,
    gout_ref,
    gdown_t_ref,
    pack_ref,
    *,
    block_f,
    lvls,
    lats,
):
    step = pl.program_id(0)
    me = me_ref[0]

    @pl.when(step == 0)
    def _():
        shape = lev_ref.shape
        slots, rows = SLOTS, shape[0] // (SLOTS * WIN_LON)
        own = (me // lats) * slots + slots // 2
        token = lax.broadcasted_iota(jnp.int32, shape, 0)
        upper = (lax.broadcasted_iota(jnp.int32, shape, 1) // 16) % 2
        line = token // WIN_LON
        lev_ref[...] = 2 * ((own + line // rows) % (slots * lvls)) + upper
        wide = jnp.zeros(shape, f32)
        for r in range(rows):
            wide = jnp.where(line % rows == r, base_ref[r : r + 1], wide)
        wide_ref[...] = wide
        num_ref[...] = jnp.zeros_like(num_ref)
        gproj_ref[...] = jnp.zeros_like(gproj_ref)
        gup_ref[...] = jnp.zeros_like(gup_ref)
        gdown_ref[...] = jnp.zeros_like(gdown_ref)
        gout_ref[...] = jnp.zeros_like(gout_ref)

    stream2 = stream2_ref[...]
    wins, win = att_ref.shape[0], att_ref.shape[2]
    ff = wup_ref.shape[1]
    hat, rstd = normalize(stream2)
    gain = gain_ref[1:2]
    normed2 = (hat * gain).astype(bf16)
    hids, slopes, gpres = [], [], []
    for n in range(0, ff, block_f):
        cols = slice(n, n + block_f)
        hidden, slope = gelu_both(nn(normed2, wup_ref[:, cols]))
        hids.append(hidden.astype(bf16))
        slopes.append(slope.astype(bf16))
    field = (stream2 + nn(jnp.concatenate(hids, 1), wdown_ref[...])).astype(bf16)
    pred = nt(field, wout_ref[...])
    relief = relief_ref[...]
    lev = jnp.concatenate([lev_ref[...]] * wins, 0)
    base = jnp.concatenate([wide_ref[...]] * wins, 0)
    cell_w = jnp.where(lev >= relief, base, 0.0)
    differ = pred - targ_ref[...].astype(f32)
    square = differ * differ + smooth_sq
    inv_err = lax.rsqrt(square)
    num_ref[...] += jnp.sum(cell_w * (square * inv_err), 0, keepdims=True)
    scale = loss_scale / wsum_ref[...]
    gpred = (scale * cell_w * differ * inv_err).astype(bf16)
    gout = nn(field.T, gpred)
    add_pieces(gout_ref, 0, gout[:, :128])
    gout_ref[1, :, : gout.shape[1] - 128] += gout[:, 128:]
    gfield = nn(gpred, wout_ref[...])
    gfb = gfield.astype(bf16)
    gfbt = gfb.T
    normed2t = normed2.T
    for n in range(0, ff, block_f):
        cols = slice(n, n + block_f)
        ghid = nt(gfb, wdown_ref[cols, :])
        gpres.append((slopes[n // block_f].astype(f32) * ghid).astype(bf16))
    for n in range(0, ff, block_f):
        cols = slice(n, n + block_f)
        gdown_ref[:, cols] += nn(gfbt, hids[n // block_f])
        add_pieces(gup_ref, n // 128, nn(normed2t, gpres[n // block_f]))
    gnorm2 = nt(jnp.concatenate(gpres, 1), wup_ref[...])
    gs2 = gfield + norm_back(gnorm2 * gain, hat, rstd)
    gs2_ref[...] = gs2
    gmix = gs2.astype(bf16)
    for w in range(wins):
        add_pieces(gproj_ref, 0, nn(att_ref[w], gmix[w * win : (w + 1) * win]))

    @pl.when(step == pl.num_programs(0) - 1)
    def _():
        wsel_ref[...] = own_rows(me, wup_ref)
        at = 0
        for ref in (gup_ref, gproj_ref, gout_ref):
            at = pack_rows(pack_ref, at, ref)
        turn_pieces(gdown_t_ref, gdown_ref)
        at = pack_rows(pack_ref, at, gdown_t_ref)
        fill_rows(pack_ref, at)
        send_ref[...] = pack_ref[...].astype(bf16)


def back_kernel(
    me_ref,
    x_ref,
    relief_ref,
    table_ref,
    gain_ref,
    wqkv_ref,
    wt_ref,
    wproj_ref,
    qt_ref,
    prob_ref,
    att_ref,
    gs2_ref,
    num_ref,
    gbias_ref,
    keep_ref,
    give_ref,
    wsel_ref,
    gqkv_ref,
    grel_ref,
    grel_t_ref,
    pack_ref,
):
    step = pl.program_id(0)

    @pl.when(step == 0)
    def _():
        gbias_ref[...] = jnp.zeros_like(gbias_ref)
        gqkv_ref[...] = jnp.zeros_like(gqkv_ref)
        grel_ref[...] = jnp.zeros_like(grel_ref)

    stream, one_hot = stream_of(x_ref, relief_ref, table_ref)
    hat, rstd = normalize(stream)
    gain = gain_ref[:1]
    normed = (hat * gain).astype(bf16)
    d = normed.shape[1]
    count, win = att_ref.shape[0], att_ref.shape[2]
    e = d // HEADS
    per = 128 // e
    gs2 = gs2_ref[...]
    gmix = gs2.astype(bf16)
    pad = jnp.zeros((WIDE - win, d), bf16)
    gatts = []
    for u in range(count):
        filled = jnp.concatenate([gmix[u * win : (u + 1) * win], pad], 0)
        gatts.append(nt(wproj_ref[...], filled).astype(bf16))
    v_tok = nn(normed, wqkv_ref[:, 2 * d :]).astype(bf16)
    kts = []
    for u in range(count):
        filled = jnp.concatenate([normed[u * win : (u + 1) * win], pad], 0)
        kts.append(nt(wt_ref[d : 2 * d], filled).astype(bf16)[:, :win])
    gturned = []
    for u in range(count):
        wrows = slice(u * win, (u + 1) * win)
        gatt_b = gatts[u]
        prod = gatt_b[:, :win].astype(f32) * att_ref[u].astype(f32)
        prod = jnp.concatenate([prod, jnp.zeros((d, WIDE - win), f32)], 1)
        qt, kt = qt_ref[u], kts[u]
        gqs, gks, gvs = [], [], []
        for g in range(d // 128):
            v_four = v_tok[wrows, g * 128 : (g + 1) * 128]
            heads = range(g * per, (g + 1) * per)
            gprobs = [nn(v_four, alone(gatt_b[h * e : (h + 1) * e], h % per, per)) for h in heads]
            gscores = []
            probs = [prob_ref[u, h] for h in heads]
            for h, gprob, prob in zip(heads, gprobs, probs):
                delta = jnp.sum(prod[h * e : (h + 1) * e], 0, keepdims=True)
                gscore = prob.astype(f32) * (gprob - delta)
                gbias_ref[h] += gscore
                gscores.append(gscore.astype(bf16))
            for h, gsb, prob in zip(heads, gscores, probs):
                rows = slice(h * e, (h + 1) * e)
                gqs.append((nn(kt[rows], gsb) * e**-0.5).astype(bf16)[:, :win])
                gks.append((nt(qt[rows], gsb) * (1.0 / log2_e)).astype(bf16))
                gvs.append(nt(gatt_b[rows], prob).astype(bf16))
        gheads = jnp.concatenate(gqs + gks + gvs, 0)
        gturned.append(gheads.T)
    gturned = jnp.concatenate(gturned, 0)
    gshift = nn(gturned, wt_ref[...]).astype(bf16).astype(f32)
    add_pieces(gqkv_ref, 0, nn(normed.T, gturned))
    gstream = gs2 + norm_back(gshift * gain, hat, rstd)
    grel_ref[...] += tn(one_hot, gstream.astype(bf16))

    @pl.when(step == pl.num_programs(0) - 1)
    def _():
        wsel_ref[...] = own_rows(me_ref[0], wqkv_ref)
        at = pack_rows(pack_ref, 0, gqkv_ref)
        classes = grel_ref.shape[0]
        wide = jnp.concatenate([grel_ref[...], jnp.zeros((128 - classes, d), f32)], 0)
        grel_t_ref[...] = wide.T
        share = d // DEVS
        num = jnp.sum(num_ref[...], 1, keepdims=True)
        high = num.astype(bf16).astype(f32)
        lane = lax.broadcasted_iota(jnp.int32, (DEVS, 128), 1)
        last = jnp.where(lane == 126, high, jnp.where(lane == 127, num - high, 0.0))
        for i in range(share):
            part = grel_t_ref[pl.ds(i, DEVS, stride=share), :]
            last += pltpu.roll(part, i * classes, 1) if i else part
        every = pack_ref.shape[0] // DEVS
        pack_ref[pl.ds(at, DEVS, stride=every), :] = last
        fill_rows(pack_ref, at + 1)
        lats = DEVS // 4
        odd = (me_ref[0] // lats) % 2
        size = lats * every
        for c in range(2):
            mine = pl.multiple_of((2 * c + odd) * size, size)
            other = pl.multiple_of((2 * c + 1 - odd) * size, size)
            keep_ref[c * size : (c + 1) * size] = pack_ref[pl.ds(mine, size), :].astype(bf16)
            give_ref[c * size : (c + 1) * size] = pack_ref[pl.ds(other, size), :].astype(bf16)


def assemble_kernel(own_ref, up_ref, side_ref, both_ref, out_ref, scr_ref):
    slots, rows, lon, _ = own_ref.shape
    hs, hr = slots // 2, rows // 2
    half = WIN_LON // 2
    win = slots * rows * WIN_LON
    for s in range(slots):
        for r in range(rows):
            if s < hs:
                plane = own_ref[hs + s, hr + r] if r < hr else side_ref[s, r - hr]
            else:
                plane = up_ref[s - hs, r] if r < hr else both_ref[s - hs, r - hr]
            plane = plane.astype(f32)
            plane = jnp.concatenate([plane[half:], plane[:half]], 0)
            for w in range(lon // WIN_LON):
                at = w * win + (s * rows + r) * WIN_LON
                scr_ref[at : at + WIN_LON] = plane[w * WIN_LON : (w + 1) * WIN_LON]
    out_ref[...] = scr_ref[...].astype(bf16)


def assemble(own, up, side, both):
    count = own.shape[0] * own.shape[1] * own.shape[2]
    return pl.pallas_call(
        assemble_kernel,
        out_shape=jax.ShapeDtypeStruct((count, own.shape[3]), bf16),
        scratch_shapes=[pltpu.VMEM((count, own.shape[3]), f32)],
        compiler_params=pltpu.CompilerParams(vmem_limit_bytes=40 * 2**20),
        name="assemble_windows",
    )(own, up, side, both)


def finish_kernel(
    weight_sum_ref, gott_ref, gotq_ref, wup_ref, wqkv_ref, gmlp_ref, gatt_ref, *outs
):
    loss_ref, gqkv_ref, gproj_ref, gup_ref, gdown_ref, gout_ref, ga_ref, gm_ref, grel_ref = outs
    got = jnp.sum(gott_ref[...].astype(f32), 0)
    at = 0
    for ref in (gup_ref, gproj_ref, gout_ref, gdown_ref):
        rows, cols = ref.shape
        for i in range(rows):
            for c in range(0, cols, 128):
                size = min(128, cols - c)
                ref[i : i + 1, c : c + size] = got[at : at + 1, :size]
                at += 1
    got = jnp.sum(gotq_ref[...].astype(f32), 0)
    at = 0
    rows, cols = gqkv_ref.shape
    for i in range(rows):
        for c in range(0, cols, 128):
            gqkv_ref[i : i + 1, c : c + 128] = got[at : at + 1]
            at += 1
    last = got[at : at + 1]
    classes = grel_ref.shape[1]
    for i in range(rows):
        grel_ref[i : i + 1, :] = last[:, i * classes : (i + 1) * classes]
    loss_ref[...] = (last[:, 126:127] + last[:, 127:128]) / weight_sum_ref[...]
    diag = lax.broadcasted_iota(jnp.int32, (rows, rows), 0) == lax.broadcasted_iota(
        jnp.int32, (rows, rows), 1
    )
    ga = jnp.sum(wqkv_ref[:rows] * gqkv_ref[...], 1, keepdims=True)
    ga_ref[...] = jnp.sum(jnp.where(diag, ga, 0.0), 0, keepdims=True) / gatt_ref[...]
    gm = jnp.sum(wup_ref[:rows] * gup_ref[...], 1, keepdims=True)
    gm_ref[...] = jnp.sum(jnp.where(diag, gm, 0.0), 0, keepdims=True) / gmlp_ref[...]


def finish(weight_sum, got_t, got_q, w_up, w_qkv, gain_mlp, gain_attn, shapes):
    vmem = pl.BlockSpec(memory_space=pltpu.VMEM)
    return pl.pallas_call(
        finish_kernel,
        in_specs=[vmem] * 7,
        out_specs=[vmem] * len(shapes),
        out_shape=[jax.ShapeDtypeStruct(shape, f32) for shape in shapes],
        compiler_params=pltpu.CompilerParams(vmem_limit_bytes=40 * 2**20),
        name="finish_sums",
    )(weight_sum, got_t, got_q, w_up, w_qkv, gain_mlp, gain_attn)


def whole(shape):
    return pl.BlockSpec(shape, lambda i: (0,) * len(shape))


def lead(shape):
    return pl.BlockSpec(shape, lambda i: (i,) + (0,) * (len(shape) - 1))


def params_of():
    return pltpu.CompilerParams(
        vmem_limit_bytes=56 * 2**20, dimension_semantics=("arbitrary",)
    )


def attention_forward(x, relief_col, table, gain, w_qkv, wt, w_proj, bias_t):
    t, d = x.shape
    win = bias_t.shape[1]
    count = t // win
    sds = jax.ShapeDtypeStruct
    return pl.pallas_call(
        att_kernel,
        grid=(count // TOGETHER,),
        in_specs=[
            lead((TOGETHER * win, d)),
            lead((TOGETHER * win, 1)),
            whole(table.shape),
            whole((2, d)),
            whole((3 * d, d)),
            whole((d, 3 * d)),
            whole((d, d)),
            whole(bias_t.shape),
        ],
        out_specs=[
            lead((TOGETHER * win, d)),
            lead((TOGETHER, d, WIDE)),
            lead((TOGETHER, HEADS, win, WIDE)),
            lead((TOGETHER, d, win)),
        ],
        out_shape=[
            sds((t, d), f32),
            sds((count, d, WIDE), bf16),
            sds((count, HEADS, win, WIDE), bf16),
            sds((count, d, win), bf16),
        ],
        compiler_params=params_of(),
        name="attention_forward",
    )(
        x,
        relief_col,
        table,
        gain,
        wt,
        w_qkv,
        w_proj,
        bias_t,
    )


def cost(flops, moved, trans):
    return pl.CostEstimate(flops=flops, bytes_accessed=moved, transcendentals=trans)


def tail_both(me, wsum, stream2, targ, relief_col, base, att, gains, w_up, w_down, w_out, group, lvls, lats):
    t, d = stream2.shape
    win = att.shape[-1]
    m = group * win
    ff, out = w_up.shape[1], w_out.shape[1]
    pieces = (d * ff + d * d + d * 256 + d * ff) // (DEVS * 128)
    pieces += -pieces % 8
    sds = jax.ShapeDtypeStruct
    return pl.pallas_call(
        functools.partial(tail_kernel, block_f=256, lvls=lvls, lats=lats),
        grid=(t // m,),
        in_specs=[
            pl.BlockSpec(memory_space=pltpu.SMEM),
            whole((1, 1)),
            lead((m, d)),
            lead((m, out)),
            lead((m, 1)),
            whole(base.shape),
            lead((group, d, win)),
            whole((2, d)),
            whole((d, ff)),
            whole((ff, d)),
            whole((out, d)),
        ],
        out_specs=[
            whole((1, out)),
            lead((m, d)),
            whole((DEVS * pieces, 128)),
            whole((8, ff)),
        ],
        out_shape=[
            sds((1, out), f32),
            sds((t, d), f32),
            sds((DEVS * pieces, 128), bf16),
            sds((8, ff), f32),
        ],
        scratch_shapes=[
            pltpu.VMEM((win, out), jnp.int32),
            pltpu.VMEM((win, out), f32),
            pltpu.VMEM((d // 128, d, 128), f32),
            pltpu.VMEM((ff // 128, d, 128), f32),
            pltpu.VMEM((d, ff), f32),
            pltpu.VMEM((2, d, 128), f32),
            pltpu.VMEM((d // 128, ff, 128), f32),
            pltpu.VMEM((DEVS * pieces, 128), f32),
        ],
        compiler_params=params_of(),
        name="tail_both",
    )(me, wsum, stream2, targ, relief_col, base, att, gains, w_up, w_down, w_out.T)


def attention_back(me, num, x, relief_col, table, gain, w_qkv, wt, w_proj, qt, probs, att, gs2):
    t, d = x.shape
    count, win = att.shape[0], att.shape[2]
    sds = jax.ShapeDtypeStruct
    return pl.pallas_call(
        back_kernel,
        grid=(count // TOGETHER,),
        in_specs=[
            pl.BlockSpec(memory_space=pltpu.SMEM),
            lead((TOGETHER * win, d)),
            lead((TOGETHER * win, 1)),
            whole(table.shape),
            whole((2, d)),
            whole((d, 3 * d)),
            whole((3 * d, d)),
            whole((d, d)),
            lead((TOGETHER, d, WIDE)),
            lead((TOGETHER, HEADS, win, WIDE)),
            lead((TOGETHER, d, win)),
            lead((TOGETHER * win, d)),
            whole(num.shape),
        ],
        out_specs=[
            whole((HEADS, win, WIDE)),
            whole((DEVS * 16, 128)),
            whole((DEVS * 16, 128)),
            whole((8, 3 * d)),
        ],
        out_shape=[
            sds((HEADS, win, WIDE), f32),
            sds((DEVS * 16, 128), bf16),
            sds((DEVS * 16, 128), bf16),
            sds((8, 3 * d), f32),
        ],
        scratch_shapes=[
            pltpu.VMEM((3 * d // 128, d, 128), f32),
            pltpu.VMEM((table.shape[0], d), f32),
            pltpu.VMEM((d, 128), f32),
            pltpu.VMEM((DEVS * 32, 128), f32),
        ],
        compiler_params=params_of(),
        cost_estimate=cost(10 * 2**30, 20 * 2**20, 0),
        name="attention_back",
    )(me, x, relief_col, table, gain, w_qkv, wt, w_proj, qt, probs, att, gs2, num)


def from_next(value, axes):
    sizes = [lax.axis_size(a) for a in ("lvl", "lat")]
    move = [1 if a in axes else 0 for a in ("lvl", "lat")]
    pairs = []
    for i in range(sizes[0]):
        for j in range(sizes[1]):
            src = (i + move[0]) % sizes[0] * sizes[1] + (j + move[1]) % sizes[1]
            pairs.append((src, i * sizes[1] + j))
    return lax.ppermute(value, ("lvl", "lat"), pairs)


def halo_of(field_in):
    slots_n, rows_n = field_in.shape[:2]
    hs, hr = slots_n // 2, rows_n // 2
    up = from_next(field_in[:hs, hr:], ("lvl",))
    side = from_next(field_in[hs:, :hr], ("lat",))
    both = from_next(field_in[:hs, :hr], ("lvl", "lat"))
    return up, side, both


def cos_latitude(fine_rows, lat_rows):
    angle = 90.0 - 180.0 * (fine_rows.astype(f32) + 0.5) / (4.0 * lat_rows)
    return jnp.cos(angle * (math.pi / 180.0))


def prepare_kernel(
    me_ref,
    var_ref,
    bias_ref,
    relief_ref,
    wqkv_ref,
    bias_t_ref,
    col_ref,
    wt_ref,
    base_ref,
    wsum_ref,
    lane_ref,
    *,
    lvls,
    lats,
):
    me = me_ref[0]
    heads, win, _ = bias_ref.shape
    slots, rows, lon = SLOTS, win // (SLOTS * WIN_LON), relief_ref.shape[0]
    shape = (win, win)
    key, query = (lax.broadcasted_iota(jnp.int32, shape, dim) for dim in (0, 1))
    block = rows * WIN_LON
    split_slots = (key >= win // 2) != (query >= win // 2)
    half = rows // 2 * WIN_LON
    split_rows = (key % block >= half) != (query % block >= half)
    low = jnp.where(me // lats == lvls - 1, masked_score, 0.0)
    band = jnp.where(me % lats == lats - 1, masked_score, 0.0)
    hidden = jnp.where(split_slots, low, 0.0) + jnp.where(split_rows, band, 0.0)
    blank = jnp.zeros((win, WIDE - win), f32)
    for h in range(heads):
        bias_t_ref[h] = jnp.concatenate([bias_ref[h].T * log2_e + hidden, blank], 1)
    grid = relief_ref[...].astype(f32)
    lane = lax.broadcasted_iota(jnp.int32, grid.shape, 1)
    first = (me % lats) * rows + rows // 2
    for r in range(rows):
        row = (first + r) % (rows * lats)
        col = jnp.sum(jnp.where(lane == row, grid, 0.0), 1, keepdims=True)
        col = jnp.concatenate([col[WIN_LON // 2 :], col[: WIN_LON // 2]], 0)
        for w in range(lon // WIN_LON):
            for s in range(slots):
                at = w * win + (s * rows + r) * WIN_LON
                lane_ref[at : at + WIN_LON] = col[w * WIN_LON : (w + 1) * WIN_LON]
    col_ref[...] = lane_ref[...].astype(jnp.int32)
    lat_rows = rows * lats
    vars_n = var_ref.shape[0]
    shape = base_ref.shape
    chan = lax.broadcasted_iota(jnp.int32, shape, 1)
    row = (first + lax.broadcasted_iota(jnp.int32, shape, 0)) % lat_rows
    var = jnp.zeros(shape, f32)
    var_sum = var_ref[0]
    for v in range(vars_n):
        var = jnp.where(chan // 32 == v, var_ref[v], var)
        var_sum = var_sum + var_ref[v] if v else var_sum
    base_ref[...] = var * cos_latitude(4 * row + (chan // 4) % 4, lat_rows)
    shape = (8, lat_rows)
    part = lax.broadcasted_iota(jnp.int32, shape, 0)
    fine = 4 * lax.broadcasted_iota(jnp.int32, shape, 1) + part
    lat_weight = jnp.sum(jnp.where(part < 4, cos_latitude(fine, lat_rows), 0.0), 0, keepdims=True)
    live = jnp.sum(2.0 * slots * lvls - grid, 0, keepdims=True)
    wsum_ref[...] = jnp.sum(lat_weight * live, 1, keepdims=True) * (4.0 * var_sum)
    wt_ref[...] = wqkv_ref[...].T


def prepare(me, var_weight, earth_bias, relief, w_qkv, lvls, lats):
    heads, win, _ = earth_bias.shape
    rows = win // (SLOTS * WIN_LON)
    tokens = SLOTS * rows * relief.shape[1]
    sds = jax.ShapeDtypeStruct
    vmem = pl.BlockSpec(memory_space=pltpu.VMEM)
    return pl.pallas_call(
        functools.partial(prepare_kernel, lvls=lvls, lats=lats),
        in_specs=[pl.BlockSpec(memory_space=pltpu.SMEM)] * 2 + [vmem] * 3,
        out_specs=[vmem] * 5,
        out_shape=[
            sds((heads, win, WIDE), f32),
            sds((tokens, 1), jnp.int32),
            sds(w_qkv.shape[::-1], bf16),
            sds((8, var_weight.shape[0] * 32), f32),
            sds((1, 1), f32),
        ],
        scratch_shapes=[pltpu.VMEM((tokens, 1), f32)],
        compiler_params=pltpu.CompilerParams(vmem_limit_bytes=40 * 2**20),
        name="prepare_inputs",
    )(me, var_weight, earth_bias, relief.T, w_qkv)


def body(
    tokens,
    targets,
    relief,
    earth_bias,
    relief_table,
    gain_attn,
    gain_mlp,
    w_qkv,
    w_proj,
    w_up,
    w_down,
    w_out,
    var_weight,
):
    axes = ("lvl", "lat")
    devs = lax.axis_size("lvl") * lax.axis_size("lat")
    token_halo = halo_of(tokens)
    me = lax.axis_index(axes)
    lvls, lats = lax.axis_size("lvl"), lax.axis_size("lat")
    bias_t, relief_col, wt, base, wsum = prepare(
        me.reshape(1), var_weight, earth_bias[0, 0], relief, w_qkv, lvls, lats
    )
    gains = jnp.stack([gain_attn, gain_mlp])
    tokens, targets, relief_col, bias_t, base, wsum, wt, gains = lax.optimization_barrier(
        (tokens, targets, relief_col, bias_t, base, wsum, wt, gains)
    )
    targ_halo = halo_of(targets)
    x = assemble(tokens, *token_halo)
    stream2, qt, probs, att = attention_forward(
        x, relief_col, relief_table, gains, w_qkv, wt, w_proj, bias_t
    )
    stream2, targets = lax.optimization_barrier((stream2, targets))
    targ = assemble(targets, *targ_halo)
    num, gs2, send_t, up_rows = tail_both(
        me.reshape(1), wsum, stream2, targ, relief_col, base, att, gains, w_up, w_down, w_out, GROUP, lvls, lats
    )
    got_t = lax.all_to_all(send_t.reshape(devs, -1, 128), axes, 0, 0, tiled=True)
    gbias_t, keep, give, qkv_rows = attention_back(
        me.reshape(1), num, x, relief_col, relief_table, gains, w_qkv, wt, w_proj, qt, probs, att, gs2
    )
    got = lax.ppermute(give, "lvl", [(i, i ^ 1) for i in range(lvls)])
    pair = (keep.astype(f32) + got.astype(f32)).astype(bf16)
    pair, got_t = lax.optimization_barrier((pair, got_t))
    groups = [
        [lvl * lats + lat for lvl in range(c, lvls, 2) for lat in range(lats)] for c in range(2)
    ]
    got_q = lax.all_to_all(
        pair.reshape(devs // 2, -1, 128), axes, 0, 0, axis_index_groups=groups, tiled=True
    )
    d = tokens.shape[-1]
    share = d // devs

    def mine(array):
        return lax.dynamic_slice_in_dim(array, me * share, share, 0)[None]

    shapes = (
        (1, 1),
        (share, w_qkv.shape[1]),
        (share, d),
        (share, w_up.shape[1]),
        (w_down.shape[0] // devs, d),
        (share, w_out.shape[1]),
        (1, share),
        (1, share),
        (share, relief_table.shape[0]),
    )
    sums = finish(
        wsum, got_t, got_q, up_rows, qkv_rows, mine(gain_mlp), mine(gain_attn), shapes
    )
    return (
        sums[0][0, 0],
        *sums[1:6],
        sums[6][0],
        sums[7][0],
        sums[8],
        gbias_t[..., : gbias_t.shape[1]].transpose(0, 2, 1)[None, None],
    )


def solution(mesh):
    field = P("lvl", "lat", None, None)
    bias = P("lvl", "lat", None, None, None)
    rows = P(("lvl", "lat"), None)
    vec = P(("lvl", "lat"))
    return jax.shard_map(
        body,
        mesh=mesh,
        in_specs=(field, field, P(), bias) + (P(),) * 9,
        out_specs=(P(), rows, rows, rows, rows, rows, vec, vec, rows, bias),
        check_vma=False,
    )
```
